32 devices in a mesh: section: 4 (over y, core), dp: 8 (over z, x).
Axes of the slice: x: 2, y: 2, z: 4, core: 2. Of those that a mesh axis runs over, the one named last changes fastest.
Arguments:
- entry_states: bfloat16 [5, 256, 4608], P(None, 'dp'), may hold values from -6 to 6
- down_proj: bfloat16 [4, 4, 4608, 128], P('section'), may hold values from -0.09375 to 0.09375
- up_proj: bfloat16 [4, 4, 4608, 128], P('section'), may hold values from -0.5 to 0.5
- label_rows: bfloat16 [256, 4608], replicated, may hold values from -0.375 to 0.375
- sampled_labels: int32 [4, 5, 256], P(None, None, 'dp'), may hold values from 0 to 255
- eval_states: bfloat16 [256, 4608], P('dp'), may hold values from -6 to 6
Outputs:
- eval_out: bfloat16 [4, 256, 4608], P('section', 'dp')
- label_logprob: float32 [4, 5, 256], P('section', None, 'dp')
- fisher_log: float32 [4, 2, 4608, 128], P('section', None, 'dp')
The draws below stay inside these ranges and needn't reach their ends.
All inputs are finite; a program needn't handle non-finite values.
Results may differ from the reference program's by a relative error of at most 0.0065.
Values may be sent and summed in bfloat16 or wider, within the bound.
No kernel may reach another device: no remote copies, remote signals or barrier semaphores. Data moves between devices by JAX's collectives and lax.ppermute only.
A program may use at most 128 MiB of HBM per device.

```python
import jax
import jax.numpy as jnp
from jax import lax

D = 4608
R = 128
LABELS = 256
TASKS = 4
MICRO = 5
SECTIONS = 4
TOKENS = 256
EVAL = 256


def touch_ends(values, rng, low, largest):
    dims = values.shape
    index_at = [jax.random.randint(jax.random.fold_in(rng, axis), (), 0, dims[axis]) for axis in range(len(dims))]
    values = values.at[tuple(index_at)].set(low)
    longest = dims.index(max(dims))
    index_at[longest] = (index_at[longest] + 1) % dims[longest]
    return values.at[tuple(index_at)].set(largest)


def strengthened(entries, stream_key, source, target, parts, factor):
    def block_of(position):
        return (jnp.arange(entries.shape[position]) // (entries.shape[position] // parts)).reshape((-1,) + (1,) * (entries.ndim - 1 - position))

    first = jax.random.permutation(stream_key, parts)[block_of(target)]
    other_side = (block_of(target) + parts // 2) % parts
    return jnp.where((block_of(source) == first) | (block_of(source) == other_side), factor * entries, entries)


def block_levels(rng, dims, pieces, low, top_value):
    level, own = 1.0, jax.random.fold_in(rng, 6)
    for dim, blocks in pieces:
        steps = jnp.exp(jax.random.uniform(jax.random.fold_in(own, dim), (blocks,), jnp.float32, low / len(pieces), top_value / len(pieces)))
        level = level * jnp.repeat(steps, dims[dim] // blocks).reshape([-1 if axis == dim else 1 for axis in range(len(dims))])
    return level


def centred(rng, dims, width, most, split=(), kind=jnp.bfloat16):
    drawn = width * jax.random.normal(rng, dims, jnp.float32)
    if split:
        drawn = drawn * block_levels(rng, dims, split, -0.22, 0.18)
    return jnp.clip(drawn, -most, most).astype(kind)


def noise_with(own_key, shape, width, limit, cuts, heavy, held_as=jnp.bfloat16):
    values = width * jax.random.normal(own_key, shape, jnp.float32)
    if cuts:
        values = values * block_levels(own_key, shape, cuts, -0.22, 0.18)
    return jnp.clip(strengthened(values, jax.random.fold_in(own_key, 3), *heavy), -limit, limit).astype(held_as)


def setup_inputs(seed: int = 0) -> dict:
    streams_of = jax.random.split(jax.random.key(seed), 7)
    return {
        "entry_states": noise_with(streams_of[0], (MICRO, TOKENS, D), 1.0, 6.0, ((1, 8),), (1, 2, 8, 2.0)),
        "down_proj": centred(streams_of[1], (SECTIONS, TASKS, D, R), D ** -0.5, 0.09375, ((0, 4),)),
        "up_proj": centred(streams_of[2], (SECTIONS, TASKS, D, R), R ** -0.5, 0.5, ((0, 4),)),
        "label_rows": centred(streams_of[3], (LABELS, D), (D // 16) ** -0.5, 0.375),
        "sampled_labels": touch_ends(jax.random.randint(streams_of[4], (TASKS, MICRO, TOKENS), 0, LABELS), jax.random.fold_in(streams_of[4], 1), 0, LABELS - 1).astype(jnp.int32),
        "eval_states": centred(streams_of[5], (EVAL, D), 1.0, 6.0, ((0, 8),)),
    }


norm_eps = 1e-06
merge_eps = 1e-06
soft_cap = 30.0
gelu_coef = 0.7978845608028654

def gelu_value(hidden):
    gelu_inner = gelu_coef * (hidden + 0.044715 * hidden * hidden * hidden)
    return 0.5 * hidden * (1.0 + jnp.tanh(gelu_inner))

def gelu_slope(hidden):
    gelu_inner = gelu_coef * (hidden + 0.044715 * hidden * hidden * hidden)
    tanh_value = jnp.tanh(gelu_inner)
    return 0.5 * (1.0 + tanh_value) + 0.5 * hidden * (1.0 - tanh_value * tanh_value) * gelu_coef * (1.0 + 3.0 * 0.044715 * hidden * hidden)

def block_forward(states, w_down, w_up):
    state_float = states.astype(jnp.float32)
    norm_scale = lax.rsqrt(lax.optimization_barrier(jnp.mean(state_float * state_float, axis=-1, keepdims=True)) + norm_eps)
    norm_float = state_float * norm_scale
    normed = norm_float.astype(jnp.bfloat16)
    hidden = jnp.einsum('tnd,tdr->tnr', normed.astype(jnp.float32), w_down.astype(jnp.float32))
    active = gelu_value(hidden).astype(jnp.bfloat16)
    update = jnp.einsum('tnr,tdr->tnd', active.astype(jnp.float32), w_up.astype(jnp.float32))
    output = (state_float + update).astype(jnp.bfloat16)
    return (output, (normed, norm_float, norm_scale, hidden, active))

def label_head(states, labels, label_rows):
    state_float = states.astype(jnp.float32)
    norm_scale = lax.rsqrt(lax.optimization_barrier(jnp.mean(state_float * state_float, axis=-1, keepdims=True)) + norm_eps)
    norm_float = state_float * norm_scale
    normed = norm_float.astype(jnp.bfloat16)
    logits = jnp.einsum('tnd,ld->tnl', normed.astype(jnp.float32), label_rows.astype(jnp.float32))
    tanh_bent = jnp.tanh(logits / soft_cap)
    capped = soft_cap * tanh_bent
    logprob_all = capped - jnp.log(lax.optimization_barrier(jnp.sum(jnp.exp(capped), axis=-1, keepdims=True)))
    one_hot = (labels[..., None] == jnp.arange(logprob_all.shape[-1], dtype=jnp.int32)).astype(jnp.float32)
    picked = lax.optimization_barrier(jnp.sum(logprob_all * one_hot, axis=-1))
    logit_slope = ((jnp.exp(logprob_all) - one_hot) * (1.0 - tanh_bent * tanh_bent)).astype(jnp.bfloat16)
    grad_norm = jnp.einsum('tnl,ld->tnd', logit_slope.astype(jnp.float32), label_rows.astype(jnp.float32))
    grad_states = (norm_scale * (grad_norm - norm_float * lax.optimization_barrier(jnp.mean(grad_norm * norm_float, axis=-1, keepdims=True)))).astype(jnp.bfloat16)
    return (grad_states, picked)

def block_backward(grad_out, saved, w_down, w_up):
    normed, norm_float, norm_scale, hidden, active = saved
    grad_float = grad_out.astype(jnp.float32)
    grad_act = jnp.einsum('tnd,tdr->tnr', grad_float, w_up.astype(jnp.float32))
    grad_hidden = (grad_act * gelu_slope(hidden)).astype(jnp.bfloat16)
    grad_norm = jnp.einsum('tnr,tdr->tnd', grad_hidden.astype(jnp.float32), w_down.astype(jnp.float32))
    grad_in = (grad_float + norm_scale * (grad_norm - norm_float * lax.optimization_barrier(jnp.mean(grad_norm * norm_float, axis=-1, keepdims=True)))).astype(jnp.bfloat16)
    normed_float = normed.astype(jnp.float32)
    hidden_float = grad_hidden.astype(jnp.float32)
    active_float = active.astype(jnp.float32)
    wide_square = jnp.stack([normed_float * normed_float, grad_float * grad_float], axis=1).astype(jnp.bfloat16)
    narrow_square = jnp.stack([hidden_float * hidden_float, active_float * active_float], axis=1).astype(jnp.bfloat16)
    return (grad_in, wide_square, narrow_square)

def reference(entry_states, down_proj, up_proj, label_rows, sampled_labels, eval_states):
    section_count = down_proj.shape[0]
    fisher = jnp.zeros((section_count, TASKS, 2, D, R), jnp.float32)
    picked_all = []
    for micro_index in range(MICRO):
        states = jnp.broadcast_to(entry_states[micro_index][None], (TASKS, TOKENS, D))
        inputs = []
        for section_step in range(section_count):
            inputs.append(states)
            states, _ = block_forward(states, down_proj[section_step], up_proj[section_step])
        grad_out, picked = label_head(states, sampled_labels[:, micro_index, :], label_rows)
        picked_all.append(picked)
        for section_step in reversed(range(section_count)):
            _, saved = block_forward(inputs[section_step], down_proj[section_step], up_proj[section_step])
            grad_out, wide_square, narrow_square = block_backward(grad_out, saved, down_proj[section_step], up_proj[section_step])
            term = jnp.einsum('tknd,tknr->tkdr', wide_square.astype(jnp.float32), narrow_square.astype(jnp.float32))
            fisher = fisher.at[section_step].add(term)
    label_logprob = jnp.stack(picked_all, axis=1)
    stacked = jnp.stack([down_proj, up_proj], axis=2).astype(jnp.float32)
    numerator = lax.optimization_barrier(jnp.sum(fisher * stacked, axis=1))
    denominator = lax.optimization_barrier(jnp.sum(fisher, axis=1))
    merged = (numerator / (denominator + merge_eps)).astype(jnp.bfloat16)
    fisher_log = jnp.log(denominator + merge_eps)
    current = eval_states[None]
    outputs = []
    for section_step in range(section_count):
        current, _ = block_forward(current, merged[section_step, 0][None], merged[section_step, 1][None])
        outputs.append(current[0])
    eval_out = jnp.stack(outputs, axis=0)
    return (eval_out, label_logprob, fisher_log)
```

```python
import functools

import jax
import jax.numpy as jnp
from jax import lax
from jax.experimental import pallas as pl
from jax.experimental.pallas import tpu as pltpu
from jax.sharding import PartitionSpec as P

norm_eps = 1e-06
merge_eps = 1e-06
soft_cap = 30.0
gelu_coef = 0.7978845608028654
vmem_bytes = 56 * 1024 * 1024
bf16 = jnp.bfloat16
f32 = jnp.float32


def nt_dot(lhs, rhs):
    return lax.dot_general(lhs, rhs, (((1,), (1,)), ((), ())), preferred_element_type=f32)


def nn_dot(lhs, rhs):
    return lax.dot_general(lhs, rhs, (((1,), (0,)), ((), ())), preferred_element_type=f32)


def tn_dot(lhs, rhs):
    return lax.dot_general(lhs, rhs, (((0,), (0,)), ((), ())), preferred_element_type=f32)


def gelu_value(hidden):
    inner = gelu_coef * (hidden + 0.044715 * hidden * hidden * hidden)
    return 0.5 * hidden * (1.0 + jnp.tanh(inner))


def gelu_slope(hidden):
    inner = gelu_coef * (hidden + 0.044715 * hidden * hidden * hidden)
    tanh_value = jnp.tanh(inner)
    return 0.5 * (1.0 + tanh_value) + 0.5 * hidden * (1.0 - tanh_value * tanh_value) * gelu_coef * (
        1.0 + 3.0 * 0.044715 * hidden * hidden
    )


def row_scale(states):
    return lax.rsqrt(jnp.mean(states * states, axis=-1, keepdims=True) + norm_eps)


def square(values):
    wide = values.astype(f32)
    return (wide * wide).astype(bf16)


def forward_layer(states, w_down, w_up):
    wide = states.astype(f32)
    scale = row_scale(wide)
    normed = (wide * scale).astype(bf16)
    hidden = nn_dot(normed, w_down)
    active = gelu_value(hidden).astype(bf16)
    output = (wide + nt_dot(active, w_up)).astype(bf16)
    return output, hidden


def backward_layer(grad, states, hidden, w_down, w_up, pass_on):
    wide = states.astype(f32)
    scale = row_scale(wide)
    norm_float = wide * scale
    active = gelu_value(hidden).astype(bf16)
    grad_hidden = (nn_dot(grad, w_up) * gelu_slope(hidden)).astype(bf16)
    squares = (
        square(norm_float.astype(bf16)),
        square(grad),
        square(grad_hidden),
        square(active),
    )
    if not pass_on:
        return None, squares
    grad_norm = nt_dot(grad_hidden, w_down)
    mean = jnp.mean(grad_norm * norm_float, axis=-1, keepdims=True)
    grad_in = (grad.astype(f32) + scale * (grad_norm - norm_float * mean)).astype(bf16)
    return grad_in, squares


def label_head(states, labels, label_rows):
    wide = states.astype(f32)
    scale = row_scale(wide)
    norm_float = wide * scale
    logits = nt_dot(norm_float.astype(bf16), label_rows)
    bent = jnp.tanh(logits / soft_cap)
    capped = soft_cap * bent
    logprob = capped - jnp.log(jnp.sum(jnp.exp(capped), axis=-1, keepdims=True))
    one_hot = (labels == lax.broadcasted_iota(jnp.int32, logprob.shape, 1)).astype(f32)
    picked = jnp.sum(logprob * one_hot, axis=-1, keepdims=True)
    slope = ((jnp.exp(logprob) - one_hot) * (1.0 - bent * bent)).astype(bf16)
    grad_norm = nn_dot(slope, label_rows)
    mean = jnp.mean(grad_norm * norm_float, axis=-1, keepdims=True)
    return (scale * (grad_norm - norm_float * mean)).astype(bf16), picked


class WeightLoads:
    def __init__(self, member, own, other, held, sems):
        self.member, self.own, self.other = member, own, other
        self.held, self.sems = held, sems
        self.tasks = held[0].shape[1]

    def copies(self, kind, task):
        first = self.member * self.tasks
        yield pltpu.make_async_copy(
            self.own[kind].at[first + task],
            self.held[kind].at[self.member, task],
            self.sems.at[kind, self.member, task],
        )
        yield pltpu.make_async_copy(
            self.other[kind].at[task],
            self.held[kind].at[1 - self.member, task],
            self.sems.at[kind, 1 - self.member, task],
        )

    def start(self, task):
        for kind in range(2):
            for copy in self.copies(kind, task):
                copy.start()

    def wait(self, kind, layer, task):
        pltpu.make_async_copy(
            self.other[kind].at[task],
            self.held[kind].at[layer, task],
            self.sems.at[kind, layer, task],
        ).wait()

    def get(self, kind, layer, task):
        return self.held[kind][layer, task]


def first_forward_kernel(place, states, down, up, down_other, up_other, out, middle, hidden, held_down, held_up, sems):
    stage, member = place[0], place[1]

    @pl.when(stage == 0)
    def _():
        tasks = out.shape[0]
        loads = WeightLoads(member, (down, up), (down_other, up_other), (held_down, held_up), sems)
        for task in range(tasks):
            loads.start(task)
        for task in range(tasks):
            current = states[...]
            for layer in range(2):
                loads.wait(0, layer, task)
                loads.wait(1, layer, task)
                current, pre = forward_layer(current, loads.get(0, layer, task), loads.get(1, layer, task))
                hidden[layer, task] = pre
                if layer == 0:
                    middle[task] = current
                else:
                    out[task] = current


def first_backward_kernel(place, grad, states, middle, hidden, down, up, down_other, up_other, wide, narrow, held_down, held_up, sems):
    stage, member = place[0], place[1]

    @pl.when(stage == 0)
    def _():
        tasks = middle.shape[0]
        loads = WeightLoads(member, (down, up), (down_other, up_other), (held_down, held_up), sems)
        for task in range(tasks):
            loads.start(task)
        for task in range(tasks):
            current = grad[task]
            for layer in (1, 0):
                loads.wait(0, layer, task)
                loads.wait(1, layer, task)
                base = middle[task] if layer == 1 else states[...]
                current, squares = backward_layer(
                    current, base, hidden[layer, task],
                    loads.get(0, layer, task), loads.get(1, layer, task), layer == 1,
                )
                wide[layer, 0, task] = squares[0]
                wide[layer, 1, task] = squares[1]
                narrow[layer, 0, task] = squares[2]
                narrow[layer, 1, task] = squares[3]


def last_stage_kernel(place, states, labels, label_rows, down, up, down_other, up_other,
                      grad_out, picked, wide, narrow, middle, tops, grads, hidden, held_down, held_up, sems):
    stage, member = place[0], place[1]

    @pl.when(stage == 1)
    def _():
        tasks, rows = states.shape[0], states.shape[1]
        loads = WeightLoads(member, (down, up), (down_other, up_other), (held_down, held_up), sems)
        for task in range(tasks):
            loads.start(task)
        for task in range(tasks):
            current = states[task]
            for layer in range(2):
                loads.wait(0, layer, task)
                loads.wait(1, layer, task)
                current, pre = forward_layer(current, loads.get(0, layer, task), loads.get(1, layer, task))
                hidden[layer, task] = pre
                if layer == 0:
                    middle[task] = current
                else:
                    tops[task * rows:(task + 1) * rows] = current
        grads[...], picked[...] = label_head(tops[...], labels[...], label_rows[...])
        for task in range(tasks):
            current = grads[task * rows:(task + 1) * rows]
            for layer in (1, 0):
                base = middle[task] if layer == 1 else states[task]
                current, squares = backward_layer(
                    current, base, hidden[layer, task],
                    loads.get(0, layer, task), loads.get(1, layer, task), True,
                )
                wide[layer, 0, task] = squares[0]
                wide[layer, 1, task] = squares[1]
                narrow[layer, 0, task] = squares[2]
                narrow[layer, 1, task] = squares[3]
            grad_out[task] = current


def fisher_kernel(turns, place, *refs):
    wides, narrows = refs[:turns], refs[turns:2 * turns]
    own = refs[2 * turns:2 * turns + 2]
    other = refs[2 * turns + 2:2 * turns + 4]
    out = refs[2 * turns + 4]
    member = place[1]
    tasks = own[0].shape[0]
    for slot in range(2):
        layer = member if slot == 0 else 1 - member
        weights = own if slot == 0 else other
        for kind in range(2):
            top, total = None, None
            for task in range(tasks):
                left = jnp.concatenate([ref[layer, kind, task] for ref in wides], axis=0)
                right = jnp.concatenate([ref[layer, kind, task] for ref in narrows], axis=0)
                term = tn_dot(left, right)
                scaled = term * weights[kind][task].astype(f32)
                top = scaled if top is None else top + scaled
                total = term if total is None else total + term
            out[slot, 0, kind] = top.astype(out.dtype)
            out[slot, 1, kind] = total.astype(out.dtype)


def block_size(width):
    return max(size for size in range(128, 513, 128) if width % size == 0)


vmem = pl.BlockSpec(memory_space=pltpu.VMEM)
smem = pl.BlockSpec(memory_space=pltpu.SMEM)
hbm = pl.BlockSpec(memory_space=pl.ANY)


def send(block, axis, route):
    return lax.ppermute(block, axis, route)


def block_forward(states, w_down, w_up):
    wide = states.astype(f32)
    normed = (wide * row_scale(wide)).astype(bf16)
    hidden = jnp.einsum("nd,dr->nr", normed, w_down, preferred_element_type=f32)
    active = gelu_value(hidden).astype(bf16)
    update = jnp.einsum("nr,dr->nd", active, w_up, preferred_element_type=f32)
    return (wide + update).astype(bf16)


def local(entry_states, down_proj, up_proj, label_rows, sampled_labels, eval_states):
    section_count = lax.axis_size("section")
    section = lax.axis_index("section")
    stage, member = section // 2, section % 2
    w_down, w_up = down_proj[0], up_proj[0]
    all_tasks, width, rank = w_down.shape
    tasks = all_tasks // 2
    micro, rows, _ = entry_states.shape
    label_count = label_rows.shape[0]
    place = jnp.stack([stage, member]).astype(jnp.int32)
    sections = range(section_count)
    swap = [(i, i ^ 1) for i in sections]
    upward = [(i, i + 2) for i in sections if i + 2 < section_count]
    downward = [(i, i - 2) for i in sections if i - 2 >= 0]

    away = (1 - member) * tasks
    down_other = send(lax.dynamic_slice_in_dim(w_down, away, tasks, 0), "section", swap)
    up_other = send(lax.dynamic_slice_in_dim(w_up, away, tasks, 0), "section", swap)
    weights = (w_down, w_up, down_other, up_other)

    held = [
        pltpu.VMEM((2, tasks, width, rank), bf16),
        pltpu.VMEM((2, tasks, width, rank), bf16),
        pltpu.SemaphoreType.DMA((2, 2, tasks)),
    ]
    params = pltpu.CompilerParams(vmem_limit_bytes=vmem_bytes)
    state_type = jax.ShapeDtypeStruct((tasks, rows, width), bf16)
    hidden_type = jax.ShapeDtypeStruct((2, tasks, rows, rank), f32)
    wide_type = jax.ShapeDtypeStruct((2, 2, tasks, rows, width), bf16)
    narrow_type = jax.ShapeDtypeStruct((2, 2, tasks, rows, rank), bf16)
    layer_flops = 4 * tasks * rows * width * rank
    weight_bytes = 8 * tasks * width * rank

    def cost(layers, extra=0):
        return pl.CostEstimate(
            flops=layers * layer_flops + extra, bytes_accessed=weight_bytes, transcendentals=0
        )

    first_forward = pl.pallas_call(
        first_forward_kernel,
        out_shape=(state_type, state_type, hidden_type),
        in_specs=[smem, vmem] + [hbm] * 4,
        out_specs=(vmem,) * 3,
        scratch_shapes=held,
        compiler_params=params,
        cost_estimate=cost(2),
        name="first_forward",
    )
    first_backward = pl.pallas_call(
        first_backward_kernel,
        out_shape=(wide_type, narrow_type),
        in_specs=[smem] + [vmem] * 4 + [hbm] * 4,
        out_specs=(vmem,) * 2,
        scratch_shapes=held,
        compiler_params=params,
        cost_estimate=cost(2),
        name="first_backward",
    )
    last_stage = pl.pallas_call(
        last_stage_kernel,
        out_shape=(
            state_type,
            jax.ShapeDtypeStruct((tasks * rows, 1), f32),
            wide_type,
            narrow_type,
        ),
        in_specs=[smem] + [vmem] * 3 + [hbm] * 4,
        out_specs=(vmem,) * 4,
        scratch_shapes=[
            pltpu.VMEM((tasks, rows, width), bf16),
            pltpu.VMEM((tasks * rows, width), bf16),
            pltpu.VMEM((tasks * rows, width), bf16),
            pltpu.VMEM((2, tasks, rows, rank), f32),
        ] + held,
        compiler_params=params,
        cost_estimate=cost(4, 4 * tasks * rows * width * label_count),
        name="last_stage",
    )

    own_labels = lax.dynamic_slice_in_dim(sampled_labels, member * tasks, tasks, 0)
    label_columns = own_labels.transpose(1, 0, 2).reshape(micro, tasks * rows, 1)

    saved, arrived, returned = [], [], []
    last_squares, first_squares, picked = [], [], []
    for turn in range(micro + 3):
        if turn < micro:
            out, middle, hidden = first_forward(place, entry_states[turn], *weights)
            saved.append((entry_states[turn], middle, hidden))
            arrived.append(send(out, "section", upward))
        if 1 <= turn <= micro:
            grad, values, wide, narrow = last_stage(
                place, arrived[turn - 1], label_columns[turn - 1], label_rows, *weights
            )
            last_squares.append((wide, narrow))
            picked.append(values)
            returned.append(send(grad, "section", downward))
        if turn >= 3:
            wide, narrow = first_backward(place, returned[turn - 3], *saved[turn - 3], *weights)
            first_squares.append((wide, narrow))

    block = block_size(width)

    def fisher(squares):
        turns = len(squares)
        call = pl.pallas_call(
            functools.partial(fisher_kernel, turns),
            out_shape=jax.ShapeDtypeStruct((2, 2, 2, width, rank), bf16),
            grid_spec=pltpu.PrefetchScalarGridSpec(
                num_scalar_prefetch=1,
                grid=(width // block,),
                in_specs=[pl.BlockSpec((2, 2, tasks, rows, block), lambda i, s: (0, 0, 0, 0, i))] * turns
                + [pl.BlockSpec((2, 2, tasks, rows, rank), lambda i, s: (0, 0, 0, 0, 0))] * turns
                + [pl.BlockSpec((tasks, block, rank), lambda i, s: (s[1], i, 0))] * 2
                + [pl.BlockSpec((tasks, block, rank), lambda i, s: (0, i, 0))] * 2,
                out_specs=pl.BlockSpec((2, 2, 2, block, rank), lambda i, s: (0, 0, 0, i, 0)),
            ),
            compiler_params=params,
            cost_estimate=pl.CostEstimate(
                flops=8 * tasks * turns * rows * width * rank,
                bytes_accessed=turns * 8 * tasks * rows * width,
                transcendentals=0,
            ),
            name="fisher",
        )
        return call(place, *[w for w, _ in squares], *[n for _, n in squares], *weights)

    sums = lax.cond(stage == 1, lambda: fisher(last_squares), lambda: fisher(first_squares))
    other_sums = send(sums[1], "section", swap)
    totals = (sums[0].astype(f32) + other_sums.astype(f32)).astype(bf16)
    totals = lax.psum_scatter(totals, "dp", scatter_dimension=2, tiled=True).astype(f32)
    numerator, denominator = totals[0], totals[1]
    merged_part = (numerator / (denominator + merge_eps)).astype(bf16)
    merged = lax.all_gather(merged_part, "dp", axis=1, tiled=True)
    fisher_log = jnp.log(denominator + merge_eps)

    picked_all = jnp.stack(picked, axis=0).reshape(micro, tasks, rows)
    label_logprob = jnp.zeros((micro, rows), f32)
    for index in range(tasks):
        route = [(section_count - 2 + m, m * tasks + index) for m in range(2)]
        landed = send(picked_all[:, index], "section", route)
        label_logprob = jnp.where(section % tasks == index, landed, label_logprob)

    current = eval_states
    result = jnp.zeros_like(eval_states)
    for step in range(section_count):
        output = block_forward(current, merged[0], merged[1])
        result = jnp.where(section == step, output, result)
        if step + 1 < section_count:
            route = [(i, i + 1) for i in sections if i + 1 < section_count]
            current = send(output, "section", route)
    return (result[None], label_logprob[None], fisher_log[None])


def solution(mesh):
    placed = (
        P(None, "dp", None),
        P("section", None, None, None),
        P("section", None, None, None),
        P(),
        P(None, None, "dp"),
        P("dp", None),
    )
    return jax.shard_map(
        local,
        mesh=mesh,
        in_specs=placed,
        out_specs=(
            P("section", "dp", None),
            P("section", None, "dp"),
            P("section", None, "dp", None),
        ),
        check_vma=False,
    )
```

```python
import functools

import jax
import jax.numpy as jnp
from jax import lax
from jax.experimental import pallas as pl
from jax.experimental.pallas import tpu as pltpu
from jax.sharding import PartitionSpec as P

norm_eps = 1e-06
merge_eps = 1e-06
soft_cap = 30.0
gelu_coef = 0.7978845608028654
vmem_bytes = 56 * 1024 * 1024
bf16 = jnp.bfloat16
f32 = jnp.float32


def nt_dot(lhs, rhs):
    return lax.dot_general(lhs, rhs, (((1,), (1,)), ((), ())), preferred_element_type=f32)


def nn_dot(lhs, rhs):
    return lax.dot_general(lhs, rhs, (((1,), (0,)), ((), ())), preferred_element_type=f32)


def tn_dot(lhs, rhs):
    return lax.dot_general(lhs, rhs, (((0,), (0,)), ((), ())), preferred_element_type=f32)


def gelu_value(hidden):
    inner = gelu_coef * (hidden + 0.044715 * hidden * hidden * hidden)
    return 0.5 * hidden * (1.0 + jnp.tanh(inner))


def gelu_slope(hidden):
    inner = gelu_coef * (hidden + 0.044715 * hidden * hidden * hidden)
    tanh_value = jnp.tanh(inner)
    return 0.5 * (1.0 + tanh_value) + 0.5 * hidden * (1.0 - tanh_value * tanh_value) * gelu_coef * (
        1.0 + 3.0 * 0.044715 * hidden * hidden
    )


def row_scale(states):
    return lax.rsqrt(jnp.mean(states * states, axis=-1, keepdims=True) + norm_eps)


def square(values):
    wide = values.astype(f32)
    return (wide * wide).astype(bf16)


def label_head(states, labels, label_rows):
    wide = states.astype(f32)
    scale = row_scale(wide)
    norm_float = wide * scale
    logits = nt_dot(norm_float.astype(bf16), label_rows)
    bent = jnp.tanh(logits / soft_cap)
    capped = soft_cap * bent
    logprob = capped - jnp.log(jnp.sum(jnp.exp(capped), axis=-1, keepdims=True))
    one_hot = (labels == lax.broadcasted_iota(jnp.int32, logprob.shape, 1)).astype(f32)
    picked = jnp.sum(logprob * one_hot, axis=-1, keepdims=True)
    slope = ((jnp.exp(logprob) - one_hot) * (1.0 - bent * bent)).astype(bf16)
    grad_norm = nn_dot(slope, label_rows)
    mean = jnp.mean(grad_norm * norm_float, axis=-1, keepdims=True)
    return (scale * (grad_norm - norm_float * mean)).astype(bf16), picked


class Copies:
    def __init__(self, sems):
        self.sems, self.used = sems, 0

    def start(self, source, target):
        copy = pltpu.make_async_copy(source, target, self.sems.at[self.used])
        self.used += 1
        copy.start()
        return copy


class StageWeights:
    def __init__(self, member, own, other, held, sems):
        self.member, self.own, self.other = member, own, other
        self.held, self.sems = held, sems
        self.tasks = held[0].shape[1]

    def copy(self, kind, layer, task):
        return pltpu.make_async_copy(
            self.other[kind].at[task], self.held[kind].at[layer, task], self.sems.at[kind, layer, task]
        )

    def start(self, order):
        for kind, layer in order:
            @pl.when(self.member == layer)
            def _():
                for task in range(self.tasks):
                    pltpu.make_async_copy(
                        self.own[kind].at[layer * self.tasks + task],
                        self.held[kind].at[layer, task],
                        self.sems.at[kind, layer, task],
                    ).start()

            @pl.when(self.member != layer)
            def _():
                for task in range(self.tasks):
                    self.copy(kind, layer, task).start()

    def get(self, kind, layer):
        for task in range(self.tasks):
            self.copy(kind, layer, task).wait()
        return [self.held[kind].at[layer, task] for task in range(self.tasks)]


def forward_layers(states, w_down, w_up):
    wide = [x.astype(f32) for x in states]
    normed = [(x * row_scale(x)).astype(bf16) for x in wide]
    hidden = [nn_dot(n, w[...]) for n, w in zip(normed, w_down())]
    active = [gelu_value(h).astype(bf16) for h in hidden]
    update = [nt_dot(a, w[...]) for a, w in zip(active, w_up())]
    return [(x + u).astype(bf16) for x, u in zip(wide, update)], hidden


def backward_layers(grads, states, hidden, w_down, w_up, keep):
    grad_act = [nn_dot(g, w[...]) for g, w in zip(grads, w_up())]
    grad_hidden = [(g * gelu_slope(h)).astype(bf16) for g, h in zip(grad_act, hidden)]
    scales, norms = [], []
    for task, states_task in enumerate(states):
        wide = states_task.astype(f32)
        scales.append(row_scale(wide))
        norms.append(wide * scales[task])
        keep(0, task, square(norms[task].astype(bf16)), square(grad_hidden[task]))
        keep(1, task, square(grads[task]), square(gelu_value(hidden[task]).astype(bf16)))
    if w_down is None:
        return None
    grad_norm = [nt_dot(g, w[...]) for g, w in zip(grad_hidden, w_down())]
    result = []
    for g, s, n, gn in zip(grads, scales, norms, grad_norm):
        mean = jnp.mean(gn * n, axis=-1, keepdims=True)
        result.append((g.astype(f32) + s * (gn - n * mean)).astype(bf16))
    return result


def square_keeper(copies, waits, layer, wide, narrow, wide_out, narrow_out):
    def keep(kind, task, wide_value, narrow_value):
        wide[layer, kind, task] = wide_value
        narrow[layer, kind, task] = narrow_value
        waits.append(copies.start(wide.at[layer, kind, task], wide_out.at[layer, kind, task]))
        waits.append(copies.start(narrow.at[layer, kind, task], narrow_out.at[layer, kind, task]))

    return keep


def first_forward_kernel(turn, place, entry, down, up, down_other, up_other, out, middle, hidden,
                         base, mid, top, pre, sems, held_down, held_up, weight_sems):
    @pl.when(place[0] == 0)
    def _():
        tasks = out.shape[0]
        copies, waits = Copies(sems), []
        loaded = copies.start(entry.at[turn], base)
        weights = StageWeights(place[1], (down, up), (down_other, up_other), (held_down, held_up), weight_sems)
        weights.start([(0, 0), (1, 0), (0, 1), (1, 1)])
        loaded.wait()
        current = [base[...]] * tasks
        for layer in range(2):
            current, made = forward_layers(
                current, lambda: weights.get(0, layer), lambda: weights.get(1, layer)
            )
            held, target = (mid, middle) if layer == 0 else (top, out)
            for task in range(tasks):
                held[task] = current[task]
                waits.append(copies.start(held.at[task], target.at[task]))
                pre[layer, task] = made[task]
        waits.append(copies.start(pre, hidden))
        for copy in waits:
            copy.wait()


def first_backward_kernel(turn, place, grad, entry, middle, hidden, down, up, down_other, up_other,
                          wide_out, narrow_out, grads, base, mid, pre, wide, narrow, sems,
                          held_down, held_up, weight_sems):
    @pl.when(place[0] == 0)
    def _():
        tasks = middle.shape[0]
        copies, waits = Copies(sems), []
        loads = [
            copies.start(source, target)
            for source, target in ((grad, grads), (hidden, pre), (middle, mid), (entry.at[turn], base))
        ]
        weights = StageWeights(place[1], (down, up), (down_other, up_other), (held_down, held_up), weight_sems)
        weights.start([(1, 1), (0, 1), (1, 0)])
        for load in loads:
            load.wait()
        current = [grads[task] for task in range(tasks)]
        for layer in (1, 0):
            states = [mid[task] if layer == 1 else base[...] for task in range(tasks)]
            current = backward_layers(
                current, states, [pre[layer, task] for task in range(tasks)],
                (lambda: weights.get(0, layer)) if layer == 1 else None,
                lambda: weights.get(1, layer),
                square_keeper(copies, waits, layer, wide, narrow, wide_out, narrow_out),
            )
        for copy in waits:
            copy.wait()


def last_stage_kernel(turn, place, states, labels, label_rows, down, up, down_other, up_other,
                      grad_out, picked, wide_out, narrow_out,
                      base, mid, tops, words, marks, chosen, grads, wide, narrow, sems,
                      held_down, held_up, weight_sems):
    @pl.when(place[0] == 1)
    def _():
        tasks, rows = states.shape[0], states.shape[1]
        copies, waits = Copies(sems), []
        loaded = copies.start(states, base)
        weights = StageWeights(place[1], (down, up), (down_other, up_other), (held_down, held_up), weight_sems)
        weights.start([(0, 0), (1, 0), (0, 1), (1, 1)])
        later = [copies.start(label_rows, words), copies.start(labels.at[turn], marks)]
        loaded.wait()
        current = [base[task] for task in range(tasks)]
        hidden, down_refs, up_refs = [], [], []
        for layer in range(2):
            def take_down():
                down_refs.append(weights.get(0, layer))
                return down_refs[-1]

            def take_up():
                up_refs.append(weights.get(1, layer))
                return up_refs[-1]

            current, made = forward_layers(current, take_down, take_up)
            hidden.append(made)
            for task in range(tasks):
                if layer == 0:
                    mid[task] = current[task]
                else:
                    tops[task * rows:(task + 1) * rows] = current[task]
        for copy in later:
            copy.wait()
        grad, chosen[...] = label_head(tops[...], marks[...], words[...])
        waits.append(copies.start(chosen, picked))
        current = [grad[task * rows:(task + 1) * rows] for task in range(tasks)]
        for layer in (1, 0):
            below = [mid[task] if layer == 1 else base[task] for task in range(tasks)]
            current = backward_layers(
                current, below, hidden[layer],
                lambda: down_refs[layer], lambda: up_refs[layer],
                square_keeper(copies, waits, layer, wide, narrow, wide_out, narrow_out),
            )
        for task in range(tasks):
            grads[task] = current[task]
            waits.append(copies.start(grads.at[task], grad_out.at[task]))
        for copy in waits:
            copy.wait()


def eval_kernel(step, where, states, before, merged, out, base, top, held, sems):
    copies = Copies(sems)

    @pl.when(where[0] == step)
    def _():
        loads = [copies.start(states, base)] + [
            copies.start(merged.at[kind], held.at[kind]) for kind in range(2)
        ]
        loads[0].wait()
        wide = base[...].astype(f32)
        normed = (wide * row_scale(wide)).astype(bf16)
        loads[1].wait()
        active = gelu_value(nn_dot(normed, held[0])).astype(bf16)
        loads[2].wait()
        top[...] = (wide + nt_dot(active, held[1])).astype(bf16)
        copies.start(top, out).wait()

    @pl.when(where[0] != step)
    def _():
        copies.start(before, base).wait()
        copies.start(base, out).wait()


def fisher_kernel(turns, place, *refs):
    wides, narrows = refs[:turns], refs[turns:2 * turns]
    own = refs[2 * turns:2 * turns + 2]
    other = refs[2 * turns + 2:2 * turns + 4]
    outs = refs[2 * turns + 4:]
    member = place[1]
    tasks = own[0].shape[0]
    for slot in range(2):
        layer = member if slot == 0 else 1 - member
        weights = own if slot == 0 else other
        for kind in range(2):
            top, total = None, None
            for task in range(tasks):
                left = jnp.concatenate([ref[layer, kind, task] for ref in wides], axis=0)
                right = jnp.concatenate([ref[layer, kind, task] for ref in narrows], axis=0)
                term = tn_dot(left, right)
                scaled = term * weights[kind][task].astype(f32)
                top = scaled if top is None else top + scaled
                total = term if total is None else total + term
            outs[slot][0, kind] = top.astype(outs[slot].dtype)
            outs[slot][1, kind] = total.astype(outs[slot].dtype)


def block_size(width):
    return max(size for size in range(128, 513, 128) if width % size == 0)


smem = pl.BlockSpec(memory_space=pltpu.SMEM)
hbm = pl.BlockSpec(memory_space=pl.ANY)


def send(block, axis, route):
    return lax.ppermute(block, axis, route)


def after(value, done):
    return lax.optimization_barrier((value, done))[0]


def local(entry_states, down_proj, up_proj, label_rows, sampled_labels, eval_states):
    section_count = lax.axis_size("section")
    section = lax.axis_index("section")
    stage, member = section // 2, section % 2
    w_down, w_up = down_proj[0], up_proj[0]
    all_tasks, width, rank = w_down.shape
    tasks = all_tasks // 2
    micro, rows, _ = entry_states.shape
    label_count = label_rows.shape[0]
    place = jnp.stack([stage, member]).astype(jnp.int32)
    sections = range(section_count)
    swap = [(i, i ^ 1) for i in sections]
    upward = [(i, i + 2) for i in sections if i + 2 < section_count]
    downward = [(i, i - 2) for i in sections if i - 2 >= 0]

    away = (1 - member) * tasks
    down_other = send(lax.dynamic_slice_in_dim(w_down, away, tasks, 0), "section", swap)
    up_other = send(lax.dynamic_slice_in_dim(w_up, away, tasks, 0), "section", swap)
    weights = (w_down, w_up, down_other, up_other)

    held = [
        pltpu.VMEM((2, tasks, width, rank), bf16),
        pltpu.VMEM((2, tasks, width, rank), bf16),
        pltpu.SemaphoreType.DMA((2, 2, tasks)),
    ]
    params = pltpu.CompilerParams(vmem_limit_bytes=vmem_bytes)
    state_shape, hidden_shape = (tasks, rows, width), (2, tasks, rows, rank)
    wide_shape, narrow_shape = (2, 2, tasks, rows, width), (2, 2, tasks, rows, rank)
    state_type = jax.ShapeDtypeStruct(state_shape, bf16)
    square_types = (jax.ShapeDtypeStruct(wide_shape, bf16), jax.ShapeDtypeStruct(narrow_shape, bf16))
    square_scratch = [pltpu.VMEM(wide_shape, bf16), pltpu.VMEM(narrow_shape, bf16)]
    layer_flops = 4 * tasks * rows * width * rank
    weight_bytes = 8 * tasks * width * rank

    def stage_call(kernel, turn, name, operands, outputs, scratch, copies, flops):
        return pl.pallas_call(
            functools.partial(kernel, turn),
            out_shape=outputs,
            in_specs=[smem] + [hbm] * operands,
            out_specs=(hbm,) * len(outputs),
            scratch_shapes=scratch + [pltpu.SemaphoreType.DMA((copies,))] + held,
            compiler_params=params,
            cost_estimate=pl.CostEstimate(flops=flops, bytes_accessed=weight_bytes, transcendentals=0),
            name=name,
        )

    own_labels = lax.dynamic_slice_in_dim(sampled_labels, member * tasks, tasks, 0)
    label_columns = own_labels.transpose(1, 0, 2).reshape(micro, tasks * rows, 1)
    saved, crossing, returned, picked = {}, {}, {}, {}
    last_squares, first_squares = [], []
    token = place

    def first_forward(turn):
        nonlocal token
        call = stage_call(
            first_forward_kernel, turn, "first_forward", 5,
            (state_type, state_type, jax.ShapeDtypeStruct(hidden_shape, f32)),
            [
                pltpu.VMEM((rows, width), bf16), pltpu.VMEM(state_shape, bf16),
                pltpu.VMEM(state_shape, bf16), pltpu.VMEM(hidden_shape, f32),
            ],
            2 + 2 * tasks, 2 * layer_flops,
        )
        out, middle, hidden = call(token, entry_states, *weights)
        saved[turn] = (entry_states, middle, hidden)
        crossing[turn] = out
        token = after(place, hidden)

    def cross(turn):
        nonlocal token
        out = lax.optimization_barrier((crossing[turn], token))[0]
        crossing[turn] = send(out, "section", upward)

    def last_stage(turn):
        nonlocal token
        call = stage_call(
            last_stage_kernel, turn, "last_stage", 7,
            (state_type, jax.ShapeDtypeStruct((tasks * rows, 1), f32)) + square_types,
            [
                pltpu.VMEM(state_shape, bf16), pltpu.VMEM(state_shape, bf16),
                pltpu.VMEM((tasks * rows, width), bf16), pltpu.VMEM(label_rows.shape, bf16),
                pltpu.VMEM((tasks * rows, 1), jnp.int32), pltpu.VMEM((tasks * rows, 1), f32),
                pltpu.VMEM(state_shape, bf16),
            ] + square_scratch,
            4 + 9 * tasks, 4 * layer_flops + 4 * tasks * rows * width * label_count,
        )
        grad, picked[turn], wide, narrow = call(
            token, crossing[turn], label_columns, label_rows, *weights
        )
        last_squares.append((wide, narrow))
        returned[turn] = send(grad, "section", downward)
        token = after(place, picked[turn])

    def first_backward(turn):
        nonlocal token
        call = stage_call(
            first_backward_kernel, turn, "first_backward", 8, square_types,
            [
                pltpu.VMEM(state_shape, bf16), pltpu.VMEM((rows, width), bf16),
                pltpu.VMEM(state_shape, bf16), pltpu.VMEM(hidden_shape, f32),
            ] + square_scratch,
            4 + 8 * tasks, 2 * layer_flops,
        )
        squares = call(token, returned[turn], *saved[turn], *weights)
        first_squares.append(squares)
        token = after(place, squares[1])

    ahead, behind = min(3, micro), 2
    for turn in range(ahead):
        first_forward(turn)
        cross(turn)
    for turn in range(micro):
        if turn + ahead < micro:
            first_forward(turn + ahead)
        if turn >= behind:
            first_backward(turn - behind)
        last_stage(turn)
        if turn + ahead < micro:
            cross(turn + ahead)
    for turn in range(max(micro - behind, 0), micro):
        first_backward(turn)

    block = block_size(width)

    def fisher(squares):
        turns = len(squares)
        call = pl.pallas_call(
            functools.partial(fisher_kernel, turns),
            out_shape=(jax.ShapeDtypeStruct((2, 2, width, rank), bf16),) * 2,
            grid_spec=pltpu.PrefetchScalarGridSpec(
                num_scalar_prefetch=1,
                grid=(width // block,),
                in_specs=[pl.BlockSpec((2, 2, tasks, rows, block), lambda i, s: (0, 0, 0, 0, i))] * turns
                + [pl.BlockSpec((2, 2, tasks, rows, rank), lambda i, s: (0, 0, 0, 0, 0))] * turns
                + [pl.BlockSpec((tasks, block, rank), lambda i, s: (s[1], i, 0))] * 2
                + [pl.BlockSpec((tasks, block, rank), lambda i, s: (0, i, 0))] * 2,
                out_specs=(pl.BlockSpec((2, 2, block, rank), lambda i, s: (0, 0, i, 0)),) * 2,
            ),
            compiler_params=params,
            cost_estimate=pl.CostEstimate(
                flops=8 * tasks * turns * rows * width * rank,
                bytes_accessed=turns * 8 * tasks * rows * width,
                transcendentals=0,
            ),
            name="fisher",
        )
        return call(place, *[w for w, _ in squares], *[n for _, n in squares], *weights)

    sums = lax.cond(stage == 1, lambda: fisher(last_squares), lambda: fisher(first_squares))
    other_sums = send(sums[1], "section", swap)
    totals = (sums[0].astype(f32) + other_sums.astype(f32)).astype(bf16)

    picked_all = jnp.stack([picked[turn] for turn in range(micro)], axis=0).reshape(micro, tasks, rows)
    label_logprob = jnp.zeros((micro, rows), f32)
    for index in range(tasks):
        route = [(section_count - 2 + m, m * tasks + index) for m in range(2)]
        landed = send(picked_all[:, index], "section", route)
        label_logprob = jnp.where(section % tasks == index, landed, label_logprob)

    shares = lax.psum_scatter(totals, "dp", scatter_dimension=2, tiled=True)
    shares, label_logprob = lax.optimization_barrier((shares, label_logprob))
    numerator, denominator = shares[0].astype(f32), shares[1].astype(f32)
    merged_part = (numerator / (denominator + merge_eps)).astype(bf16)
    merged = lax.all_gather(merged_part, "dp", axis=1, tiled=True)
    fisher_log = jnp.log(denominator + merge_eps)

    where = section.astype(jnp.int32)[None]
    current, result = eval_states, eval_states
    for step in range(section_count):
        result = pl.pallas_call(
            functools.partial(eval_kernel, step),
            out_shape=jax.ShapeDtypeStruct(eval_states.shape, bf16),
            in_specs=[smem] + [hbm] * 3,
            out_specs=hbm,
            scratch_shapes=[
                pltpu.VMEM(eval_states.shape, bf16), pltpu.VMEM(eval_states.shape, bf16),
                pltpu.VMEM((2, width, rank), bf16), pltpu.SemaphoreType.DMA((6,)),
            ],
            compiler_params=pltpu.CompilerParams(vmem_limit_bytes=vmem_bytes),
            cost_estimate=pl.CostEstimate(
                flops=4 * eval_states.size * rank, bytes_accessed=4 * width * rank, transcendentals=0
            ),
            name="eval_block",
        )(where, current, result, merged)
        if step + 1 < section_count:
            current = send(result, "section", [(step, step + 1)])
    return (result[None], label_logprob[None], fisher_log[None])


def solution(mesh):
    placed = (
        P(None, "dp", None),
        P("section", None, None, None),
        P("section", None, None, None),
        P(),
        P(None, None, "dp"),
        P("dp", None),
    )
    return jax.shard_map(
        local,
        mesh=mesh,
        in_specs=placed,
        out_specs=(
            P("section", "dp", None),
            P("section", None, "dp"),
            P("section", None, "dp", None),
        ),
        check_vma=False,
    )
```

```python
import functools

import jax
import jax.numpy as jnp
from jax import lax
from jax.experimental import pallas as pl
from jax.experimental.pallas import tpu as pltpu
from jax.sharding import PartitionSpec as P

norm_eps = 1e-06
merge_eps = 1e-06
soft_cap = 30.0
gelu_coef = 0.7978845608028654
vmem_bytes = 56 * 1024 * 1024
bf16 = jnp.bfloat16
f32 = jnp.float32


def nt_dot(lhs, rhs):
    return lax.dot_general(lhs, rhs, (((1,), (1,)), ((), ())), preferred_element_type=f32)


def nn_dot(lhs, rhs):
    return lax.dot_general(lhs, rhs, (((1,), (0,)), ((), ())), preferred_element_type=f32)


def tn_dot(lhs, rhs):
    return lax.dot_general(lhs, rhs, (((0,), (0,)), ((), ())), preferred_element_type=f32)


def gelu_value(hidden):
    inner = gelu_coef * (hidden + 0.044715 * hidden * hidden * hidden)
    return 0.5 * hidden * (1.0 + jnp.tanh(inner))


def gelu_slope(hidden):
    inner = gelu_coef * (hidden + 0.044715 * hidden * hidden * hidden)
    tanh_value = jnp.tanh(inner)
    return 0.5 * (1.0 + tanh_value) + 0.5 * hidden * (1.0 - tanh_value * tanh_value) * gelu_coef * (
        1.0 + 3.0 * 0.044715 * hidden * hidden
    )


def row_scale(states):
    return lax.rsqrt(jnp.mean(states * states, axis=-1, keepdims=True) + norm_eps)


def square(values):
    wide = values.astype(f32)
    return (wide * wide).astype(bf16)


def label_head(states, labels, label_rows):
    wide = states.astype(f32)
    scale = row_scale(wide)
    norm_float = wide * scale
    logits = nt_dot(norm_float.astype(bf16), label_rows)
    bent = jnp.tanh(logits / soft_cap)
    capped = soft_cap * bent
    logprob = capped - jnp.log(jnp.sum(jnp.exp(capped), axis=-1, keepdims=True))
    one_hot = (labels == lax.broadcasted_iota(jnp.int32, logprob.shape, 1)).astype(f32)
    picked = jnp.sum(logprob * one_hot, axis=-1, keepdims=True)
    slope = ((jnp.exp(logprob) - one_hot) * (1.0 - bent * bent)).astype(bf16)
    grad_norm = nn_dot(slope, label_rows)
    mean = jnp.mean(grad_norm * norm_float, axis=-1, keepdims=True)
    return (scale * (grad_norm - norm_float * mean)).astype(bf16), picked


class Copies:
    def __init__(self, sems):
        self.sems, self.used = sems, 0

    def start(self, source, target):
        copy = pltpu.make_async_copy(source, target, self.sems.at[self.used])
        self.used += 1
        copy.start()
        return copy


class StageWeights:
    def __init__(self, member, own, other, held, sems):
        self.member, self.own, self.other = member, own, other
        self.held, self.sems = held, sems
        self.tasks = held[0].shape[1]

    def copy(self, kind, layer, task):
        return pltpu.make_async_copy(
            self.other[kind].at[task], self.held[kind].at[layer, task], self.sems.at[kind, layer, task]
        )

    def start(self, order):
        for kind, layer in order:
            @pl.when(self.member == layer)
            def _():
                for task in range(self.tasks):
                    pltpu.make_async_copy(
                        self.own[kind].at[layer * self.tasks + task],
                        self.held[kind].at[layer, task],
                        self.sems.at[kind, layer, task],
                    ).start()

            @pl.when(self.member != layer)
            def _():
                for task in range(self.tasks):
                    self.copy(kind, layer, task).start()

    def get(self, kind, layer):
        for task in range(self.tasks):
            self.copy(kind, layer, task).wait()
        return [self.held[kind].at[layer, task] for task in range(self.tasks)]


def forward_layers(states, w_down, w_up):
    wide = [x.astype(f32) for x in states]
    normed = [(x * row_scale(x)).astype(bf16) for x in wide]
    hidden = [nn_dot(n, w[...]) for n, w in zip(normed, w_down())]
    active = [gelu_value(h).astype(bf16) for h in hidden]
    update = [nt_dot(a, w[...]) for a, w in zip(active, w_up())]
    return [(x + u).astype(bf16) for x, u in zip(wide, update)], hidden


def backward_layers(grads, states, hidden, w_down, w_up, keep):
    grad_act = [nn_dot(g, w[...]) for g, w in zip(grads, w_up())]
    grad_hidden = [(g * gelu_slope(h)).astype(bf16) for g, h in zip(grad_act, hidden)]
    scales, norms = [], []
    for task, states_task in enumerate(states):
        wide = states_task.astype(f32)
        scales.append(row_scale(wide))
        norms.append(wide * scales[task])
        keep(0, task, square(norms[task].astype(bf16)), square(grad_hidden[task]))
        keep(1, task, square(grads[task]), square(gelu_value(hidden[task]).astype(bf16)))
    if w_down is None:
        return None
    grad_norm = [nt_dot(g, w[...]) for g, w in zip(grad_hidden, w_down())]
    result = []
    for g, s, n, gn in zip(grads, scales, norms, grad_norm):
        mean = jnp.mean(gn * n, axis=-1, keepdims=True)
        result.append((g.astype(f32) + s * (gn - n * mean)).astype(bf16))
    return result


def square_keeper(copies, waits, layer, wide, narrow, wide_out, narrow_out):
    def keep(kind, task, wide_value, narrow_value):
        wide[layer, kind, task] = wide_value
        narrow[layer, kind, task] = narrow_value
        waits.append(copies.start(wide.at[layer, kind, task], wide_out.at[layer, kind, task]))
        waits.append(copies.start(narrow.at[layer, kind, task], narrow_out.at[layer, kind, task]))

    return keep


def first_forward_kernel(place, entry, down, up, down_other, up_other, out, middle, hidden,
                         base, mid, top, pre, sems, held_down, held_up, weight_sems):
    @pl.when(place[0] == 0)
    def _():
        tasks = out.shape[0]
        copies, waits = Copies(sems), []
        loaded = copies.start(entry.at[place[2]], base)
        weights = StageWeights(place[1], (down, up), (down_other, up_other), (held_down, held_up), weight_sems)
        weights.start([(0, 0), (1, 0), (0, 1), (1, 1)])
        loaded.wait()
        current = [base[...]] * tasks
        for layer in range(2):
            current, made = forward_layers(
                current, lambda: weights.get(0, layer), lambda: weights.get(1, layer)
            )
            held, target = (mid, middle) if layer == 0 else (top, out)
            for task in range(tasks):
                held[task] = current[task]
                waits.append(copies.start(held.at[task], target.at[task]))
                pre[layer, task] = made[task]
        waits.append(copies.start(pre, hidden))
        for copy in waits:
            copy.wait()


def first_backward_kernel(place, grad, entry, middle, hidden, down, up, down_other, up_other,
                          wide_out, narrow_out, grads, base, mid, pre, wide, narrow, sems,
                          held_down, held_up, weight_sems):
    @pl.when(place[0] == 0)
    def _():
        tasks = middle.shape[0]
        copies, waits = Copies(sems), []
        loads = [
            copies.start(source, target)
            for source, target in ((grad, grads), (hidden, pre), (middle, mid), (entry.at[place[2]], base))
        ]
        weights = StageWeights(place[1], (down, up), (down_other, up_other), (held_down, held_up), weight_sems)
        weights.start([(1, 1), (0, 1), (1, 0)])
        for load in loads:
            load.wait()
        current = [grads[task] for task in range(tasks)]
        for layer in (1, 0):
            states = [mid[task] if layer == 1 else base[...] for task in range(tasks)]
            current = backward_layers(
                current, states, [pre[layer, task] for task in range(tasks)],
                (lambda: weights.get(0, layer)) if layer == 1 else None,
                lambda: weights.get(1, layer),
                square_keeper(copies, waits, layer, wide, narrow, wide_out, narrow_out),
            )
        for copy in waits:
            copy.wait()


def last_stage_kernel(place, states, labels, label_rows, down, up, down_other, up_other,
                      grad_out, picked, wide_out, narrow_out,
                      base, mid, tops, words, marks, chosen, grads, wide, narrow, sems,
                      held_down, held_up, weight_sems):
    @pl.when(place[0] == 1)
    def _():
        tasks, rows = states.shape[0], states.shape[1]
        copies, waits = Copies(sems), []
        loaded = copies.start(states, base)
        weights = StageWeights(place[1], (down, up), (down_other, up_other), (held_down, held_up), weight_sems)
        weights.start([(0, 0), (1, 0), (0, 1), (1, 1)])
        later = [copies.start(label_rows, words), copies.start(labels.at[place[2]], marks)]
        loaded.wait()
        current = [base[task] for task in range(tasks)]
        hidden, down_refs, up_refs = [], [], []
        for layer in range(2):
            def take_down():
                down_refs.append(weights.get(0, layer))
                return down_refs[-1]

            def take_up():
                up_refs.append(weights.get(1, layer))
                return up_refs[-1]

            current, made = forward_layers(current, take_down, take_up)
            hidden.append(made)
            for task in range(tasks):
                if layer == 0:
                    mid[task] = current[task]
                else:
                    tops[task * rows:(task + 1) * rows] = current[task]
        for copy in later:
            copy.wait()
        grad, chosen[...] = label_head(tops[...], marks[...], words[...])
        waits.append(copies.start(chosen, picked))
        current = [grad[task * rows:(task + 1) * rows] for task in range(tasks)]
        for layer in (1, 0):
            below = [mid[task] if layer == 1 else base[task] for task in range(tasks)]
            current = backward_layers(
                current, below, hidden[layer],
                lambda: down_refs[layer], lambda: up_refs[layer],
                square_keeper(copies, waits, layer, wide, narrow, wide_out, narrow_out),
            )
        for task in range(tasks):
            grads[task] = current[task]
            waits.append(copies.start(grads.at[task], grad_out.at[task]))
        for copy in waits:
            copy.wait()


def eval_kernel(step, where, states, before, *refs):
    *pieces, out, base, top, held, sems = refs
    copies = Copies(sems)
    rows = pieces[0].shape[1]

    @pl.when(where[0] == step)
    def _():
        loads = [[copies.start(states, base)], [], []]
        for kind in range(2):
            for index, piece in enumerate(pieces):
                spot = pl.ds(pl.multiple_of(where[1 + index] * rows, 16), rows)
                loads[1 + kind].append(copies.start(piece.at[kind], held.at[kind, spot]))
        for load in loads[0]:
            load.wait()
        wide = base[...].astype(f32)
        normed = (wide * row_scale(wide)).astype(bf16)
        for load in loads[1]:
            load.wait()
        active = gelu_value(nn_dot(normed, held[0])).astype(bf16)
        for load in loads[2]:
            load.wait()
        top[...] = (wide + nt_dot(active, held[1])).astype(bf16)
        copies.start(top, out).wait()

    @pl.when(where[0] != step)
    def _():
        copies.start(before, base).wait()
        copies.start(base, out).wait()


def fisher_kernel(turns, place, *refs):
    wides, narrows = refs[:turns], refs[turns:2 * turns]
    own = refs[2 * turns:2 * turns + 2]
    other = refs[2 * turns + 2:2 * turns + 4]
    outs = refs[2 * turns + 4:]
    member = place[1]
    tasks = own[0].shape[0]
    for slot in range(2):
        layer = member if slot == 0 else 1 - member
        weights = own if slot == 0 else other
        for kind in range(2):
            top, total = None, None
            for task in range(tasks):
                left = jnp.concatenate([ref[layer, kind, task] for ref in wides], axis=0)
                right = jnp.concatenate([ref[layer, kind, task] for ref in narrows], axis=0)
                term = tn_dot(left, right)
                scaled = term * weights[kind][task].astype(f32)
                top = scaled if top is None else top + scaled
                total = term if total is None else total + term
            outs[slot][0, kind] = top.astype(outs[slot].dtype)
            outs[slot][1, kind] = total.astype(outs[slot].dtype)


def block_size(width):
    return max(size for size in range(128, 513, 128) if width % size == 0)


smem = pl.BlockSpec(memory_space=pltpu.SMEM)
hbm = pl.BlockSpec(memory_space=pl.ANY)


def send(block, axis, route):
    return lax.ppermute(block, axis, route)


def ring_order(count):
    if count % 2:
        return list(range(count))
    return list(range(0, count, 2)) + list(range(count - 1, 0, -2))


def ring_place(axis):
    count = lax.axis_size(axis)
    order = ring_order(count)
    spots = [order.index(device) for device in range(count)]
    spot = jnp.array(spots, jnp.int32)[lax.axis_index(axis)]
    table = jnp.array(order, jnp.int32)

    def block_at(offset):
        return table[lax.rem(spot + offset + 2 * count, count)]

    ahead = [(order[i], order[(i + 1) % count]) for i in range(count)]
    back = [(j, i) for i, j in ahead]
    return count, block_at, ahead, back


def ring_scatter(own, other, axis):
    count, block_at, ahead, back = ring_place(axis)
    rows = own.shape[2] // count

    def part(index, block):
        return sum(
            lax.dynamic_slice_in_dim(array[index], block * rows, rows, 1).astype(f32) for array in (own, other)
        )

    moving = [part(0, block_at(-1)).astype(bf16), part(1, block_at(1)).astype(bf16)]
    for step in range(count - 1):
        last = step == count - 2
        landed = [send(moving[0], axis, ahead), send(moving[1], axis, back)]
        sums = [
            landed[0].astype(f32) + part(0, block_at(-2 - step)),
            landed[1].astype(f32) + part(1, block_at(2 + step)),
        ]
        moving = sums if last else [value.astype(bf16) for value in sums]
    return moving


def ring_gather(own, axis):
    count, block_at, ahead, back = ring_place(axis)
    pieces, blocks = [own], [block_at(0)]
    down = up = own
    for step in range(1, count // 2 + 1):
        down = send(down, axis, ahead)
        pieces.append(down)
        blocks.append(block_at(-step))
        if len(pieces) < count:
            up = send(up, axis, back)
            pieces.append(up)
            blocks.append(block_at(step))
    return pieces, blocks


def after(value, done):
    return lax.optimization_barrier((value, done))[0]


def local(entry_states, down_proj, up_proj, label_rows, sampled_labels, eval_states):
    section_count = lax.axis_size("section")
    section = lax.axis_index("section")
    stage, member = section // 2, section % 2
    w_down, w_up = down_proj[0], up_proj[0]
    all_tasks, width, rank = w_down.shape
    tasks = all_tasks // 2
    micro, rows, _ = entry_states.shape
    label_count = label_rows.shape[0]
    place = jnp.stack([stage, member]).astype(jnp.int32)
    sections = range(section_count)
    swap = [(i, i ^ 1) for i in sections]
    upward = [(i, i + 2) for i in sections if i + 2 < section_count]
    downward = [(i, i - 2) for i in sections if i - 2 >= 0]

    away = (1 - member) * tasks
    down_other = send(lax.dynamic_slice_in_dim(w_down, away, tasks, 0), "section", swap)
    up_other = send(lax.dynamic_slice_in_dim(w_up, away, tasks, 0), "section", swap)
    weights = (w_down, w_up, down_other, up_other)

    held = [
        pltpu.VMEM((2, tasks, width, rank), bf16),
        pltpu.VMEM((2, tasks, width, rank), bf16),
        pltpu.SemaphoreType.DMA((2, 2, tasks)),
    ]
    params = pltpu.CompilerParams(vmem_limit_bytes=vmem_bytes)
    state_shape, hidden_shape = (tasks, rows, width), (2, tasks, rows, rank)
    wide_shape, narrow_shape = (2, 2, tasks, rows, width), (2, 2, tasks, rows, rank)
    state_type = jax.ShapeDtypeStruct(state_shape, bf16)
    square_types = (jax.ShapeDtypeStruct(wide_shape, bf16), jax.ShapeDtypeStruct(narrow_shape, bf16))
    square_scratch = [pltpu.VMEM(wide_shape, bf16), pltpu.VMEM(narrow_shape, bf16)]
    layer_flops = 4 * tasks * rows * width * rank
    weight_bytes = 8 * tasks * width * rank

    def stage_call(kernel, name, operands, outputs, scratch, copies, flops):
        return pl.pallas_call(
            kernel,
            out_shape=outputs,
            in_specs=[smem] + [hbm] * operands,
            out_specs=(hbm,) * len(outputs),
            scratch_shapes=scratch + [pltpu.SemaphoreType.DMA((copies,))] + held,
            compiler_params=params,
            cost_estimate=pl.CostEstimate(flops=flops, bytes_accessed=weight_bytes, transcendentals=0),
            name=name,
        )

    own_labels = lax.dynamic_slice_in_dim(sampled_labels, member * tasks, tasks, 0)
    label_columns = own_labels.transpose(1, 0, 2).reshape(micro, tasks * rows, 1)
    saved, crossing, returned, picked = {}, {}, {}, {}
    last_squares, first_squares = [], []
    token = place

    def at_turn(turn):
        return jnp.concatenate([token, jnp.full((1,), turn, jnp.int32)])

    def first_forward(turn):
        nonlocal token
        call = stage_call(
            first_forward_kernel, "first_forward", 5,
            (state_type, state_type, jax.ShapeDtypeStruct(hidden_shape, f32)),
            [
                pltpu.VMEM((rows, width), bf16), pltpu.VMEM(state_shape, bf16),
                pltpu.VMEM(state_shape, bf16), pltpu.VMEM(hidden_shape, f32),
            ],
            2 + 2 * tasks, 2 * layer_flops,
        )
        out, middle, hidden = call(at_turn(turn), entry_states, *weights)
        saved[turn] = (entry_states, middle, hidden)
        crossing[turn] = out
        token = after(place, hidden)

    def cross(turn):
        nonlocal token
        out = lax.optimization_barrier((crossing[turn], token))[0]
        crossing[turn] = send(out, "section", upward)

    def last_stage(turn):
        nonlocal token
        call = stage_call(
            last_stage_kernel, "last_stage", 7,
            (state_type, jax.ShapeDtypeStruct((tasks * rows, 1), f32)) + square_types,
            [
                pltpu.VMEM(state_shape, bf16), pltpu.VMEM(state_shape, bf16),
                pltpu.VMEM((tasks * rows, width), bf16), pltpu.VMEM(label_rows.shape, bf16),
                pltpu.VMEM((tasks * rows, 1), jnp.int32), pltpu.VMEM((tasks * rows, 1), f32),
                pltpu.VMEM(state_shape, bf16),
            ] + square_scratch,
            4 + 9 * tasks, 4 * layer_flops + 4 * tasks * rows * width * label_count,
        )
        grad, picked[turn], wide, narrow = call(
            at_turn(turn), crossing[turn], label_columns, label_rows, *weights
        )
        last_squares.append((wide, narrow))
        returned[turn] = send(grad, "section", downward)
        token = after(place, picked[turn])

    def first_backward(turn):
        nonlocal token
        call = stage_call(
            first_backward_kernel, "first_backward", 8, square_types,
            [
                pltpu.VMEM(state_shape, bf16), pltpu.VMEM((rows, width), bf16),
                pltpu.VMEM(state_shape, bf16), pltpu.VMEM(hidden_shape, f32),
            ] + square_scratch,
            4 + 8 * tasks, 2 * layer_flops,
        )
        squares = call(at_turn(turn), returned[turn], *saved[turn], *weights)
        first_squares.append(squares)
        token = after(place, squares[1])

    ahead, behind = min(3, micro), 2
    for turn in range(ahead):
        first_forward(turn)
        cross(turn)
    for turn in range(micro):
        if turn + ahead < micro:
            first_forward(turn + ahead)
        if turn >= behind:
            first_backward(turn - behind)
            if turn + 1 in crossing:
                token = after(token, crossing[turn + 1])
        last_stage(turn)
        if turn + ahead < micro:
            cross(turn + ahead)
    picked_all = jnp.stack([picked[turn] for turn in range(micro)], axis=0).reshape(micro, tasks, rows)
    label_logprob = jnp.zeros((micro, rows), f32)
    for index in range(tasks):
        route = [(section_count - 2 + m, m * tasks + index) for m in range(2)]
        landed = send(picked_all[:, index], "section", route)
        label_logprob = jnp.where(section % tasks == index, landed, label_logprob)

    token = after(place, label_logprob)
    for turn in range(max(micro - behind, 0), micro):
        first_backward(turn)

    block = block_size(width)

    def fisher(squares):
        turns = len(squares)
        call = pl.pallas_call(
            functools.partial(fisher_kernel, turns),
            out_shape=(jax.ShapeDtypeStruct((2, 2, width, rank), bf16),) * 2,
            grid_spec=pltpu.PrefetchScalarGridSpec(
                num_scalar_prefetch=1,
                grid=(width // block,),
                in_specs=[pl.BlockSpec((2, 2, tasks, rows, block), lambda i, s: (0, 0, 0, 0, i))] * turns
                + [pl.BlockSpec((2, 2, tasks, rows, rank), lambda i, s: (0, 0, 0, 0, 0))] * turns
                + [pl.BlockSpec((tasks, block, rank), lambda i, s: (s[1], i, 0))] * 2
                + [pl.BlockSpec((tasks, block, rank), lambda i, s: (0, i, 0))] * 2,
                out_specs=(pl.BlockSpec((2, 2, block, rank), lambda i, s: (0, 0, i, 0)),) * 2,
            ),
            compiler_params=params,
            cost_estimate=pl.CostEstimate(
                flops=8 * tasks * turns * rows * width * rank,
                bytes_accessed=turns * 8 * tasks * rows * width,
                transcendentals=0,
            ),
            name="fisher",
        )
        return call(place, *[w for w, _ in squares], *[n for _, n in squares], *weights)

    sums = lax.cond(stage == 1, lambda: fisher(last_squares), lambda: fisher(first_squares))
    other_sums = send(sums[1], "section", swap)
    shares = ring_scatter(sums[0], other_sums, "dp")
    numerator, denominator = shares
    merged_part = (numerator / (denominator + merge_eps)).astype(bf16)
    pieces, blocks = ring_gather(merged_part, "dp")
    fisher_log = jnp.log(denominator + merge_eps)

    where = jnp.stack([section] + blocks).astype(jnp.int32)
    current, result = eval_states, eval_states
    for step in range(section_count):
        result = pl.pallas_call(
            functools.partial(eval_kernel, step),
            out_shape=jax.ShapeDtypeStruct(eval_states.shape, bf16),
            in_specs=[smem] + [hbm] * (2 + len(pieces)),
            out_specs=hbm,
            scratch_shapes=[
                pltpu.VMEM(eval_states.shape, bf16), pltpu.VMEM(eval_states.shape, bf16),
                pltpu.VMEM((2, width, rank), bf16), pltpu.SemaphoreType.DMA((4 + 2 * len(pieces),)),
            ],
            compiler_params=pltpu.CompilerParams(vmem_limit_bytes=vmem_bytes),
            cost_estimate=pl.CostEstimate(
                flops=4 * eval_states.size * rank, bytes_accessed=4 * width * rank, transcendentals=0
            ),
            name="eval_block",
        )(where, current, result, *pieces)
        if step + 1 < section_count:
            current = send(result, "section", [(step, step + 1)])
    return (result[None], label_logprob[None], fisher_log[None])


def solution(mesh):
    placed = (
        P(None, "dp", None),
        P("section", None, None, None),
        P("section", None, None, None),
        P(),
        P(None, None, "dp"),
        P("dp", None),
    )
    return jax.shard_map(
        local,
        mesh=mesh,
        in_specs=placed,
        out_specs=(
            P("section", "dp", None),
            P("section", None, "dp"),
            P("section", None, "dp", None),
        ),
        check_vma=False,
    )
```

```python
import functools

import jax
import jax.numpy as jnp
from jax import lax
from jax.experimental import pallas as pl
from jax.experimental.pallas import tpu as pltpu
from jax.sharding import PartitionSpec as P

norm_eps = 1e-06
merge_eps = 1e-06
soft_cap = 30.0
gelu_coef = 0.7978845608028654
vmem_bytes = 56 * 1024 * 1024
bf16 = jnp.bfloat16
f32 = jnp.float32


def nt_dot(lhs, rhs):
    return lax.dot_general(lhs, rhs, (((1,), (1,)), ((), ())), preferred_element_type=f32)


def nn_dot(lhs, rhs):
    return lax.dot_general(lhs, rhs, (((1,), (0,)), ((), ())), preferred_element_type=f32)


def tn_dot(lhs, rhs):
    return lax.dot_general(lhs, rhs, (((0,), (0,)), ((), ())), preferred_element_type=f32)


def gelu_value(hidden):
    inner = gelu_coef * (hidden + 0.044715 * hidden * hidden * hidden)
    return 0.5 * hidden * (1.0 + jnp.tanh(inner))


def gelu_slope(hidden):
    inner = gelu_coef * (hidden + 0.044715 * hidden * hidden * hidden)
    tanh_value = jnp.tanh(inner)
    return 0.5 * (1.0 + tanh_value) + 0.5 * hidden * (1.0 - tanh_value * tanh_value) * gelu_coef * (
        1.0 + 3.0 * 0.044715 * hidden * hidden
    )


def row_scale(states):
    return lax.rsqrt(jnp.mean(states * states, axis=-1, keepdims=True) + norm_eps)


def square(values):
    wide = values.astype(f32)
    return (wide * wide).astype(bf16)


def label_head(states, labels, label_rows):
    wide = states.astype(f32)
    scale = row_scale(wide)
    norm_float = wide * scale
    logits = nt_dot(norm_float.astype(bf16), label_rows)
    bent = jnp.tanh(logits / soft_cap)
    capped = soft_cap * bent
    logprob = capped - jnp.log(jnp.sum(jnp.exp(capped), axis=-1, keepdims=True))
    one_hot = (labels == lax.broadcasted_iota(jnp.int32, logprob.shape, 1)).astype(f32)
    picked = jnp.sum(logprob * one_hot, axis=-1, keepdims=True)
    slope = ((jnp.exp(logprob) - one_hot) * (1.0 - bent * bent)).astype(bf16)
    grad_norm = nn_dot(slope, label_rows)
    mean = jnp.mean(grad_norm * norm_float, axis=-1, keepdims=True)
    return (scale * (grad_norm - norm_float * mean)).astype(bf16), picked


class Copies:
    def __init__(self, sems):
        self.sems, self.used = sems, 0

    def start(self, source, target):
        copy = pltpu.make_async_copy(source, target, self.sems.at[self.used])
        self.used += 1
        copy.start()
        return copy


class StageWeights:
    def __init__(self, member, own, other, held, sems):
        self.member, self.own, self.other = member, own, other
        self.held, self.sems = held, sems
        self.tasks = held[0].shape[1]

    def copy(self, kind, layer, task):
        return pltpu.make_async_copy(
            self.other[kind].at[task], self.held[kind].at[layer, task], self.sems.at[kind, layer, task]
        )

    def start(self, order):
        for kind, layer in order:
            @pl.when(self.member == layer)
            def _():
                for task in range(self.tasks):
                    pltpu.make_async_copy(
                        self.own[kind].at[layer * self.tasks + task],
                        self.held[kind].at[layer, task],
                        self.sems.at[kind, layer, task],
                    ).start()

            @pl.when(self.member != layer)
            def _():
                for task in range(self.tasks):
                    self.copy(kind, layer, task).start()

    def wait(self, kind, layer, task):
        self.copy(kind, layer, task).wait()


def forward_loop(levels, hidden, weights, held_down, held_up, done):
    tasks = levels.shape[1]

    @pl.loop(0, 2 * tasks)
    def _(index):
        layer, task = index // tasks, index % tasks
        wide = levels[layer, task].astype(f32)
        normed = (wide * row_scale(wide)).astype(bf16)
        weights.wait(0, layer, task)
        pre = nn_dot(normed, held_down[layer, task])
        hidden[layer, task] = pre
        active = gelu_value(pre).astype(bf16)
        weights.wait(1, layer, task)
        update = nt_dot(active, held_up[layer, task])
        levels[layer + 1, task] = (levels[layer, task].astype(f32) + update).astype(bf16)
        done(layer, task)


class Squares:
    def __init__(self, wide, narrow, wide_out, narrow_out, sems):
        self.pairs = ((wide, wide_out), (narrow, narrow_out))
        self.sems = sems

    def copy(self, width, layer, kind, task):
        source, target = self.pairs[width]
        return pltpu.make_async_copy(
            source.at[layer, kind, task], target.at[layer, kind, task], self.sems.at[width, layer, kind, task]
        )

    def keep(self, layer, kind, task, wide, narrow):
        self.pairs[0][0][layer, kind, task] = wide
        self.pairs[1][0][layer, kind, task] = narrow
        for width in range(2):
            self.copy(width, layer, kind, task).start()

    def wait(self):
        tasks = self.pairs[0][0].shape[2]

        @pl.loop(0, 2 * tasks)
        def _(index):
            for kind in range(2):
                for width in range(2):
                    self.copy(width, index // tasks, kind, index % tasks).wait()


def backward_step(layer, task, levels, grads, hidden, weights, held_down, held_up, squares, pass_on):
    grad = grads[layer + 1, task]
    pre = hidden[layer, task]
    if weights is not None:
        weights.wait(1, layer, task)
    grad_hidden = (nn_dot(grad, held_up[layer, task]) * gelu_slope(pre)).astype(bf16)
    if weights is not None and pass_on:
        weights.wait(0, layer, task)
    wide = levels[layer, task].astype(f32)
    scale = row_scale(wide)
    norm = wide * scale
    squares.keep(layer, 0, task, square(norm.astype(bf16)), square(grad_hidden))
    squares.keep(layer, 1, task, square(grad), square(gelu_value(pre).astype(bf16)))
    if pass_on:
        grad_norm = nt_dot(grad_hidden, held_down[layer, task])
        mean = jnp.mean(grad_norm * norm, axis=-1, keepdims=True)
        grads[layer, task] = (grad.astype(f32) + scale * (grad_norm - norm * mean)).astype(bf16)


def first_forward_kernel(turn, place, entry, down, up, down_other, up_other, out, middle, hidden,
                         levels, pre, sems, held_down, held_up, weight_sems):
    @pl.when(place[0] == 0)
    def _():
        tasks = out.shape[0]
        copies = Copies(sems)
        loads = [copies.start(entry.at[turn], levels.at[0, task]) for task in range(tasks)]
        weights = StageWeights(place[1], (down, up), (down_other, up_other), (held_down, held_up), weight_sems)
        weights.start([(0, 0), (1, 0), (0, 1), (1, 1)])
        for load in loads:
            load.wait()
        base = copies.used

        def leave(layer, task):
            return pltpu.make_async_copy(
                levels.at[layer + 1, task], (middle, out)[layer].at[task], sems.at[base + layer * tasks + task]
            )

        def done(layer, task):
            for fixed in range(2):
                @pl.when(layer == fixed)
                def _():
                    leave(fixed, task).start()

        forward_loop(levels, pre, weights, held_down, held_up, done)
        last = pltpu.make_async_copy(pre, hidden, sems.at[0])
        last.start()
        for layer in range(2):
            for task in range(tasks):
                leave(layer, task).wait()
        last.wait()


def first_backward_kernel(turn, place, grad, entry, middle, hidden, wide_in, narrow_in, down, up, down_other, up_other,
                          wide_out, narrow_out, grads, levels, pre, wide, narrow, square_sems, sems,
                          held_down, held_up, weight_sems):
    del wide_in, narrow_in

    @pl.when(place[0] == 0)
    def _():
        tasks = middle.shape[0]
        copies = Copies(sems)
        loads = [copies.start(grad, grads.at[2]), copies.start(hidden, pre), copies.start(middle, levels.at[1])]
        weights = StageWeights(place[1], (down, up), (down_other, up_other), (held_down, held_up), weight_sems)
        weights.start([(1, 1), (0, 1), (1, 0)])
        loads += [copies.start(entry.at[turn], levels.at[0, task]) for task in range(tasks)]
        squares = Squares(wide, narrow, wide_out, narrow_out, square_sems)
        for load in loads:
            load.wait()
        for layer in (1, 0):
            @pl.loop(0, tasks)
            def _(task):
                backward_step(
                    layer, task, levels, grads, pre, weights, held_down, held_up, squares, layer == 1
                )
        squares.wait()


def last_stage_kernel(turn, place, states, labels, label_rows, down, up, down_other, up_other,
                      grad_out, picked, wide_out, narrow_out,
                      levels, words, marks, chosen, pre, grads, wide, narrow, square_sems, sems,
                      held_down, held_up, weight_sems):
    @pl.when(place[0] == 1)
    def _():
        tasks, rows = states.shape[0], states.shape[1]
        copies = Copies(sems)
        loaded = copies.start(states, levels.at[0])
        weights = StageWeights(place[1], (down, up), (down_other, up_other), (held_down, held_up), weight_sems)
        weights.start([(0, 0), (1, 0), (0, 1), (1, 1)])
        later = [copies.start(label_rows, words), copies.start(labels.at[turn], marks)]
        loaded.wait()
        forward_loop(levels, pre, weights, held_down, held_up, lambda layer, task: None)
        for copy in later:
            copy.wait()

        @pl.loop(0, tasks)
        def _(task):
            grad, values = label_head(levels[2, task], marks[task], words[...])
            grads[2, task] = grad
            chosen[task] = jnp.broadcast_to(values, (rows, 128)).T[0:8]

        out_copy = copies.start(chosen, picked)
        squares = Squares(wide, narrow, wide_out, narrow_out, square_sems)

        @pl.loop(0, 2 * tasks)
        def _(index):
            backward_step(
                1 - index // tasks, index % tasks, levels, grads, pre, None, held_down, held_up, squares, True
            )

        last = copies.start(grads.at[0], grad_out)
        squares.wait()
        out_copy.wait()
        last.wait()


def eval_kernel(step, offsets, place, states, before, *refs):
    *pieces, out, base, top, held, sems = refs
    copies = Copies(sems)
    rows = pieces[0].shape[1]

    @pl.when(place[2] == step)
    def _():
        loads = [[copies.start(states, base)], [], []]
        for kind in range(2):
            for index, piece in enumerate(pieces):
                block = block_at(place[3], offsets[index], len(pieces))
                spot = pl.ds(pl.multiple_of(block * rows, 16), rows)
                loads[1 + kind].append(copies.start(piece.at[kind], held.at[kind, spot]))
        for load in loads[0]:
            load.wait()
        wide = base[...].astype(f32)
        normed = (wide * row_scale(wide)).astype(bf16)
        for load in loads[1]:
            load.wait()
        active = gelu_value(nn_dot(normed, held[0])).astype(bf16)
        for load in loads[2]:
            load.wait()
        top[...] = (wide + nt_dot(active, held[1])).astype(bf16)
        copies.start(top, out).wait()

    @pl.when(place[2] != step)
    def _():
        copies.start(before, base).wait()
        copies.start(base, out).wait()


def fisher_kernel(turns, place, *refs):
    wides, narrows = refs[:turns], refs[turns:2 * turns]
    own = refs[2 * turns:2 * turns + 2]
    other = refs[2 * turns + 2:2 * turns + 4]
    top_out, total_out, away_out = refs[2 * turns + 4:]
    member = place[1]
    tasks = own[0].shape[0]
    for slot in range(2):
        layer = member if slot == 0 else 1 - member
        weights = own if slot == 0 else other
        for kind in range(2):
            top, total = None, None
            for task in range(tasks):
                left = jnp.concatenate([ref[layer, kind, task] for ref in wides], axis=0)
                right = jnp.concatenate([ref[layer, kind, task] for ref in narrows], axis=0)
                term = tn_dot(left, right)
                scaled = term * weights[kind][task].astype(f32)
                top = scaled if top is None else top + scaled
                total = term if total is None else total + term
            if slot == 0:
                top_out[kind] = top.astype(bf16)
                total_out[kind] = total.astype(bf16)
            else:
                away_out[0, kind] = top.astype(bf16)
                away_out[1, kind] = total.astype(bf16)


def block_size(width):
    return max(size for size in range(128, 513, 128) if width % size == 0)


smem = pl.BlockSpec(memory_space=pltpu.SMEM)
hbm = pl.BlockSpec(memory_space=pl.ANY)


def send(block, axis, route):
    return lax.ppermute(block, axis, route)


def walk(spot, count):
    if count % 2:
        return spot
    return jnp.where(spot < count // 2, 2 * spot, 2 * (count - 1 - spot) + 1)


def spot_of(device, count):
    if count % 2:
        return device
    return jnp.where(lax.rem(device, 2) == 0, lax.div(device, 2), count - 1 - lax.div(device, 2))


def block_at(spot, offset, count):
    return walk(lax.rem(spot + offset + 2 * count, count), count)


def ring_routes(axis):
    count = lax.axis_size(axis)
    order = list(range(count)) if count % 2 else list(range(0, count, 2)) + list(range(count - 1, 0, -2))
    ahead = [(order[i], order[(i + 1) % count]) for i in range(count)]
    return count, ahead, [(j, i) for i, j in ahead]


def ring_scatter(own, other, spot, axis):
    count, ahead, back = ring_routes(axis)
    rows = own[0].shape[1] // count

    def part(index, offset):
        start = block_at(spot, offset, count) * rows
        mine = lax.dynamic_slice_in_dim(own[index], start, rows, 1)
        sizes = (1,) + mine.shape
        theirs = lax.dynamic_slice(other, (index, 0, start, 0), sizes).reshape(mine.shape)
        return mine.astype(f32) + theirs.astype(f32)

    moving = [part(0, -1).astype(bf16), part(1, 1).astype(bf16)]
    for step in range(count - 1):
        last = step == count - 2
        landed = [send(moving[0], axis, ahead), send(moving[1], axis, back)]
        sums = [landed[0].astype(f32) + part(0, -2 - step), landed[1].astype(f32) + part(1, 2 + step)]
        moving = sums if last else [value.astype(bf16) for value in sums]
    return moving


def ring_gather(own, axis):
    count, ahead, back = ring_routes(axis)
    pieces, offsets = [own], [0]
    down = up = own
    for step in range(1, count // 2 + 1):
        down = send(down, axis, ahead)
        pieces.append(down)
        offsets.append(-step)
        if len(pieces) < count:
            up = send(up, axis, back)
            pieces.append(up)
            offsets.append(step)
    return pieces, offsets


def after(value, done):
    return lax.optimization_barrier((value, done))[0]


def local(entry_states, down_proj, up_proj, label_rows, sampled_labels, eval_states):
    section_count = lax.axis_size("section")
    section = lax.axis_index("section")
    stage, member = section // 2, section % 2
    w_down, w_up = down_proj[0], up_proj[0]
    all_tasks, width, rank = w_down.shape
    tasks = all_tasks // 2
    micro, rows, _ = entry_states.shape
    label_count = label_rows.shape[0]
    spot = spot_of(lax.axis_index("dp"), lax.axis_size("dp"))
    place = jnp.stack([stage, member, section, spot]).astype(jnp.int32)
    sections = range(section_count)
    swap = [(i, i ^ 1) for i in sections]
    upward = [(i, i + 2) for i in sections if i + 2 < section_count]
    downward = [(i, i - 2) for i in sections if i - 2 >= 0]

    away = (1 - member) * tasks
    down_other = send(lax.dynamic_slice_in_dim(w_down, away, tasks, 0), "section", swap)
    up_other = send(lax.dynamic_slice_in_dim(w_up, away, tasks, 0), "section", swap)
    weights = (w_down, w_up, down_other, up_other)

    held = [
        pltpu.VMEM((2, tasks, width, rank), bf16),
        pltpu.VMEM((2, tasks, width, rank), bf16),
        pltpu.SemaphoreType.DMA((2, 2, tasks)),
    ]
    params = pltpu.CompilerParams(vmem_limit_bytes=vmem_bytes)
    state_shape, hidden_shape = (tasks, rows, width), (2, tasks, rows, rank)
    wide_shape, narrow_shape = (2, 2, tasks, rows, width), (2, 2, tasks, rows, rank)
    state_type = jax.ShapeDtypeStruct(state_shape, bf16)
    square_types = (jax.ShapeDtypeStruct(wide_shape, bf16), jax.ShapeDtypeStruct(narrow_shape, bf16))
    square_scratch = [
        pltpu.VMEM(wide_shape, bf16),
        pltpu.VMEM(narrow_shape, bf16),
        pltpu.SemaphoreType.DMA((2, 2, 2, tasks)),
    ]
    layer_flops = 4 * tasks * rows * width * rank
    weight_bytes = 8 * tasks * width * rank

    def stage_call(kernel, turn, name, operands, outputs, scratch, flops, **more):
        return pl.pallas_call(
            functools.partial(kernel, turn),
            out_shape=outputs,
            in_specs=[smem] + [hbm] * operands,
            out_specs=(hbm,) * len(outputs),
            scratch_shapes=scratch + held,
            compiler_params=params,
            cost_estimate=pl.CostEstimate(flops=flops, bytes_accessed=weight_bytes, transcendentals=0),
            name=name,
            **more,
        )

    own_labels = lax.dynamic_slice_in_dim(sampled_labels, member * tasks, tasks, 0)
    label_columns = own_labels.transpose(1, 0, 2).reshape(micro, tasks, rows, 1)
    saved, crossing, returned, picked = {}, {}, {}, {}
    squares = {}
    token = place

    levels, pre = pltpu.VMEM((3,) + state_shape, bf16), pltpu.VMEM(hidden_shape, f32)

    def first_forward(turn):
        nonlocal token
        call = stage_call(
            first_forward_kernel, turn, "first_forward", 5,
            (state_type, state_type, jax.ShapeDtypeStruct(hidden_shape, f32)),
            [levels, pre, pltpu.SemaphoreType.DMA((3 * tasks,))],
            2 * layer_flops,
        )
        out, middle, hidden = call(token, entry_states, *weights)
        saved[turn] = (entry_states, middle, hidden)
        crossing[turn] = out
        token = after(place, hidden)

    def cross(turn):
        nonlocal token
        out = lax.optimization_barrier((crossing[turn], token))[0]
        crossing[turn] = send(out, "section", upward)

    def last_stage(turn):
        nonlocal token
        call = stage_call(
            last_stage_kernel, turn, "last_stage", 7,
            (state_type, jax.ShapeDtypeStruct((tasks, 8, rows), f32)) + square_types,
            [
                levels, pltpu.VMEM(label_rows.shape, bf16),
                pltpu.VMEM((tasks, rows, 1), jnp.int32), pltpu.VMEM((tasks, 8, rows), f32),
                pre, levels,
            ] + square_scratch + [pltpu.SemaphoreType.DMA((5,))],
            4 * layer_flops + 4 * tasks * rows * width * label_count,
        )
        grad, picked[turn], *squares[turn] = call(
            token, crossing[turn], label_columns, label_rows, *weights
        )
        returned[turn] = send(grad, "section", downward)
        token = after(place, picked[turn])

    def first_backward(turn):
        nonlocal token
        call = stage_call(
            first_backward_kernel, turn, "first_backward", 10, square_types,
            [levels, levels, pre] + square_scratch + [pltpu.SemaphoreType.DMA((3 + tasks,))],
            2 * layer_flops,
            input_output_aliases={5: 0, 6: 1},
        )
        squares[turn] = call(token, returned[turn], *saved[turn], *squares[turn], *weights)
        token = after(place, squares[turn][1])

    ahead, behind = min(3, micro), 2
    for turn in range(ahead):
        first_forward(turn)
        cross(turn)
    for turn in range(micro):
        if turn + ahead < micro:
            first_forward(turn + ahead)
        if turn >= behind:
            first_backward(turn - behind)
            if turn + 1 in crossing:
                token = after(token, crossing[turn + 1])
        last_stage(turn)
        if turn + ahead < micro:
            cross(turn + ahead)
    picked_all = jnp.stack([picked[turn][:, 0] for turn in range(micro)], axis=0)
    label_logprob = jnp.zeros((micro, rows), f32)
    for index in range(tasks):
        route = [(section_count - 2 + m, m * tasks + index) for m in range(2)]
        landed = send(picked_all[:, index], "section", route)
        label_logprob = jnp.where(section % tasks == index, landed, label_logprob)

    token = after(place, label_logprob)
    for turn in range(max(micro - behind, 0), micro):
        first_backward(turn)

    block = block_size(width)

    def fisher(squares):
        turns = len(squares)
        call = pl.pallas_call(
            functools.partial(fisher_kernel, turns),
            out_shape=(jax.ShapeDtypeStruct((2, width, rank), bf16),) * 2
            + (jax.ShapeDtypeStruct((2, 2, width, rank), bf16),),
            grid_spec=pltpu.PrefetchScalarGridSpec(
                num_scalar_prefetch=1,
                grid=(width // block,),
                in_specs=[pl.BlockSpec((2, 2, tasks, rows, block), lambda i, s: (0, 0, 0, 0, i))] * turns
                + [pl.BlockSpec((2, 2, tasks, rows, rank), lambda i, s: (0, 0, 0, 0, 0))] * turns
                + [pl.BlockSpec((tasks, block, rank), lambda i, s: (s[1], i, 0))] * 2
                + [pl.BlockSpec((tasks, block, rank), lambda i, s: (0, i, 0))] * 2,
                out_specs=(pl.BlockSpec((2, block, rank), lambda i, s: (0, i, 0)),) * 2
                + (pl.BlockSpec((2, 2, block, rank), lambda i, s: (0, 0, i, 0)),),
            ),
            compiler_params=params,
            cost_estimate=pl.CostEstimate(
                flops=8 * tasks * turns * rows * width * rank,
                bytes_accessed=turns * 8 * tasks * rows * width,
                transcendentals=0,
            ),
            name="fisher",
        )
        return call(place, *[w for w, _ in squares], *[n for _, n in squares], *weights)

    *sums, away_sums = fisher([squares[turn] for turn in range(micro)])
    other_sums = send(away_sums, "section", swap)
    shares = ring_scatter(sums, other_sums, spot, "dp")
    numerator, denominator = shares
    merged_part = (numerator / (denominator + merge_eps)).astype(bf16)
    pieces, offsets = ring_gather(merged_part, "dp")
    fisher_log = jnp.log(denominator + merge_eps)

    current, result = eval_states, eval_states
    for step in range(section_count):
        result = pl.pallas_call(
            functools.partial(eval_kernel, step, offsets),
            out_shape=jax.ShapeDtypeStruct(eval_states.shape, bf16),
            in_specs=[smem] + [hbm] * (2 + len(pieces)),
            out_specs=hbm,
            scratch_shapes=[
                pltpu.VMEM(eval_states.shape, bf16), pltpu.VMEM(eval_states.shape, bf16),
                pltpu.VMEM((2, width, rank), bf16), pltpu.SemaphoreType.DMA((4 + 2 * len(pieces),)),
            ],
            compiler_params=pltpu.CompilerParams(vmem_limit_bytes=vmem_bytes),
            cost_estimate=pl.CostEstimate(
                flops=4 * eval_states.size * rank, bytes_accessed=4 * width * rank, transcendentals=0
            ),
            name="eval_block",
        )(place, current, result, *pieces)
        if step + 1 < section_count:
            current = send(result, "section", [(step, step + 1)])
    return (result[None], label_logprob[None], fisher_log[None])


def solution(mesh):
    placed = (
        P(None, "dp", None),
        P("section", None, None, None),
        P("section", None, None, None),
        P(),
        P(None, None, "dp"),
        P("dp", None),
    )
    return jax.shard_map(
        local,
        mesh=mesh,
        in_specs=placed,
        out_specs=(
            P("section", "dp", None),
            P("section", None, "dp"),
            P("section", None, "dp", None),
        ),
        check_vma=False,
    )
```

```python
import functools

import jax
import jax.numpy as jnp
from jax import lax
from jax.experimental import pallas as pl
from jax.experimental.pallas import tpu as pltpu
from jax.sharding import PartitionSpec as P

norm_eps = 1e-06
merge_eps = 1e-06
soft_cap = 30.0
gelu_coef = 0.7978845608028654
vmem_bytes = 36 * 1024 * 1024
bf16 = jnp.bfloat16
f32 = jnp.float32


def nt_dot(lhs, rhs):
    return lax.dot_general(lhs, rhs, (((1,), (1,)), ((), ())), preferred_element_type=f32)


def nn_dot(lhs, rhs):
    return lax.dot_general(lhs, rhs, (((1,), (0,)), ((), ())), preferred_element_type=f32)


def tn_dot(lhs, rhs):
    return lax.dot_general(lhs, rhs, (((0,), (0,)), ((), ())), preferred_element_type=f32)


def gelu_value(hidden):
    inner = gelu_coef * (hidden + 0.044715 * hidden * hidden * hidden)
    return 0.5 * hidden * (1.0 + jnp.tanh(inner))


def gelu_slope(hidden):
    inner = gelu_coef * (hidden + 0.044715 * hidden * hidden * hidden)
    tanh_value = jnp.tanh(inner)
    return 0.5 * (1.0 + tanh_value) + 0.5 * hidden * (1.0 - tanh_value * tanh_value) * gelu_coef * (
        1.0 + 3.0 * 0.044715 * hidden * hidden
    )


def row_scale(states):
    return lax.rsqrt(jnp.mean(states * states, axis=-1, keepdims=True) + norm_eps)


def square(values):
    wide = values.astype(f32)
    return (wide * wide).astype(bf16)


def label_head(states, labels, label_rows):
    wide = states.astype(f32)
    scale = row_scale(wide)
    norm_float = wide * scale
    logits = nt_dot(norm_float.astype(bf16), label_rows)
    bent = jnp.tanh(logits / soft_cap)
    capped = soft_cap * bent
    logprob = capped - jnp.log(jnp.sum(jnp.exp(capped), axis=-1, keepdims=True))
    one_hot = (labels == lax.broadcasted_iota(jnp.int32, logprob.shape, 1)).astype(f32)
    picked = jnp.sum(logprob * one_hot, axis=-1, keepdims=True)
    slope = ((jnp.exp(logprob) - one_hot) * (1.0 - bent * bent)).astype(bf16)
    grad_norm = nn_dot(slope, label_rows)
    mean = jnp.mean(grad_norm * norm_float, axis=-1, keepdims=True)
    return (scale * (grad_norm - norm_float * mean)).astype(bf16), picked


class Copies:
    def __init__(self, sems):
        self.sems, self.used = sems, 0

    def start(self, source, target):
        copy = pltpu.make_async_copy(source, target, self.sems.at[self.used])
        self.used += 1
        copy.start()
        return copy


class StageWeights:
    def __init__(self, member, own, other, held, sems):
        self.member, self.own, self.other = member, own, other
        self.held, self.sems = held, sems
        self.tasks = held[0].shape[1]

    def copy(self, kind, layer, task):
        return pltpu.make_async_copy(
            self.other[kind].at[task], self.held[kind].at[layer, task], self.sems.at[kind, layer, task]
        )

    def start(self, order):
        for kind, layer in order:
            @pl.when(self.member == layer)
            def _():
                for task in range(self.tasks):
                    pltpu.make_async_copy(
                        self.own[kind].at[layer * self.tasks + task],
                        self.held[kind].at[layer, task],
                        self.sems.at[kind, layer, task],
                    ).start()

            @pl.when(self.member != layer)
            def _():
                for task in range(self.tasks):
                    self.copy(kind, layer, task).start()

    def wait(self, kind, layer, task):
        self.copy(kind, layer, task).wait()


def forward_loop(levels, hidden, weights, held_down, held_up, done):
    tasks = range(levels.shape[1])

    @pl.loop(0, 2)
    def _(layer):
        wide = [levels[layer, task].astype(f32) for task in tasks]
        normed = [(x * row_scale(x)).astype(bf16) for x in wide]
        for task in tasks:
            weights.wait(0, layer, task)
        pre = [nn_dot(normed[task], held_down[layer, task]) for task in tasks]
        for task in tasks:
            hidden[layer, task] = pre[task]
        active = [gelu_value(h).astype(bf16) for h in pre]
        for task in tasks:
            weights.wait(1, layer, task)
        update = [nt_dot(active[task], held_up[layer, task]) for task in tasks]
        for task in tasks:
            levels[layer + 1, task] = (levels[layer, task].astype(f32) + update[task]).astype(bf16)
        done(layer)


class Squares:
    def __init__(self, wide, narrow, wide_out, narrow_out, sems):
        self.pairs = ((wide, wide_out), (narrow, narrow_out))
        self.sems = sems

    def copy(self, width, layer, kind, task):
        source, target = self.pairs[width]
        return pltpu.make_async_copy(
            source.at[layer, kind, task], target.at[layer, kind, task], self.sems.at[width, layer, kind, task]
        )

    def set(self, layer, kind, task, wide, narrow):
        self.pairs[0][0][layer, kind, task] = wide
        self.pairs[1][0][layer, kind, task] = narrow

    def start(self, layer, kind, task):
        for width in range(2):
            self.copy(width, layer, kind, task).start()

    def wait(self):
        tasks = self.pairs[0][0].shape[2]

        @pl.loop(0, 2 * tasks)
        def _(index):
            for kind in range(2):
                for width in range(2):
                    self.copy(width, index // tasks, kind, index % tasks).wait()


def backward_step(layer, levels, grads, hidden, weights, held_down, held_up, squares, pass_on):
    tasks = range(levels.shape[1])
    grad = [grads[layer + 1, task] for task in tasks]
    pre = [hidden[layer, task] for task in tasks]
    if weights is not None:
        for task in tasks:
            weights.wait(1, layer, task)
    grad_act = [nn_dot(grad[task], held_up[layer, task]) for task in tasks]
    grad_hidden = [(g * gelu_slope(h)).astype(bf16) for g, h in zip(grad_act, pre)]
    if weights is not None and pass_on:
        for task in tasks:
            weights.wait(0, layer, task)
    scales, norms = [], []
    for task in tasks:
        wide = levels[layer, task].astype(f32)
        scales.append(row_scale(wide))
        norms.append(wide * scales[task])
    if pass_on:
        grad_norm = [nt_dot(grad_hidden[task], held_down[layer, task]) for task in tasks]
    for task in tasks:
        squares.set(layer, 0, task, square(norms[task].astype(bf16)), square(grad_hidden[task]))
        squares.set(layer, 1, task, square(grad[task]), square(gelu_value(pre[task]).astype(bf16)))
    if pass_on:
        for task in tasks:
            mean = jnp.mean(grad_norm[task] * norms[task], axis=-1, keepdims=True)
            grads[layer, task] = (
                grad[task].astype(f32) + scales[task] * (grad_norm[task] - norms[task] * mean)
            ).astype(bf16)
    for task in tasks:
        for kind in range(2):
            squares.start(layer, kind, task)


def first_forward_kernel(turn, place, entry, down, up, down_other, up_other, out, middle, hidden,
                         levels, pre, sems, held_down, held_up, weight_sems):
    @pl.when(place[0] == 0)
    def _():
        tasks = out.shape[0]
        copies = Copies(sems)
        loads = [copies.start(entry.at[turn], levels.at[0, task]) for task in range(tasks)]
        weights = StageWeights(place[1], (down, up), (down_other, up_other), (held_down, held_up), weight_sems)
        weights.start([(0, 0), (1, 0), (0, 1), (1, 1)])
        for load in loads:
            load.wait()
        base = copies.used

        def leave(layer, task):
            return pltpu.make_async_copy(
                levels.at[layer + 1, task], (middle, out)[layer].at[task], sems.at[base + layer * tasks + task]
            )

        def done(layer):
            for fixed in range(2):
                @pl.when(layer == fixed)
                def _():
                    for task in range(tasks):
                        leave(fixed, task).start()

        forward_loop(levels, pre, weights, held_down, held_up, done)
        last = pltpu.make_async_copy(pre, hidden, sems.at[0])
        last.start()
        for layer in range(2):
            for task in range(tasks):
                leave(layer, task).wait()
        last.wait()


def first_backward_kernel(turn, place, grad, entry, middle, hidden, wide_in, narrow_in, down, up, down_other, up_other,
                          wide_out, narrow_out, grads, levels, pre, wide, narrow, square_sems, sems,
                          held_down, held_up, weight_sems):
    del wide_in, narrow_in

    @pl.when(place[0] == 0)
    def _():
        tasks = middle.shape[0]
        copies = Copies(sems)
        loads = [copies.start(grad, grads.at[2]), copies.start(hidden, pre), copies.start(middle, levels.at[1])]
        weights = StageWeights(place[1], (down, up), (down_other, up_other), (held_down, held_up), weight_sems)
        weights.start([(1, 1), (0, 1), (1, 0)])
        loads += [copies.start(entry.at[turn], levels.at[0, task]) for task in range(tasks)]
        squares = Squares(wide, narrow, wide_out, narrow_out, square_sems)
        for load in loads:
            load.wait()
        for layer in (1, 0):
            backward_step(layer, levels, grads, pre, weights, held_down, held_up, squares, layer == 1)
        squares.wait()


def last_stage_kernel(turn, place, states, labels, label_rows, down, up, down_other, up_other,
                      grad_out, picked, wide_out, narrow_out,
                      levels, words, marks, chosen, pre, grads, wide, narrow, square_sems, sems,
                      held_down, held_up, weight_sems):
    @pl.when(place[0] == 1)
    def _():
        tasks, rows = states.shape[0], states.shape[1]
        copies = Copies(sems)
        loaded = copies.start(states, levels.at[0])
        weights = StageWeights(place[1], (down, up), (down_other, up_other), (held_down, held_up), weight_sems)
        weights.start([(0, 0), (1, 0), (0, 1), (1, 1)])
        later = [copies.start(label_rows, words), copies.start(labels.at[turn], marks)]
        loaded.wait()
        forward_loop(levels, pre, weights, held_down, held_up, lambda layer: None)
        for copy in later:
            copy.wait()

        joined = jnp.concatenate([levels[2, task] for task in range(tasks)], axis=0)
        grad, values = label_head(joined, marks[...], words[...])
        for task in range(tasks):
            part = slice(task * rows, (task + 1) * rows)
            grads[2, task] = grad[part]
            chosen[task] = jnp.broadcast_to(values[part], (rows, 128)).T[0:8]

        out_copy = copies.start(chosen, picked)
        squares = Squares(wide, narrow, wide_out, narrow_out, square_sems)

        @pl.loop(0, 2)
        def _(index):
            backward_step(1 - index, levels, grads, pre, None, held_down, held_up, squares, True)

        last = copies.start(grads.at[0], grad_out)
        squares.wait()
        out_copy.wait()
        last.wait()


def eval_kernel(step, offsets, place, states, before, *refs):
    *pieces, out, base, top, held, sems = refs
    copies = Copies(sems)
    rows = pieces[0].shape[1]

    @pl.when(place[2] == step)
    def _():
        loads = [[copies.start(states, base)], [], []]
        for kind in range(2):
            for index, piece in enumerate(pieces):
                block = block_at(place[3], offsets[index], len(pieces))
                spot = pl.ds(pl.multiple_of(block * rows, 16), rows)
                loads[1 + kind].append(copies.start(piece.at[kind], held.at[kind, spot]))
        for load in loads[0]:
            load.wait()
        wide = base[...].astype(f32)
        normed = (wide * row_scale(wide)).astype(bf16)
        for load in loads[1]:
            load.wait()
        active = gelu_value(nn_dot(normed, held[0])).astype(bf16)
        for load in loads[2]:
            load.wait()
        top[...] = (wide + nt_dot(active, held[1])).astype(bf16)
        copies.start(top, out).wait()

    @pl.when(place[2] != step)
    def _():
        copies.start(before, base).wait()
        copies.start(base, out).wait()


def fisher_kernel(turns, place, *refs):
    wides, narrows = refs[:turns], refs[turns:2 * turns]
    weights, outs = refs[2 * turns:2 * turns + 2], refs[2 * turns + 2:]
    del place
    for kind in range(2):
        top, total = None, None
        for task in range(weights[0].shape[0]):
            left = jnp.concatenate([ref[0, kind, task] for ref in wides], axis=0)
            right = jnp.concatenate([ref[0, kind, task] for ref in narrows], axis=0)
            term = tn_dot(left, right)
            scaled = term * weights[kind][task].astype(f32)
            top = scaled if top is None else top + scaled
            total = term if total is None else total + term
        outs[0][kind] = top.astype(bf16)
        outs[1][kind] = total.astype(bf16)


def block_size(width):
    return max(size for size in range(128, 513, 128) if width % size == 0)


smem = pl.BlockSpec(memory_space=pltpu.SMEM)
anywhere = pl.BlockSpec(memory_space=pl.ANY)
hbm = pl.BlockSpec(memory_space=pltpu.HBM)


def send(block, axis, route):
    return lax.ppermute(block, axis, route)


def walk(spot, count):
    if count % 2:
        return spot
    return jnp.where(spot < count // 2, 2 * spot, 2 * (count - 1 - spot) + 1)


def spot_of(device, count):
    if count % 2:
        return device
    return jnp.where(lax.rem(device, 2) == 0, lax.div(device, 2), count - 1 - lax.div(device, 2))


def block_at(spot, offset, count):
    return walk(lax.rem(spot + offset + 2 * count, count), count)


def ring_routes(axis):
    count = lax.axis_size(axis)
    order = list(range(count)) if count % 2 else list(range(0, count, 2)) + list(range(count - 1, 0, -2))
    ahead = [(order[i], order[(i + 1) % count]) for i in range(count)]
    return count, ahead, [(j, i) for i, j in ahead]


def ring_scatter(own, other, spot, axis):
    count, ahead, back = ring_routes(axis)
    rows = own[0].shape[1] // count

    def part(index, offset):
        start = block_at(spot, offset, count) * rows
        return sum(
            lax.dynamic_slice_in_dim(array[index], start, rows, 1).astype(f32) for array in (own, other)
        )

    moving = [part(0, -1).astype(bf16), part(1, 1).astype(bf16)]
    for step in range(count - 1):
        last = step == count - 2
        landed = [send(moving[0], axis, ahead), send(moving[1], axis, back)]
        sums = [landed[0].astype(f32) + part(0, -2 - step), landed[1].astype(f32) + part(1, 2 + step)]
        moving = sums if last else [value.astype(bf16) for value in sums]
    return moving


def ring_gather(own, axis):
    count, ahead, back = ring_routes(axis)
    pieces, offsets = [own], [0]
    down = up = own
    for step in range(1, count // 2 + 1):
        down = send(down, axis, ahead)
        pieces.append(down)
        offsets.append(-step)
        if len(pieces) < count:
            up = send(up, axis, back)
            pieces.append(up)
            offsets.append(step)
    return pieces, offsets


def after(value, done):
    return lax.optimization_barrier((value, done))[0]


def local(entry_states, down_proj, up_proj, label_rows, sampled_labels, eval_states):
    section_count = lax.axis_size("section")
    section = lax.axis_index("section")
    stage, member = section // 2, section % 2
    w_down, w_up = down_proj[0], up_proj[0]
    all_tasks, width, rank = w_down.shape
    tasks = all_tasks // 2
    micro, rows, _ = entry_states.shape
    label_count = label_rows.shape[0]
    spot = spot_of(lax.axis_index("dp"), lax.axis_size("dp"))
    place = jnp.stack([stage, member, section, spot]).astype(jnp.int32)
    sections = range(section_count)
    swap = [(i, i ^ 1) for i in sections]
    upward = [(i, i + 2) for i in sections if i + 2 < section_count]
    downward = [(i, i - 2) for i in sections if i - 2 >= 0]

    away = (1 - member) * tasks
    down_other = send(lax.dynamic_slice_in_dim(w_down, away, tasks, 0), "section", swap)
    up_other = send(lax.dynamic_slice_in_dim(w_up, away, tasks, 0), "section", swap)
    weights = (w_down, w_up, down_other, up_other)

    held = [
        pltpu.VMEM((2, tasks, width, rank), bf16),
        pltpu.VMEM((2, tasks, width, rank), bf16),
        pltpu.SemaphoreType.DMA((2, 2, tasks)),
    ]
    params = pltpu.CompilerParams(vmem_limit_bytes=vmem_bytes)
    state_shape, hidden_shape = (tasks, rows, width), (2, tasks, rows, rank)
    wide_shape, narrow_shape = (2, 2, tasks, rows, width), (2, 2, tasks, rows, rank)
    state_type = jax.ShapeDtypeStruct(state_shape, bf16)
    square_types = (jax.ShapeDtypeStruct(wide_shape, bf16), jax.ShapeDtypeStruct(narrow_shape, bf16))
    square_scratch = [
        pltpu.VMEM(wide_shape, bf16),
        pltpu.VMEM(narrow_shape, bf16),
        pltpu.SemaphoreType.DMA((2, 2, 2, tasks)),
    ]
    layer_flops = 4 * tasks * rows * width * rank
    weight_bytes = 8 * tasks * width * rank

    def stage_call(kernel, turn, name, operands, outputs, scratch, flops, held_out=(), **more):
        return pl.pallas_call(
            functools.partial(kernel, turn),
            out_shape=outputs,
            in_specs=[smem] + [hbm if index in held_out else anywhere for index in range(1, operands + 1)],
            out_specs=(anywhere,) * (len(outputs) - 2) + (hbm,) * 2,
            scratch_shapes=scratch + held,
            compiler_params=params,
            cost_estimate=pl.CostEstimate(flops=flops, bytes_accessed=weight_bytes, transcendentals=0),
            name=name,
            **more,
        )

    own_labels = lax.dynamic_slice_in_dim(sampled_labels, member * tasks, tasks, 0)
    label_columns = own_labels.transpose(1, 0, 2).reshape(micro, tasks * rows, 1)
    saved, crossing, returned, picked = {}, {}, {}, {}
    squares = {}
    token = place

    levels, pre = pltpu.VMEM((3,) + state_shape, bf16), pltpu.VMEM(hidden_shape, f32)

    def first_forward(turn):
        nonlocal token
        call = stage_call(
            first_forward_kernel, turn, "first_forward", 5,
            (state_type, state_type, jax.ShapeDtypeStruct(hidden_shape, f32)),
            [levels, pre, pltpu.SemaphoreType.DMA((3 * tasks,))],
            2 * layer_flops,
        )
        out, middle, hidden = call(token, entry_states, *weights)
        saved[turn] = (entry_states, middle, hidden)
        crossing[turn] = out
        token = after(place, hidden)

    def cross(turn):
        nonlocal token
        out = lax.optimization_barrier((crossing[turn], token))[0]
        crossing[turn] = send(out, "section", upward)

    def last_stage(turn):
        nonlocal token
        call = stage_call(
            last_stage_kernel, turn, "last_stage", 7,
            (state_type, jax.ShapeDtypeStruct((tasks, 8, rows), f32)) + square_types,
            [
                levels, pltpu.VMEM(label_rows.shape, bf16),
                pltpu.VMEM((tasks * rows, 1), jnp.int32), pltpu.VMEM((tasks, 8, rows), f32),
                pre, levels,
            ] + square_scratch + [pltpu.SemaphoreType.DMA((5,))],
            4 * layer_flops + 4 * tasks * rows * width * label_count,
        )
        grad, picked[turn], *squares[turn] = call(
            token, crossing[turn], label_columns, label_rows, *weights
        )
        returned[turn] = send(grad, "section", downward)
        token = after(place, picked[turn])

    def first_backward(turn):
        nonlocal token
        call = stage_call(
            first_backward_kernel, turn, "first_backward", 10, square_types,
            [levels, levels, pre] + square_scratch + [pltpu.SemaphoreType.DMA((3 + tasks,))],
            2 * layer_flops,
            held_out=(3, 4, 5, 6),
            input_output_aliases={5: 0, 6: 1},
        )
        squares[turn] = call(token, returned[turn], *saved[turn], *squares[turn], *weights)
        token = after(place, squares[turn][1])

    ahead, behind = min(3, micro), 2
    for turn in range(ahead):
        first_forward(turn)
        cross(turn)
    for turn in range(micro):
        if turn + ahead < micro:
            first_forward(turn + ahead)
        if turn >= behind:
            first_backward(turn - behind)
            if turn + 1 in crossing:
                token = after(token, crossing[turn + 1])
        last_stage(turn)
        if turn + ahead < micro:
            cross(turn + ahead)
    picked_all = jnp.stack([picked[turn][:, 0] for turn in range(micro)], axis=0)
    label_logprob = jnp.zeros((micro, rows), f32)
    for index in range(tasks):
        route = [(section_count - 2 + m, m * tasks + index) for m in range(2)]
        landed = send(picked_all[:, index], "section", route)
        label_logprob = jnp.where(section % tasks == index, landed, label_logprob)

    token = after(place, label_logprob)
    for turn in range(max(micro - behind, 0), micro):
        first_backward(turn)

    block = block_size(width)

    def fisher(away, order):
        turns = len(squares)

        def layer_of(s):
            return 1 - s[1] if away else s[1]

        call = pl.pallas_call(
            functools.partial(fisher_kernel, turns),
            out_shape=(jax.ShapeDtypeStruct((2, width, rank), bf16),) * 2,
            grid_spec=pltpu.PrefetchScalarGridSpec(
                num_scalar_prefetch=1,
                grid=(width // block,),
                in_specs=[pl.BlockSpec((1, 2, tasks, rows, block), lambda i, s: (layer_of(s), 0, 0, 0, i))] * turns
                + [pl.BlockSpec((1, 2, tasks, rows, rank), lambda i, s: (layer_of(s), 0, 0, 0, 0))] * turns
                + [pl.BlockSpec((tasks, block, rank), lambda i, s: (0 if away else s[1], i, 0))] * 2,
                out_specs=(pl.BlockSpec((2, block, rank), lambda i, s: (0, i, 0)),) * 2,
            ),
            compiler_params=params,
            cost_estimate=pl.CostEstimate(
                flops=4 * tasks * turns * rows * width * rank,
                bytes_accessed=turns * 8 * tasks * rows * width,
                transcendentals=0,
            ),
            name="fisher_away" if away else "fisher_own",
        )
        return call(
            order, *[squares[turn][0] for turn in range(turns)], *[squares[turn][1] for turn in range(turns)],
            *(weights[2:] if away else weights[:2]),
        )

    away_sums = fisher(True, token)
    other_sums = [send(value, "section", swap) for value in away_sums]
    sums = fisher(False, after(place, away_sums[0]))
    shares = ring_scatter(sums, other_sums, spot, "dp")
    numerator, denominator = shares
    merged_part = (numerator / (denominator + merge_eps)).astype(bf16)
    pieces, offsets = ring_gather(merged_part, "dp")
    fisher_log = jnp.log(denominator + merge_eps)

    current, result = eval_states, eval_states
    for step in range(section_count):
        result = pl.pallas_call(
            functools.partial(eval_kernel, step, offsets),
            out_shape=jax.ShapeDtypeStruct(eval_states.shape, bf16),
            in_specs=[smem] + [anywhere] * (2 + len(pieces)),
            out_specs=anywhere,
            scratch_shapes=[
                pltpu.VMEM(eval_states.shape, bf16), pltpu.VMEM(eval_states.shape, bf16),
                pltpu.VMEM((2, width, rank), bf16), pltpu.SemaphoreType.DMA((4 + 2 * len(pieces),)),
            ],
            compiler_params=pltpu.CompilerParams(vmem_limit_bytes=vmem_bytes // 3),
            cost_estimate=pl.CostEstimate(
                flops=4 * eval_states.size * rank, bytes_accessed=4 * width * rank, transcendentals=0
            ),
            name="eval_block",
        )(place, current, result, *pieces)
        if step + 1 < section_count:
            current = send(result, "section", [(step, step + 1)])
    return (result[None], label_logprob[None], fisher_log[None])


def solution(mesh):
    placed = (
        P(None, "dp", None),
        P("section", None, None, None),
        P("section", None, None, None),
        P(),
        P(None, None, "dp"),
        P("dp", None),
    )
    return jax.shard_map(
        local,
        mesh=mesh,
        in_specs=placed,
        out_specs=(
            P("section", "dp", None),
            P("section", None, "dp"),
            P("section", None, "dp", None),
        ),
        check_vma=False,
    )
```

```python
import functools

import jax
import jax.numpy as jnp
from jax import lax
from jax.experimental import pallas as pl
from jax.experimental.pallas import tpu as pltpu
from jax.sharding import PartitionSpec as P

norm_eps = 1e-06
merge_eps = 1e-06
soft_cap = 30.0
gelu_coef = 0.7978845608028654
vmem_bytes = 56 * 1024 * 1024
bf16 = jnp.bfloat16
f32 = jnp.float32


def nt_dot(lhs, rhs):
    return lax.dot_general(lhs, rhs, (((1,), (1,)), ((), ())), preferred_element_type=f32)


def nn_dot(lhs, rhs):
    return lax.dot_general(lhs, rhs, (((1,), (0,)), ((), ())), preferred_element_type=f32)


def tn_dot(lhs, rhs):
    return lax.dot_general(lhs, rhs, (((0,), (0,)), ((), ())), preferred_element_type=f32)


def gelu_value(hidden):
    inner = gelu_coef * (hidden + 0.044715 * hidden * hidden * hidden)
    return 0.5 * hidden * (1.0 + jnp.tanh(inner))


def gelu_slope(hidden):
    inner = gelu_coef * (hidden + 0.044715 * hidden * hidden * hidden)
    tanh_value = jnp.tanh(inner)
    return 0.5 * (1.0 + tanh_value) + 0.5 * hidden * (1.0 - tanh_value * tanh_value) * gelu_coef * (
        1.0 + 3.0 * 0.044715 * hidden * hidden
    )


def tiled(width):
    count = max(n for n in (1, 2, 3) if width % (128 * n) == 0)
    size = width // count

    def loop(body, start=None):
        def step(index, carry):
            return body(pl.ds(pl.multiple_of(index * size, 128), size), carry)

        return lax.fori_loop(0, count, step, start)

    return loop


def row_scale(total, width):
    return lax.rsqrt(total / width + norm_eps)


def row_sum(values):
    return jnp.sum(values, axis=-1, keepdims=True)


def square(values):
    wide = values.astype(f32)
    return (wide * wide).astype(bf16)


def zeros(*shape):
    return jnp.zeros(shape, f32)


def label_head(states, labels, label_rows, grads):
    tasks, rows, width = states.shape
    loop, words = tiled(width), label_rows.shape[0]

    def joined(cols):
        return jnp.concatenate([states[task, :, cols] for task in range(tasks)], axis=0)

    def score(cols, carry):
        total, logits = carry
        part = joined(cols)
        wide = part.astype(f32)
        return total + row_sum(wide * wide), logits + nt_dot(part, label_rows[:, cols])

    total, logits = loop(score, (zeros(tasks * rows, 1), zeros(tasks * rows, words)))
    scale = row_scale(total, width)
    bent = jnp.tanh(logits * scale / soft_cap)
    capped = soft_cap * bent
    logprob = capped - jnp.log(row_sum(jnp.exp(capped)))
    one_hot = (labels == lax.broadcasted_iota(jnp.int32, logprob.shape, 1)).astype(f32)
    slope = ((jnp.exp(logprob) - one_hot) * (1.0 - bent * bent)).astype(bf16)

    def product(cols, total):
        return total + row_sum(nn_dot(slope, label_rows[:, cols]) * joined(cols).astype(f32))

    mean = loop(product, zeros(tasks * rows, 1)) * scale / width

    def finish(cols, carry):
        wide = joined(cols).astype(f32)
        grad = (scale * (nn_dot(slope, label_rows[:, cols]) - wide * (scale * mean))).astype(bf16)
        for task in range(tasks):
            grads[task, :, cols] = grad[task * rows:(task + 1) * rows]
        return carry

    loop(finish, 0)
    return row_sum(logprob * one_hot)


class Copies:
    def __init__(self, sems):
        self.sems, self.used = sems, 0

    def start(self, source, target):
        copy = pltpu.make_async_copy(source, target, self.sems.at[self.used])
        self.used += 1
        copy.start()
        return copy


class StageWeights:
    def __init__(self, member, own, other, held, sems):
        self.member, self.own, self.other = member, own, other
        self.held, self.sems = held, sems
        self.tasks = held[0].shape[1]

    def copy(self, kind, layer, task):
        return pltpu.make_async_copy(
            self.other[kind].at[task], self.held[kind].at[layer, task], self.sems.at[kind, layer, task]
        )

    def start(self, order):
        for kind, layer in order:
            @pl.when(self.member == layer)
            def _():
                for task in range(self.tasks):
                    pltpu.make_async_copy(
                        self.own[kind].at[layer * self.tasks + task],
                        self.held[kind].at[layer, task],
                        self.sems.at[kind, layer, task],
                    ).start()

            @pl.when(self.member != layer)
            def _():
                for task in range(self.tasks):
                    self.copy(kind, layer, task).start()

    def wait(self, kind, layer, task):
        self.copy(kind, layer, task).wait()


def forward_loop(levels, hidden, scales, weights, held_down, held_up, done):
    tasks, (rows, width), rank = range(levels.shape[1]), levels.shape[2:], held_down.shape[-1]
    loop = tiled(width)

    @pl.loop(0, 2)
    def _(layer):
        for task in tasks:
            weights.wait(0, layer, task)

        def down(cols, carry):
            result = []
            for task in tasks:
                part = levels[layer, task, :, cols]
                wide = part.astype(f32)
                total, pre = carry[task]
                result.append((total + row_sum(wide * wide), pre + nn_dot(part, held_down[layer, task, cols])))
            return tuple(result)

        found = loop(down, tuple((zeros(rows, 1), zeros(rows, rank)) for _ in tasks))
        active = []
        for task in tasks:
            scale = row_scale(found[task][0], width)
            pre = found[task][1] * scale
            scales[layer, task] = jnp.broadcast_to(scale, (rows, 128))
            hidden[layer, task] = pre
            active.append(gelu_value(pre).astype(bf16))
        for task in tasks:
            weights.wait(1, layer, task)

        def up(cols, carry):
            update = [nt_dot(active[task], held_up[layer, task, cols]) for task in tasks]
            for task in tasks:
                levels[layer + 1, task, :, cols] = (
                    levels[layer, task, :, cols].astype(f32) + update[task]
                ).astype(bf16)
            return carry

        loop(up, 0)
        done(layer)


class Squares:
    def __init__(self, wide, narrow, wide_out, narrow_out, sems):
        self.pairs = ((wide, wide_out), (narrow, narrow_out))
        self.sems = sems

    def copy(self, width, layer, kind, task):
        source, target = self.pairs[width]
        return pltpu.make_async_copy(
            source.at[layer, kind, task], target.at[layer, kind, task], self.sems.at[width, layer, kind, task]
        )

    def set_wide(self, layer, kind, task, cols, value):
        self.pairs[0][0][layer, kind, task, :, cols] = value

    def set_narrow(self, layer, kind, task, value):
        self.pairs[1][0][layer, kind, task] = value

    def start(self, layer, kind, task):
        for width in range(2):
            self.copy(width, layer, kind, task).start()

    def wait(self):
        tasks = self.pairs[0][0].shape[2]

        @pl.loop(0, 2 * tasks)
        def _(index):
            for kind in range(2):
                for width in range(2):
                    self.copy(width, index // tasks, kind, index % tasks).wait()


def backward_step(layer, levels, grads, hidden, scales, weights, held_down, held_up, squares, pass_on):
    tasks, (rows, width), rank = range(levels.shape[1]), levels.shape[2:], held_down.shape[-1]
    loop = tiled(width)
    if weights is not None:
        for task in tasks:
            weights.wait(1, layer, task)
    scale = [scales[layer, task][:, :1] for task in tasks]

    def up(cols, carry):
        result = []
        for task in tasks:
            grad = grads[layer + 1, task, :, cols]
            result.append(carry[task] + nn_dot(grad, held_up[layer, task, cols]))
            norm = (levels[layer, task, :, cols].astype(f32) * scale[task]).astype(bf16)
            squares.set_wide(layer, 0, task, cols, square(norm))
            squares.set_wide(layer, 1, task, cols, square(grad))
        return tuple(result)

    grad_act = loop(up, tuple(zeros(rows, rank) for _ in tasks))
    grad_hidden = []
    for task in tasks:
        pre = hidden[layer, task]
        grad_hidden.append((grad_act[task] * gelu_slope(pre)).astype(bf16))
        squares.set_narrow(layer, 0, task, square(grad_hidden[task]))
        squares.set_narrow(layer, 1, task, square(gelu_value(pre).astype(bf16)))
    for task in tasks:
        for kind in range(2):
            squares.start(layer, kind, task)
    if not pass_on:
        return
    if weights is not None:
        for task in tasks:
            weights.wait(0, layer, task)

    def product(cols, carry):
        grad_norm = [nt_dot(grad_hidden[task], held_down[layer, task, cols]) for task in tasks]
        return tuple(
            carry[task] + row_sum(grad_norm[task] * levels[layer, task, :, cols].astype(f32)) for task in tasks
        )

    found = loop(product, tuple(zeros(rows, 1) for _ in tasks))
    pull = [scale[task] * scale[task] * found[task] / width for task in tasks]

    def finish(cols, carry):
        grad_norm = [nt_dot(grad_hidden[task], held_down[layer, task, cols]) for task in tasks]
        for task in tasks:
            wide = levels[layer, task, :, cols].astype(f32)
            grads[layer, task, :, cols] = (
                grads[layer + 1, task, :, cols].astype(f32) + scale[task] * (grad_norm[task] - wide * pull[task])
            ).astype(bf16)
        return carry

    loop(finish, 0)


def first_forward_kernel(turn, place, entry, down, up, down_other, up_other, out, middle, hidden, scales_out,
                         levels, pre, scales, sems, held_down, held_up, weight_sems):
    @pl.when(place[0] == 0)
    def _():
        tasks = out.shape[0]
        copies = Copies(sems)
        loads = [copies.start(entry.at[turn], levels.at[0, task]) for task in range(tasks)]
        weights = StageWeights(place[1], (down, up), (down_other, up_other), (held_down, held_up), weight_sems)
        weights.start([(0, 0), (1, 0), (0, 1), (1, 1)])
        for load in loads:
            load.wait()
        base = copies.used

        def leave(layer, task):
            return pltpu.make_async_copy(
                levels.at[layer + 1, task], (middle, out)[layer].at[task], sems.at[base + layer * tasks + task]
            )

        def done(layer):
            for fixed in range(2):
                @pl.when(layer == fixed)
                def _():
                    for task in range(tasks):
                        leave(fixed, task).start()

        forward_loop(levels, pre, scales, weights, held_down, held_up, done)
        last = [pltpu.make_async_copy(pre, hidden, sems.at[0]), pltpu.make_async_copy(scales, scales_out, sems.at[1])]
        for copy in last:
            copy.start()
        for layer in range(2):
            for task in range(tasks):
                leave(layer, task).wait()
        for copy in last:
            copy.wait()


def first_backward_kernel(turn, place, grad, entry, middle, hidden, scales_in, wide_in, narrow_in, down, up, down_other, up_other,
                          wide_out, narrow_out, grads, levels, pre, scales, wide, narrow, square_sems, sems,
                          held_down, held_up, weight_sems):
    del wide_in, narrow_in

    @pl.when(place[0] == 0)
    def _():
        tasks = middle.shape[0]
        copies = Copies(sems)
        loads = [copies.start(grad, grads.at[2]), copies.start(hidden, pre), copies.start(middle, levels.at[1])]
        loads.append(copies.start(scales_in, scales))
        weights = StageWeights(place[1], (down, up), (down_other, up_other), (held_down, held_up), weight_sems)
        weights.start([(1, 1), (0, 1), (1, 0)])
        loads += [copies.start(entry.at[turn], levels.at[0, task]) for task in range(tasks)]
        squares = Squares(wide, narrow, wide_out, narrow_out, square_sems)
        for load in loads:
            load.wait()
        for layer in (1, 0):
            backward_step(layer, levels, grads, pre, scales, weights, held_down, held_up, squares, layer == 1)
        squares.wait()


def last_stage_kernel(turn, place, states, labels, label_rows, down, up, down_other, up_other,
                      grad_out, picked, wide_out, narrow_out,
                      levels, words, marks, chosen, pre, scales, grads, wide, narrow, square_sems, sems,
                      held_down, held_up, weight_sems):
    @pl.when(place[0] == 1)
    def _():
        tasks, rows = states.shape[0], states.shape[1]
        copies = Copies(sems)
        loaded = copies.start(states, levels.at[0])
        weights = StageWeights(place[1], (down, up), (down_other, up_other), (held_down, held_up), weight_sems)
        weights.start([(0, 0), (1, 0), (0, 1), (1, 1)])
        later = [copies.start(label_rows, words), copies.start(labels.at[turn], marks)]
        loaded.wait()
        forward_loop(levels, pre, scales, weights, held_down, held_up, lambda layer: None)
        for copy in later:
            copy.wait()

        values = label_head(levels.at[2], marks[...], words, grads.at[2])
        for task in range(tasks):
            part = slice(task * rows, (task + 1) * rows)
            chosen[task] = jnp.broadcast_to(values[part], (rows, 128)).T[0:8]

        out_copy = copies.start(chosen, picked)
        squares = Squares(wide, narrow, wide_out, narrow_out, square_sems)

        @pl.loop(0, 2)
        def _(index):
            backward_step(1 - index, levels, grads, pre, scales, None, held_down, held_up, squares, True)

        last = copies.start(grads.at[0], grad_out)
        squares.wait()
        out_copy.wait()
        last.wait()


def eval_kernel(step, offsets, place, states, before, *refs):
    *pieces, out, base, top, held, sems = refs
    copies = Copies(sems)
    rows = pieces[0].shape[1]

    @pl.when(place[2] == step)
    def _():
        loads = [[copies.start(states, base)], [], []]
        for kind in range(2):
            for index, piece in enumerate(pieces):
                block = block_at(place[3], offsets[index], len(pieces))
                spot = pl.ds(pl.multiple_of(block * rows, 16), rows)
                loads[1 + kind].append(copies.start(piece.at[kind], held.at[kind, spot]))
        for load in loads[0]:
            load.wait()
        total_rows, width = base.shape
        loop = tiled(width)

        def squared(cols, total):
            wide = base[:, cols].astype(f32)
            return total + row_sum(wide * wide)

        scale = row_scale(loop(squared, zeros(total_rows, 1)), width)
        for load in loads[1]:
            load.wait()
        pre = loop(lambda cols, sums: sums + nn_dot(base[:, cols], held[0, cols]), zeros(total_rows, held.shape[-1]))
        active = gelu_value(pre * scale).astype(bf16)
        for load in loads[2]:
            load.wait()

        def up(cols, carry):
            top[:, cols] = (base[:, cols].astype(f32) + nt_dot(active, held[1, cols])).astype(bf16)
            return carry

        loop(up, 0)
        copies.start(top, out).wait()

    @pl.when(place[2] != step)
    def _():
        copies.start(before, base).wait()
        copies.start(base, out).wait()


def fisher_kernel(turns, place, *refs):
    wides, narrows = refs[:turns], refs[turns:2 * turns]
    weights, outs = refs[2 * turns:2 * turns + 2], refs[2 * turns + 2:]
    del place
    for kind in range(2):
        top, total = None, None
        for task in range(weights[0].shape[0]):
            left = jnp.concatenate([ref[0, kind, task] for ref in wides], axis=0)
            right = jnp.concatenate([ref[0, kind, task] for ref in narrows], axis=0)
            term = tn_dot(left, right)
            scaled = term * weights[kind][task].astype(f32)
            top = scaled if top is None else top + scaled
            total = term if total is None else total + term
        outs[0][kind] = top.astype(bf16)
        outs[1][kind] = total.astype(bf16)


def block_size(width):
    return max(size for size in range(128, 513, 128) if width % size == 0)


smem = pl.BlockSpec(memory_space=pltpu.SMEM)
anywhere = pl.BlockSpec(memory_space=pl.ANY)
hbm = pl.BlockSpec(memory_space=pltpu.HBM)


def send(block, axis, route):
    return lax.ppermute(block, axis, route)


def walk(spot, count):
    if count % 2:
        return spot
    return jnp.where(spot < count // 2, 2 * spot, 2 * (count - 1 - spot) + 1)


def spot_of(device, count):
    if count % 2:
        return device
    return jnp.where(lax.rem(device, 2) == 0, lax.div(device, 2), count - 1 - lax.div(device, 2))


def block_at(spot, offset, count):
    return walk(lax.rem(spot + offset + 2 * count, count), count)


def ring_routes(axis):
    count = lax.axis_size(axis)
    order = list(range(count)) if count % 2 else list(range(0, count, 2)) + list(range(count - 1, 0, -2))
    ahead = [(order[i], order[(i + 1) % count]) for i in range(count)]
    return count, ahead, [(j, i) for i, j in ahead]


def ring_scatter(own, other, spot, axis):
    count, ahead, back = ring_routes(axis)
    rows = own[0].shape[1] // count

    def part(index, offset):
        start = block_at(spot, offset, count) * rows
        return sum(
            lax.dynamic_slice_in_dim(array[index], start, rows, 1).astype(f32) for array in (own, other)
        )

    moving = [part(0, -1).astype(bf16), part(1, 1).astype(bf16)]
    for step in range(count - 1):
        last = step == count - 2
        landed = [send(moving[0], axis, ahead), send(moving[1], axis, back)]
        sums = [landed[0].astype(f32) + part(0, -2 - step), landed[1].astype(f32) + part(1, 2 + step)]
        moving = sums if last else [value.astype(bf16) for value in sums]
    return moving


def ring_gather(own, axis):
    count, ahead, back = ring_routes(axis)
    pieces, offsets = [own], [0]
    down = up = own
    for step in range(1, count // 2 + 1):
        down = send(down, axis, ahead)
        pieces.append(down)
        offsets.append(-step)
        if len(pieces) < count:
            up = send(up, axis, back)
            pieces.append(up)
            offsets.append(step)
    return pieces, offsets


def after(value, done):
    return lax.optimization_barrier((value, done))[0]


def local(entry_states, down_proj, up_proj, label_rows, sampled_labels, eval_states):
    section_count = lax.axis_size("section")
    section = lax.axis_index("section")
    stage, member = section // 2, section % 2
    w_down, w_up = down_proj[0], up_proj[0]
    all_tasks, width, rank = w_down.shape
    tasks = all_tasks // 2
    micro, rows, _ = entry_states.shape
    label_count = label_rows.shape[0]
    spot = spot_of(lax.axis_index("dp"), lax.axis_size("dp"))
    place = jnp.stack([stage, member, section, spot]).astype(jnp.int32)
    sections = range(section_count)
    swap = [(i, i ^ 1) for i in sections]
    upward = [(i, i + 2) for i in sections if i + 2 < section_count]
    downward = [(i, i - 2) for i in sections if i - 2 >= 0]

    away = (1 - member) * tasks
    down_other = send(lax.dynamic_slice_in_dim(w_down, away, tasks, 0), "section", swap)
    up_other = send(lax.dynamic_slice_in_dim(w_up, away, tasks, 0), "section", swap)
    weights = (w_down, w_up, down_other, up_other)

    held = [
        pltpu.VMEM((2, tasks, width, rank), bf16),
        pltpu.VMEM((2, tasks, width, rank), bf16),
        pltpu.SemaphoreType.DMA((2, 2, tasks)),
    ]
    params = pltpu.CompilerParams(vmem_limit_bytes=vmem_bytes)
    state_shape, hidden_shape = (tasks, rows, width), (2, tasks, rows, rank)
    wide_shape, narrow_shape = (2, 2, tasks, rows, width), (2, 2, tasks, rows, rank)
    state_type = jax.ShapeDtypeStruct(state_shape, bf16)
    square_types = (jax.ShapeDtypeStruct(wide_shape, bf16), jax.ShapeDtypeStruct(narrow_shape, bf16))
    square_scratch = [
        pltpu.VMEM(wide_shape, bf16),
        pltpu.VMEM(narrow_shape, bf16),
        pltpu.SemaphoreType.DMA((2, 2, 2, tasks)),
    ]
    layer_flops = 4 * tasks * rows * width * rank
    weight_bytes = 8 * tasks * width * rank

    def stage_call(kernel, turn, name, operands, outputs, scratch, flops, hbm_in=(), hbm_out=(), **more):
        return pl.pallas_call(
            functools.partial(kernel, turn),
            out_shape=outputs,
            in_specs=[smem] + [hbm if index in hbm_in else anywhere for index in range(1, operands + 1)],
            out_specs=tuple(hbm if index in hbm_out else anywhere for index in range(len(outputs))),
            scratch_shapes=scratch + held,
            compiler_params=params,
            cost_estimate=pl.CostEstimate(flops=flops, bytes_accessed=weight_bytes, transcendentals=0),
            name=name,
            **more,
        )

    own_labels = lax.dynamic_slice_in_dim(sampled_labels, member * tasks, tasks, 0)
    label_columns = own_labels.transpose(1, 0, 2).reshape(micro, tasks * rows, 1)
    saved, crossing, returned, picked = {}, {}, {}, {}
    squares = {}
    token = place

    levels, pre = pltpu.VMEM((3,) + state_shape, bf16), pltpu.VMEM(hidden_shape, f32)
    scale_shape = (2, tasks, rows, 128)
    scales, scale_type = pltpu.VMEM(scale_shape, f32), jax.ShapeDtypeStruct(scale_shape, f32)

    def first_forward(turn):
        nonlocal token
        call = stage_call(
            first_forward_kernel, turn, "first_forward", 5,
            (state_type, state_type, jax.ShapeDtypeStruct(hidden_shape, f32), scale_type),
            [levels, pre, scales, pltpu.SemaphoreType.DMA((3 * tasks,))],
            2 * layer_flops, hbm_in=(1, 2, 3, 4, 5), hbm_out=(1, 2, 3),
        )
        out, middle, hidden, scale = call(token, entry_states, *weights)
        saved[turn] = (entry_states, middle, hidden, scale)
        crossing[turn] = out
        token = after(place, scale)

    def cross(turn):
        nonlocal token
        out = lax.optimization_barrier((crossing[turn], token))[0]
        crossing[turn] = send(out, "section", upward)

    def last_stage(turn):
        nonlocal token
        call = stage_call(
            last_stage_kernel, turn, "last_stage", 7,
            (state_type, jax.ShapeDtypeStruct((tasks, 8, rows), f32)) + square_types,
            [
                levels, pltpu.VMEM(label_rows.shape, bf16),
                pltpu.VMEM((tasks * rows, 1), jnp.int32), pltpu.VMEM((tasks, 8, rows), f32),
                pre, scales, levels,
            ] + square_scratch + [pltpu.SemaphoreType.DMA((5,))],
            4 * layer_flops + 4 * tasks * rows * width * label_count,
            hbm_in=(3, 4, 5, 6, 7), hbm_out=(2, 3),
        )
        grad, picked[turn], *squares[turn] = call(
            token, crossing[turn], label_columns, label_rows, *weights
        )
        returned[turn] = send(grad, "section", downward)
        token = after(place, picked[turn])

    def first_backward(turn):
        nonlocal token
        call = stage_call(
            first_backward_kernel, turn, "first_backward", 11, square_types,
            [levels, levels, pre, scales] + square_scratch + [pltpu.SemaphoreType.DMA((4 + tasks,))],
            2 * layer_flops,
            hbm_in=range(2, 12), hbm_out=(0, 1),
            input_output_aliases={6: 0, 7: 1},
        )
        squares[turn] = call(token, returned[turn], *saved[turn], *squares[turn], *weights)
        token = after(place, squares[turn][1])

    ahead, behind = min(3, micro), 2
    for turn in range(ahead):
        first_forward(turn)
        cross(turn)
    for turn in range(micro):
        if turn + ahead < micro:
            first_forward(turn + ahead)
        if turn >= behind:
            first_backward(turn - behind)
            if turn + 1 in crossing:
                token = after(token, crossing[turn + 1])
        last_stage(turn)
        if turn + ahead < micro:
            cross(turn + ahead)
    for turn in range(max(micro - behind, 0), micro - 1):
        first_backward(turn)
    picked_all = jnp.stack([picked[turn][:, 0] for turn in range(micro)], axis=0)
    label_logprob = jnp.zeros((micro, rows), f32)
    for index in range(tasks):
        route = [(section_count - 2 + m, m * tasks + index) for m in range(2)]
        landed = send(picked_all[:, index], "section", route)
        label_logprob = jnp.where(section % tasks == index, landed, label_logprob)

    token = after(place, label_logprob)
    first_backward(micro - 1)

    block = block_size(width)

    def fisher(away, order):
        turns = len(squares)

        def layer_of(s):
            return 1 - s[1] if away else s[1]

        call = pl.pallas_call(
            functools.partial(fisher_kernel, turns),
            out_shape=(jax.ShapeDtypeStruct((2, width, rank), bf16),) * 2,
            grid_spec=pltpu.PrefetchScalarGridSpec(
                num_scalar_prefetch=1,
                grid=(width // block,),
                in_specs=[pl.BlockSpec((1, 2, tasks, rows, block), lambda i, s: (layer_of(s), 0, 0, 0, i))] * turns
                + [pl.BlockSpec((1, 2, tasks, rows, rank), lambda i, s: (layer_of(s), 0, 0, 0, 0))] * turns
                + [pl.BlockSpec((tasks, block, rank), lambda i, s: (0 if away else s[1], i, 0))] * 2,
                out_specs=(pl.BlockSpec((2, block, rank), lambda i, s: (0, i, 0)),) * 2,
            ),
            compiler_params=pltpu.CompilerParams(vmem_limit_bytes=vmem_bytes),
            cost_estimate=pl.CostEstimate(
                flops=4 * tasks * turns * rows * width * rank,
                bytes_accessed=turns * 8 * tasks * rows * width,
                transcendentals=0,
            ),
            name="fisher_away" if away else "fisher_own",
        )
        return call(
            order, *[squares[turn][0] for turn in range(turns)], *[squares[turn][1] for turn in range(turns)],
            *(weights[2:] if away else weights[:2]),
        )

    away_sums = fisher(True, token)
    other_sums = [send(value, "section", swap) for value in away_sums]
    sums = fisher(False, after(place, away_sums[0]))
    shares = ring_scatter(sums, other_sums, spot, "dp")
    numerator, denominator = shares
    merged_part = (numerator / (denominator + merge_eps)).astype(bf16)
    pieces, offsets = ring_gather(merged_part, "dp")
    fisher_log = jnp.log(denominator + merge_eps)

    current, result = eval_states, eval_states
    for step in range(section_count):
        result = pl.pallas_call(
            functools.partial(eval_kernel, step, offsets),
            out_shape=jax.ShapeDtypeStruct(eval_states.shape, bf16),
            in_specs=[smem] + [anywhere] * (2 + len(pieces)),
            out_specs=anywhere,
            scratch_shapes=[
                pltpu.VMEM(eval_states.shape, bf16), pltpu.VMEM(eval_states.shape, bf16),
                pltpu.VMEM((2, width, rank), bf16), pltpu.SemaphoreType.DMA((4 + 2 * len(pieces),)),
            ],
            compiler_params=pltpu.CompilerParams(vmem_limit_bytes=vmem_bytes // 4),
            cost_estimate=pl.CostEstimate(
                flops=4 * eval_states.size * rank, bytes_accessed=4 * width * rank, transcendentals=0
            ),
            name="eval_block",
        )(place, current, result, *pieces)
        if step + 1 < section_count:
            current = send(result, "section", [(step, step + 1)])
    return (result[None], label_logprob[None], fisher_log[None])


def solution(mesh):
    placed = (
        P(None, "dp", None),
        P("section", None, None, None),
        P("section", None, None, None),
        P(),
        P(None, None, "dp"),
        P("dp", None),
    )
    return jax.shard_map(
        local,
        mesh=mesh,
        in_specs=placed,
        out_specs=(
            P("section", "dp", None),
            P("section", None, "dp"),
            P("section", None, "dp", None),
        ),
        check_vma=False,
    )
```

```python
import functools

import jax
import jax.numpy as jnp
from jax import lax
from jax.experimental import pallas as pl
from jax.experimental.pallas import tpu as pltpu
from jax.sharding import PartitionSpec as P

norm_eps = 1e-06
merge_eps = 1e-06
soft_cap = 30.0
gelu_coef = 0.7978845608028654
vmem_bytes = 56 * 1024 * 1024
bf16 = jnp.bfloat16
f32 = jnp.float32


def nt_dot(lhs, rhs):
    return lax.dot_general(lhs, rhs, (((1,), (1,)), ((), ())), preferred_element_type=f32)


def nn_dot(lhs, rhs):
    return lax.dot_general(lhs, rhs, (((1,), (0,)), ((), ())), preferred_element_type=f32)


def tn_dot(lhs, rhs):
    return lax.dot_general(lhs, rhs, (((0,), (0,)), ((), ())), preferred_element_type=f32)


def gelu_value(hidden):
    inner = gelu_coef * (hidden + 0.044715 * hidden * hidden * hidden)
    return 0.5 * hidden * (1.0 + jnp.tanh(inner))


def gelu_slope(hidden):
    inner = gelu_coef * (hidden + 0.044715 * hidden * hidden * hidden)
    tanh_value = jnp.tanh(inner)
    return 0.5 * (1.0 + tanh_value) + 0.5 * hidden * (1.0 - tanh_value * tanh_value) * gelu_coef * (
        1.0 + 3.0 * 0.044715 * hidden * hidden
    )


def tiled(width):
    count = max(n for n in (1, 2, 3) if width % (128 * n) == 0)
    size = width // count

    def loop(body, start=None):
        def step(index, carry):
            return body(pl.ds(pl.multiple_of(index * size, 128), size), carry)

        return lax.fori_loop(0, count, step, start)

    return loop


def row_scale(total, width):
    return lax.rsqrt(total / width + norm_eps)


def row_sum(values):
    return jnp.sum(values, axis=-1, keepdims=True)


def square(values):
    wide = values.astype(f32)
    return (wide * wide).astype(bf16)


def zeros(*shape):
    return jnp.zeros(shape, f32)


def label_head(states, labels, label_rows, grads):
    rows, width = states.shape
    loop, words = tiled(width), label_rows.shape[0]

    def score(cols, carry):
        total, logits = carry
        part = states[:, cols]
        wide = part.astype(f32)
        return total + row_sum(wide * wide), logits + nt_dot(part, label_rows[:, cols])

    total, logits = loop(score, (zeros(rows, 1), zeros(rows, words)))
    scale = row_scale(total, width)
    logits = logits * scale
    bent = jnp.tanh(logits / soft_cap)
    capped = soft_cap * bent
    logprob = capped - jnp.log(row_sum(jnp.exp(capped)))
    one_hot = (labels == lax.broadcasted_iota(jnp.int32, logprob.shape, 1)).astype(f32)
    slope = ((jnp.exp(logprob) - one_hot) * (1.0 - bent * bent)).astype(bf16)
    pull = scale * row_sum(slope.astype(f32) * logits) / width

    def finish(cols, carry):
        wide = states[:, cols].astype(f32)
        grads[:, cols] = (scale * nn_dot(slope, label_rows[:, cols]) - scale * (wide * pull)).astype(bf16)
        return carry

    loop(finish, 0)
    return row_sum(logprob * one_hot)


class Copies:
    def __init__(self, sems):
        self.sems, self.used = sems, 0

    def start(self, source, target):
        copy = pltpu.make_async_copy(source, target, self.sems.at[self.used])
        self.used += 1
        copy.start()
        return copy


class StageWeights:
    def __init__(self, member, task, own, other, held, sems):
        self.member, self.task, self.own, self.other = member, task, own, other
        self.held, self.sems = held, sems

    def copy(self, kind, layer):
        return pltpu.make_async_copy(
            self.other[kind].at[self.task], self.held[kind].at[layer], self.sems.at[kind, layer]
        )

    def start(self, order):
        tasks = self.other[0].shape[0]
        for kind, layer in order:
            @pl.when(self.member == layer)
            def _():
                pltpu.make_async_copy(
                    self.own[kind].at[layer * tasks + self.task], self.held[kind].at[layer], self.sems.at[kind, layer]
                ).start()

            @pl.when(self.member != layer)
            def _():
                self.copy(kind, layer).start()

    def wait(self, kind, layer):
        self.copy(kind, layer).wait()


def forward_loop(levels, hidden, scales, weights, held_down, held_up, done):
    (rows, width), rank = levels.shape[1:], held_down.shape[-1]
    loop = tiled(width)

    @pl.loop(0, 2)
    def _(layer):
        weights.wait(0, layer)

        def down(cols, carry):
            total, pre = carry
            part = levels[layer, :, cols]
            wide = part.astype(f32)
            return total + row_sum(wide * wide), pre + nn_dot(part, held_down[layer, cols])

        total, pre = loop(down, (zeros(rows, 1), zeros(rows, rank)))
        scale = row_scale(total, width)
        pre = pre * scale
        scales[layer] = jnp.broadcast_to(scale, (rows, 128))
        hidden[layer] = pre
        active = gelu_value(pre).astype(bf16)
        weights.wait(1, layer)

        def up(cols, carry):
            update = nt_dot(active, held_up[layer, cols])
            levels[layer + 1, :, cols] = (levels[layer, :, cols].astype(f32) + update).astype(bf16)
            return carry

        loop(up, 0)
        done(layer)


class Squares:
    def __init__(self, wide, narrow, wide_out, narrow_out, sems):
        self.wide, self.narrow = wide, narrow
        self.pairs = ((wide, wide_out), (narrow, narrow_out))
        self.sems = sems

    def copy(self, which, layer, kind):
        source, target = self.pairs[which]
        return pltpu.make_async_copy(
            source.at[layer, kind], target.at[layer, kind], self.sems.at[which, layer, kind]
        )

    def start(self, layer):
        for kind in range(2):
            for which in range(2):
                self.copy(which, layer, kind).start()

    def wait(self):
        for layer in range(2):
            for kind in range(2):
                for which in range(2):
                    self.copy(which, layer, kind).wait()


def backward_step(layer, levels, grads, hidden, scales, weights, held_down, held_up, squares, pass_on):
    (rows, width), rank = levels.shape[1:], held_down.shape[-1]
    loop = tiled(width)
    if weights is not None:
        weights.wait(1, layer)
    scale = scales[layer][:, :1]
    pre = hidden[layer]

    def up(cols, total):
        grad = grads[layer + 1, :, cols]
        total = total + nn_dot(grad, held_up[layer, cols])
        norm = (levels[layer, :, cols].astype(f32) * scale).astype(bf16)
        squares.wide[layer, 0, :, cols] = square(norm)
        squares.wide[layer, 1, :, cols] = square(grad)
        return total

    grad_hidden = (loop(up, zeros(rows, rank)) * gelu_slope(pre)).astype(bf16)
    squares.narrow[layer, 0] = square(grad_hidden)
    squares.narrow[layer, 1] = square(gelu_value(pre).astype(bf16))
    squares.start(layer)
    if not pass_on:
        return
    if weights is not None:
        weights.wait(0, layer)
    pull = scale * row_sum(grad_hidden.astype(f32) * pre) / width

    def finish(cols, carry):
        grad_norm = nt_dot(grad_hidden, held_down[layer, cols])
        wide = levels[layer, :, cols].astype(f32)
        grads[layer, :, cols] = (
            grads[layer + 1, :, cols].astype(f32) + scale * (grad_norm - wide * pull)
        ).astype(bf16)
        return carry

    loop(finish, 0)


def first_forward_kernel(task, half, place, entry, down, up, down_other, up_other, out, middle, hidden, scales_out,
                         levels, pre, scales, sems, held_down, held_up, weight_sems):
    @pl.when(place[0] == 0)
    def _():
        rows = levels.shape[1]
        copies = Copies(sems)
        load = copies.start(entry.at[pl.ds(half * rows, rows)], levels.at[0])
        weights = StageWeights(
            place[1], task, (down, up), (down_other, up_other), (held_down, held_up), weight_sems
        )
        weights.start([(0, 0), (1, 0), (0, 1), (1, 1)])
        load.wait()

        def leave(layer):
            return pltpu.make_async_copy(levels.at[layer + 1], (middle, out)[layer], sems.at[1 + layer])

        def done(layer):
            for fixed in range(2):
                @pl.when(layer == fixed)
                def _():
                    leave(fixed).start()

        forward_loop(levels, pre, scales, weights, held_down, held_up, done)
        last = [
            pltpu.make_async_copy(pre, hidden, sems.at[0]),
            pltpu.make_async_copy(scales, scales_out, sems.at[3]),
        ]
        for copy in last:
            copy.start()
        for copy in [leave(0), leave(1)] + last:
            copy.wait()


def first_backward_kernel(task, half, place, grad, entry, middle, hidden, scales_in, wide_in, narrow_in,
                          down, up, down_other, up_other, wide_out, narrow_out,
                          grads, levels, pre, scales, wide, narrow, square_sems, sems,
                          held_down, held_up, weight_sems):
    del wide_in, narrow_in

    @pl.when(place[0] == 0)
    def _():
        rows = levels.shape[1]
        copies = Copies(sems)
        loads = [
            copies.start(source, target)
            for source, target in (
                (grad, grads.at[2]), (hidden, pre), (scales_in, scales), (middle, levels.at[1]),
                (entry.at[pl.ds(half * rows, rows)], levels.at[0]),
            )
        ]
        weights = StageWeights(
            place[1], task, (down, up), (down_other, up_other), (held_down, held_up), weight_sems
        )
        weights.start([(1, 1), (0, 1), (1, 0)])
        squares = Squares(wide, narrow, wide_out, narrow_out, square_sems)
        for load in loads:
            load.wait()
        for layer in (1, 0):
            backward_step(layer, levels, grads, pre, scales, weights, held_down, held_up, squares, layer == 1)
        squares.wait()


def last_stage_kernel(task, half, place, states, labels, label_rows, down, up, down_other, up_other,
                      grad_out, picked, wide_out, narrow_out,
                      levels, words, marks, chosen, pre, scales, grads, wide, narrow, square_sems, sems,
                      held_down, held_up, weight_sems):
    @pl.when(place[0] == 1)
    def _():
        rows = levels.shape[1]
        copies = Copies(sems)
        loaded = copies.start(states, levels.at[0])
        weights = StageWeights(
            place[1], task, (down, up), (down_other, up_other), (held_down, held_up), weight_sems
        )
        weights.start([(0, 0), (1, 0), (0, 1), (1, 1)])
        later = [copies.start(label_rows, words), copies.start(labels.at[task, half], marks)]
        loaded.wait()
        forward_loop(levels, pre, scales, weights, held_down, held_up, lambda layer: None)
        for copy in later:
            copy.wait()
        values = label_head(levels.at[2], marks[...], words, grads.at[2])
        lanes = 128 * ((rows + 127) // 128)
        spread = jnp.broadcast_to(values, (rows, 128))
        if lanes > rows:
            spread = jnp.concatenate([spread, zeros(lanes - rows, 128)], axis=0)
        chosen[...] = spread.T[0:8]
        out_copy = copies.start(chosen, picked)
        squares = Squares(wide, narrow, wide_out, narrow_out, square_sems)

        @pl.loop(0, 2)
        def _(index):
            backward_step(1 - index, levels, grads, pre, scales, None, held_down, held_up, squares, True)

        last = copies.start(grads.at[0], grad_out)
        squares.wait()
        out_copy.wait()
        last.wait()


def eval_kernel(step, offsets, place, states, before, *refs):
    *pieces, out, base, top, held, sems = refs
    copies = Copies(sems)
    rows = pieces[0].shape[1]

    @pl.when(place[2] == step)
    def _():
        loads = [[copies.start(states, base)], [], []]
        for kind in range(2):
            for index, piece in enumerate(pieces):
                block = block_at(place[3], offsets[index], len(pieces))
                spot = pl.ds(pl.multiple_of(block * rows, 16), rows)
                loads[1 + kind].append(copies.start(piece.at[kind], held.at[kind, spot]))
        for load in loads[0]:
            load.wait()
        total_rows, width = base.shape
        loop = tiled(width)

        def squared(cols, total):
            wide = base[:, cols].astype(f32)
            return total + row_sum(wide * wide)

        scale = row_scale(loop(squared, zeros(total_rows, 1)), width)
        for load in loads[1]:
            load.wait()
        pre = loop(lambda cols, sums: sums + nn_dot(base[:, cols], held[0, cols]), zeros(total_rows, held.shape[-1]))
        active = gelu_value(pre * scale).astype(bf16)
        for load in loads[2]:
            load.wait()

        def up(cols, carry):
            top[:, cols] = (base[:, cols].astype(f32) + nt_dot(active, held[1, cols])).astype(bf16)
            return carry

        loop(up, 0)
        copies.start(top, out).wait()

    @pl.when(place[2] != step)
    def _():
        copies.start(before, base).wait()
        copies.start(base, out).wait()


def fisher_kernel(halves, first, place, *refs):
    del place
    wides, narrows, weights = refs[:halves], refs[halves:2 * halves], refs[2 * halves:2 * halves + 2]
    before, outs = ((), refs[2 * halves + 2:]) if first else (refs[2 * halves + 2:-2], refs[-2:])
    for kind in range(2):
        left = jnp.concatenate([ref[0, kind] for ref in wides], axis=0)
        right = jnp.concatenate([ref[0, kind] for ref in narrows], axis=0)
        term = tn_dot(left, right)
        values = (term * weights[kind][0].astype(f32), term)
        for index, out in enumerate(outs):
            value = values[index] if first else values[index] + before[index][kind]
            out[kind] = value.astype(out.dtype)


def block_size(width):
    return max(size for size in range(128, 513, 128) if width % size == 0)


smem = pl.BlockSpec(memory_space=pltpu.SMEM)
anywhere = pl.BlockSpec(memory_space=pl.ANY)
hbm = pl.BlockSpec(memory_space=pltpu.HBM)


def send(block, axis, route):
    return lax.ppermute(block, axis, route)


def walk(spot, count):
    if count % 2:
        return spot
    return jnp.where(spot < count // 2, 2 * spot, 2 * (count - 1 - spot) + 1)


def spot_of(device, count):
    if count % 2:
        return device
    return jnp.where(lax.rem(device, 2) == 0, lax.div(device, 2), count - 1 - lax.div(device, 2))


def block_at(spot, offset, count):
    return walk(lax.rem(spot + offset + 2 * count, count), count)


def ring_routes(axis):
    count = lax.axis_size(axis)
    order = list(range(count)) if count % 2 else list(range(0, count, 2)) + list(range(count - 1, 0, -2))
    ahead = [(order[i], order[(i + 1) % count]) for i in range(count)]
    return count, ahead, [(j, i) for i, j in ahead]


def ring_scatter(own, other, spot, axis):
    count, ahead, back = ring_routes(axis)
    rows = own[0].shape[1] // count

    def part(index, offset):
        start = block_at(spot, offset, count) * rows
        return sum(
            lax.dynamic_slice_in_dim(array[index], start, rows, 1).astype(f32) for array in (own, other)
        )

    moving = [part(0, -1).astype(bf16), part(1, 1).astype(bf16)]
    for step in range(count - 1):
        last = step == count - 2
        landed = [send(moving[0], axis, ahead), send(moving[1], axis, back)]
        sums = [landed[0].astype(f32) + part(0, -2 - step), landed[1].astype(f32) + part(1, 2 + step)]
        moving = sums if last else [value.astype(bf16) for value in sums]
    return moving


def ring_gather(own, axis):
    count, ahead, back = ring_routes(axis)
    pieces, offsets = [own], [0]
    down = up = own
    for step in range(1, count // 2 + 1):
        down = send(down, axis, ahead)
        pieces.append(down)
        offsets.append(-step)
        if len(pieces) < count:
            up = send(up, axis, back)
            pieces.append(up)
            offsets.append(step)
    return pieces, offsets


def after(value, done):
    return lax.optimization_barrier((value, done))[0]


def local(entry_states, down_proj, up_proj, label_rows, sampled_labels, eval_states):
    section_count = lax.axis_size("section")
    section = lax.axis_index("section")
    stage, member = section // 2, section % 2
    w_down, w_up = down_proj[0], up_proj[0]
    all_tasks, width, rank = w_down.shape
    tasks = all_tasks // 2
    micro, rows, _ = entry_states.shape
    label_count = label_rows.shape[0]
    halves = 2
    chunks, part = tasks * halves, micro * rows // halves
    spot = spot_of(lax.axis_index("dp"), lax.axis_size("dp"))
    place = jnp.stack([stage, member, section, spot]).astype(jnp.int32)
    sections = range(section_count)
    swap = [(i, i ^ 1) for i in sections]
    upward = [(i, i + 2) for i in sections if i + 2 < section_count]
    downward = [(i, i - 2) for i in sections if i - 2 >= 0]

    away = (1 - member) * tasks
    down_other = send(lax.dynamic_slice_in_dim(w_down, away, tasks, 0), "section", swap)
    up_other = send(lax.dynamic_slice_in_dim(w_up, away, tasks, 0), "section", swap)
    weights = (w_down, w_up, down_other, up_other)

    held = [
        pltpu.VMEM((2, width, rank), bf16),
        pltpu.VMEM((2, width, rank), bf16),
        pltpu.SemaphoreType.DMA((2, 2)),
    ]
    params = pltpu.CompilerParams(vmem_limit_bytes=vmem_bytes)
    state_shape, hidden_shape = (part, width), (2, part, rank)
    wide_shape, narrow_shape = (2, 2, part, width), (2, 2, part, rank)
    state_type = jax.ShapeDtypeStruct(state_shape, bf16)
    square_types = (jax.ShapeDtypeStruct(wide_shape, bf16), jax.ShapeDtypeStruct(narrow_shape, bf16))
    square_scratch = [
        pltpu.VMEM(wide_shape, bf16),
        pltpu.VMEM(narrow_shape, bf16),
        pltpu.SemaphoreType.DMA((2, 2, 2)),
    ]
    layer_flops = 4 * part * width * rank
    weight_bytes = 8 * width * rank

    def stage_call(kernel, turn, name, operands, outputs, scratch, flops, hbm_in=(), hbm_out=(), **more):
        return pl.pallas_call(
            functools.partial(kernel, turn // halves, turn % halves),
            out_shape=outputs,
            in_specs=[smem] + [hbm if index in hbm_in else anywhere for index in range(1, operands + 1)],
            out_specs=tuple(hbm if index in hbm_out else anywhere for index in range(len(outputs))),
            scratch_shapes=scratch + held,
            compiler_params=params,
            cost_estimate=pl.CostEstimate(flops=flops, bytes_accessed=weight_bytes, transcendentals=0),
            name=name,
            **more,
        )

    own_labels = lax.dynamic_slice_in_dim(sampled_labels, member * tasks, tasks, 0)
    label_columns = own_labels.reshape(tasks, halves, part, 1)
    entry = entry_states.reshape(micro * rows, width)
    saved, crossing, returned, picked = {}, {}, {}, {}
    squares = {}
    token = place

    levels, pre = pltpu.VMEM((3,) + state_shape, bf16), pltpu.VMEM(hidden_shape, f32)
    scale_shape = (2, part, 128)
    lanes = 128 * ((part + 127) // 128)
    scales, scale_type = pltpu.VMEM(scale_shape, f32), jax.ShapeDtypeStruct(scale_shape, f32)

    def first_forward(turn):
        nonlocal token
        call = stage_call(
            first_forward_kernel, turn, "first_forward", 5,
            (state_type, state_type, jax.ShapeDtypeStruct(hidden_shape, f32), scale_type),
            [levels, pre, scales, pltpu.SemaphoreType.DMA((4,))],
            2 * layer_flops, hbm_in=(1, 2, 3, 4, 5), hbm_out=(1, 2, 3),
        )
        out, middle, hidden, scale = call(token, entry, *weights)
        saved[turn] = (entry, middle, hidden, scale)
        crossing[turn] = out
        token = after(place, scale)

    def cross(turn):
        nonlocal token
        out = lax.optimization_barrier((crossing[turn], token))[0]
        crossing[turn] = send(out, "section", upward)

    def last_stage(turn):
        nonlocal token
        call = stage_call(
            last_stage_kernel, turn, "last_stage", 7,
            (state_type, jax.ShapeDtypeStruct((8, lanes), f32)) + square_types,
            [
                levels, pltpu.VMEM(label_rows.shape, bf16),
                pltpu.VMEM((part, 1), jnp.int32), pltpu.VMEM((8, lanes), f32),
                pre, scales, levels,
            ] + square_scratch + [pltpu.SemaphoreType.DMA((5,))],
            4 * layer_flops + 4 * part * width * label_count,
            hbm_in=(3, 4, 5, 6, 7), hbm_out=(2, 3),
        )
        grad, picked[turn], *squares[turn] = call(
            token, crossing[turn], label_columns, label_rows, *weights
        )
        returned[turn] = send(grad, "section", downward)
        token = after(place, picked[turn])

    def first_backward(turn):
        nonlocal token
        call = stage_call(
            first_backward_kernel, turn, "first_backward", 11, square_types,
            [levels, levels, pre, scales] + square_scratch + [pltpu.SemaphoreType.DMA((5,))],
            2 * layer_flops,
            hbm_in=range(2, 12), hbm_out=(0, 1),
            input_output_aliases={6: 0, 7: 1},
        )
        squares[turn] = call(token, returned[turn], *saved[turn], *squares[turn], *weights)
        token = after(place, squares[turn][1])

    block = block_size(width)

    def fisher(task, away, sums=()):
        first = not sums

        def layer_of(s):
            return 1 - s[1] if away else s[1]

        pairs = [squares[task * halves + half] for half in range(halves)]
        sum_spec = pl.BlockSpec((2, block, rank), lambda i, s: (0, i, 0))
        call = pl.pallas_call(
            functools.partial(fisher_kernel, halves, first),
            out_shape=(jax.ShapeDtypeStruct((2, width, rank), bf16 if task == tasks - 1 else f32),) * 2,
            grid_spec=pltpu.PrefetchScalarGridSpec(
                num_scalar_prefetch=1,
                grid=(width // block,),
                in_specs=[pl.BlockSpec((1, 2, part, block), lambda i, s: (layer_of(s), 0, 0, i))] * halves
                + [pl.BlockSpec((1, 2, part, rank), lambda i, s: (layer_of(s), 0, 0, 0))] * halves
                + [pl.BlockSpec((1, block, rank), lambda i, s: (task if away else s[1] * tasks + task, i, 0))] * 2
                + [sum_spec] * len(sums),
                out_specs=(sum_spec,) * 2,
            ),
            compiler_params=params,
            cost_estimate=pl.CostEstimate(
                flops=4 * halves * part * width * rank,
                bytes_accessed=8 * halves * part * width,
                transcendentals=0,
            ),
            name="fisher_away" if away else "fisher_own",
        )
        return call(
            token, *[wide for wide, _ in pairs], *[narrow for _, narrow in pairs],
            *(weights[2:] if away else weights[:2]), *sums,
        )

    sums = {True: (), False: ()}

    def add_task(task):
        nonlocal token
        for away in (True, False):
            sums[away] = fisher(task, away, sums[away])
            token = after(place, sums[away][0])

    for turn in range(chunks):
        first_forward(turn)
        cross(turn)
    for turn in range(chunks):
        if turn >= 2:
            first_backward(turn - 2)
        last_stage(turn)
    first_backward(chunks - 2)
    for task in range(tasks - 1):
        add_task(task)
    values = jnp.stack([picked[turn][0, :part] for turn in range(chunks)]).reshape(tasks, micro, rows)
    values = after(values, token)
    label_logprob = jnp.zeros((micro, rows), f32)
    for index in range(tasks):
        route = [(section_count - 2 + m, m * tasks + index) for m in range(2)]
        landed = send(values[index], "section", route)
        label_logprob = jnp.where(section % tasks == index, landed, label_logprob)
    token = after(token, label_logprob)
    first_backward(chunks - 1)
    away_sums = fisher(tasks - 1, True, sums[True])
    other_sums = [send(value, "section", swap) for value in away_sums]
    token = after(place, away_sums[0])
    sums = fisher(tasks - 1, False, sums[False])
    shares = ring_scatter(sums, other_sums, spot, "dp")
    numerator, denominator = shares
    merged_part = (numerator / (denominator + merge_eps)).astype(bf16)
    pieces, offsets = ring_gather(merged_part, "dp")
    fisher_log = jnp.log(denominator + merge_eps)

    current, result = eval_states, eval_states
    for step in range(section_count):
        result = pl.pallas_call(
            functools.partial(eval_kernel, step, offsets),
            out_shape=jax.ShapeDtypeStruct(eval_states.shape, bf16),
            in_specs=[smem] + [anywhere] * (2 + len(pieces)),
            out_specs=anywhere,
            scratch_shapes=[
                pltpu.VMEM(eval_states.shape, bf16), pltpu.VMEM(eval_states.shape, bf16),
                pltpu.VMEM((2, width, rank), bf16), pltpu.SemaphoreType.DMA((4 + 2 * len(pieces),)),
            ],
            compiler_params=pltpu.CompilerParams(vmem_limit_bytes=vmem_bytes // 4),
            cost_estimate=pl.CostEstimate(
                flops=4 * eval_states.size * rank, bytes_accessed=4 * width * rank, transcendentals=0
            ),
            name="eval_block",
        )(place, current, result, *pieces)
        if step + 1 < section_count:
            current = send(result, "section", [(step, step + 1)])
    return (result[None], label_logprob[None], fisher_log[None])


def solution(mesh):
    placed = (
        P(None, "dp", None),
        P("section", None, None, None),
        P("section", None, None, None),
        P(),
        P(None, None, "dp"),
        P("dp", None),
    )
    return jax.shard_map(
        local,
        mesh=mesh,
        in_specs=placed,
        out_specs=(
            P("section", "dp", None),
            P("section", None, "dp"),
            P("section", None, "dp", None),
        ),
        check_vma=False,
    )
```

```python
import functools

import jax
import jax.numpy as jnp
from jax import lax
from jax.experimental import pallas as pl
from jax.experimental.pallas import tpu as pltpu
from jax.sharding import PartitionSpec as P

norm_eps = 1e-06
merge_eps = 1e-06
soft_cap = 30.0
gelu_coef = 0.7978845608028654
vmem_bytes = 56 * 1024 * 1024
bf16 = jnp.bfloat16
f32 = jnp.float32


def nt_dot(lhs, rhs):
    return lax.dot_general(lhs, rhs, (((1,), (1,)), ((), ())), preferred_element_type=f32)


def nn_dot(lhs, rhs):
    return lax.dot_general(lhs, rhs, (((1,), (0,)), ((), ())), preferred_element_type=f32)


def tn_dot(lhs, rhs):
    return lax.dot_general(lhs, rhs, (((0,), (0,)), ((), ())), preferred_element_type=f32)


def gelu_value(hidden):
    inner = gelu_coef * (hidden + 0.044715 * hidden * hidden * hidden)
    return 0.5 * hidden * (1.0 + jnp.tanh(inner))


def gelu_slope(hidden):
    inner = gelu_coef * (hidden + 0.044715 * hidden * hidden * hidden)
    tanh_value = jnp.tanh(inner)
    return 0.5 * (1.0 + tanh_value) + 0.5 * hidden * (1.0 - tanh_value * tanh_value) * gelu_coef * (
        1.0 + 3.0 * 0.044715 * hidden * hidden
    )


def tiled(width):
    count = max(n for n in (1, 2, 3) if width % (128 * n) == 0)
    size = width // count

    def loop(body, start=None):
        def step(index, carry):
            return body(pl.ds(pl.multiple_of(index * size, 128), size), carry)

        return lax.fori_loop(0, count, step, start)

    return loop


def row_scale(total, width):
    return lax.rsqrt(total / width + norm_eps)


def row_sum(values):
    return jnp.sum(values, axis=-1, keepdims=True)


def square(values):
    wide = values.astype(f32)
    return (wide * wide).astype(bf16)


def zeros(*shape):
    return jnp.zeros(shape, f32)


def label_head(states, labels, label_rows, grads):
    rows, width = states.shape
    loop, words = tiled(width), label_rows.shape[0]

    def score(cols, carry):
        total, logits = carry
        part = states[:, cols]
        wide = part.astype(f32)
        return total + row_sum(wide * wide), logits + nt_dot(part, label_rows[:, cols])

    total, logits = loop(score, (zeros(rows, 1), zeros(rows, words)))
    scale = row_scale(total, width)
    logits = logits * scale
    bent = jnp.tanh(logits / soft_cap)
    capped = soft_cap * bent
    logprob = capped - jnp.log(row_sum(jnp.exp(capped)))
    one_hot = (labels == lax.broadcasted_iota(jnp.int32, logprob.shape, 1)).astype(f32)
    slope = ((jnp.exp(logprob) - one_hot) * (1.0 - bent * bent)).astype(bf16)
    pull = scale * row_sum(slope.astype(f32) * logits) / width

    def finish(cols, carry):
        wide = states[:, cols].astype(f32)
        grads[:, cols] = (scale * nn_dot(slope, label_rows[:, cols]) - scale * (wide * pull)).astype(bf16)
        return carry

    loop(finish, 0)
    return row_sum(logprob * one_hot)


class Copies:
    def __init__(self, sems):
        self.sems, self.used = sems, 0

    def start(self, source, target):
        copy = pltpu.make_async_copy(source, target, self.sems.at[self.used])
        self.used += 1
        copy.start()
        return copy


class StageWeights:
    def __init__(self, member, task, own, other, held, sems):
        self.member, self.task, self.own, self.other = member, task, own, other
        self.held, self.sems = held, sems

    def copy(self, kind, layer):
        return pltpu.make_async_copy(self.other[kind], self.held[kind].at[layer], self.sems.at[kind, layer])

    def start(self, order):
        tasks = self.own[0].shape[0] // 2
        for kind, layer in order:
            @pl.when(self.member == layer)
            def _():
                pltpu.make_async_copy(
                    self.own[kind].at[layer * tasks + self.task], self.held[kind].at[layer], self.sems.at[kind, layer]
                ).start()

            @pl.when(self.member != layer)
            def _():
                self.copy(kind, layer).start()

    def wait(self, kind, layer):
        self.copy(kind, layer).wait()


def forward_loop(levels, hidden, scales, weights, held_down, held_up, done):
    (rows, width), rank = levels.shape[1:], held_down.shape[-1]
    loop = tiled(width)

    @pl.loop(0, 2)
    def _(layer):
        weights.wait(0, layer)

        def down(cols, carry):
            total, pre = carry
            part = levels[layer, :, cols]
            wide = part.astype(f32)
            return total + row_sum(wide * wide), pre + nn_dot(part, held_down[layer, cols])

        total, pre = loop(down, (zeros(rows, 1), zeros(rows, rank)))
        scale = row_scale(total, width)
        pre = pre * scale
        scales[layer] = jnp.broadcast_to(scale, (rows, 128))
        hidden[layer] = pre
        active = gelu_value(pre).astype(bf16)
        weights.wait(1, layer)

        def up(cols, carry):
            update = nt_dot(active, held_up[layer, cols])
            levels[layer + 1, :, cols] = (levels[layer, :, cols].astype(f32) + update).astype(bf16)
            return carry

        loop(up, 0)
        done(layer)


class Squares:
    def __init__(self, wide, narrow, wide_out, narrow_out, sems):
        self.wide, self.narrow = wide, narrow
        self.pairs = ((wide, wide_out), (narrow, narrow_out))
        self.sems = sems

    def copy(self, which, layer, kind):
        source, target = self.pairs[which]
        return pltpu.make_async_copy(
            source.at[layer, kind], target.at[layer, kind], self.sems.at[which, layer, kind]
        )

    def start(self, layer):
        for kind in range(2):
            for which in range(2):
                self.copy(which, layer, kind).start()

    def wait(self):
        for layer in range(2):
            for kind in range(2):
                for which in range(2):
                    self.copy(which, layer, kind).wait()


def backward_step(layer, levels, grads, hidden, scales, weights, held_down, held_up, squares, pass_on):
    (rows, width), rank = levels.shape[1:], held_down.shape[-1]
    loop = tiled(width)
    if weights is not None:
        weights.wait(1, layer)
    scale = scales[layer][:, :1]
    pre = hidden[layer]

    def up(cols, total):
        grad = grads[layer + 1, :, cols]
        total = total + nn_dot(grad, held_up[layer, cols])
        norm = (levels[layer, :, cols].astype(f32) * scale).astype(bf16)
        squares.wide[layer, 0, :, cols] = square(norm)
        squares.wide[layer, 1, :, cols] = square(grad)
        return total

    grad_hidden = (loop(up, zeros(rows, rank)) * gelu_slope(pre)).astype(bf16)
    squares.narrow[layer, 0] = square(grad_hidden)
    squares.narrow[layer, 1] = square(gelu_value(pre).astype(bf16))
    squares.start(layer)
    if not pass_on:
        return
    if weights is not None:
        weights.wait(0, layer)
    pull = scale * row_sum(grad_hidden.astype(f32) * pre) / width

    def finish(cols, carry):
        grad_norm = nt_dot(grad_hidden, held_down[layer, cols])
        wide = levels[layer, :, cols].astype(f32)
        grads[layer, :, cols] = (
            grads[layer + 1, :, cols].astype(f32) + scale * (grad_norm - wide * pull)
        ).astype(bf16)
        return carry

    loop(finish, 0)


def first_forward_kernel(task, half, place, entry, down, up, down_other, up_other, out, middle, hidden, scales_out,
                         levels, pre, scales, sems, held_down, held_up, weight_sems):
    @pl.when(place[0] == 0)
    def _():
        rows = levels.shape[1]
        copies = Copies(sems)
        load = copies.start(entry.at[pl.ds(half * rows, rows)], levels.at[0])
        weights = StageWeights(
            place[1], task, (down, up), (down_other, up_other), (held_down, held_up), weight_sems
        )
        weights.start([(0, 0), (1, 0), (0, 1), (1, 1)])
        load.wait()

        def leave(layer):
            return pltpu.make_async_copy(levels.at[layer + 1], (middle, out)[layer], sems.at[1 + layer])

        def done(layer):
            for fixed in range(2):
                @pl.when(layer == fixed)
                def _():
                    leave(fixed).start()

        forward_loop(levels, pre, scales, weights, held_down, held_up, done)
        last = [
            pltpu.make_async_copy(pre, hidden, sems.at[0]),
            pltpu.make_async_copy(scales, scales_out, sems.at[3]),
        ]
        for copy in last:
            copy.start()
        for copy in [leave(0), leave(1)] + last:
            copy.wait()


def first_backward_kernel(task, half, place, grad, entry, middle, hidden, scales_in, wide_in, narrow_in,
                          down, up, down_other, up_other, wide_out, narrow_out,
                          grads, levels, pre, scales, wide, narrow, square_sems, sems,
                          held_down, held_up, weight_sems):
    del wide_in, narrow_in

    @pl.when(place[0] == 0)
    def _():
        rows = levels.shape[1]
        copies = Copies(sems)
        loads = [
            copies.start(source, target)
            for source, target in (
                (grad, grads.at[2]), (hidden, pre), (scales_in, scales), (middle, levels.at[1]),
                (entry.at[pl.ds(half * rows, rows)], levels.at[0]),
            )
        ]
        weights = StageWeights(
            place[1], task, (down, up), (down_other, up_other), (held_down, held_up), weight_sems
        )
        weights.start([(1, 1), (0, 1), (1, 0)])
        squares = Squares(wide, narrow, wide_out, narrow_out, square_sems)
        for load in loads:
            load.wait()
        for layer in (1, 0):
            backward_step(layer, levels, grads, pre, scales, weights, held_down, held_up, squares, layer == 1)
        squares.wait()


def last_stage_kernel(task, half, place, states, labels, label_rows, down, up, down_other, up_other,
                      grad_out, picked, wide_out, narrow_out,
                      levels, words, marks, chosen, pre, scales, grads, wide, narrow, square_sems, sems,
                      held_down, held_up, weight_sems):
    @pl.when(place[0] == 1)
    def _():
        rows = levels.shape[1]
        copies = Copies(sems)
        loaded = copies.start(states, levels.at[0])
        weights = StageWeights(
            place[1], task, (down, up), (down_other, up_other), (held_down, held_up), weight_sems
        )
        weights.start([(0, 0), (1, 0), (0, 1), (1, 1)])
        later = [copies.start(label_rows, words), copies.start(labels.at[task, half], marks)]
        loaded.wait()
        forward_loop(levels, pre, scales, weights, held_down, held_up, lambda layer: None)
        for copy in later:
            copy.wait()
        values = label_head(levels.at[2], marks[...], words, grads.at[2])
        lanes = 128 * ((rows + 127) // 128)
        spread = jnp.broadcast_to(values, (rows, 128))
        if lanes > rows:
            spread = jnp.concatenate([spread, zeros(lanes - rows, 128)], axis=0)
        chosen[...] = spread.T[0:8]
        out_copy = copies.start(chosen, picked)
        squares = Squares(wide, narrow, wide_out, narrow_out, square_sems)

        @pl.loop(0, 2)
        def _(index):
            backward_step(1 - index, levels, grads, pre, scales, None, held_down, held_up, squares, True)

        last = copies.start(grads.at[0], grad_out)
        squares.wait()
        out_copy.wait()
        last.wait()


def eval_kernel(step, offsets, place, states, before, *refs):
    *pieces, out, base, top, held, sems = refs
    copies = Copies(sems)
    rows = pieces[0].shape[1]

    @pl.when(place[2] == step)
    def _():
        loads = [[copies.start(states, base)], [], []]
        for kind in range(2):
            for index, piece in enumerate(pieces):
                block = block_at(place[3], offsets[index], len(pieces))
                spot = pl.ds(pl.multiple_of(block * rows, 16), rows)
                loads[1 + kind].append(copies.start(piece.at[kind], held.at[kind, spot]))
        for load in loads[0]:
            load.wait()
        width = base.shape[1]
        wide = base[...].astype(f32)
        scale = row_scale(row_sum(wide * wide), width)
        for load in loads[1]:
            load.wait()
        active = gelu_value(nn_dot(base[...], held[0]) * scale).astype(bf16)
        for load in loads[2]:
            load.wait()
        top[...] = (base[...].astype(f32) + nt_dot(active, held[1])).astype(bf16)
        copies.start(top, out).wait()

    @pl.when(place[2] != step)
    def _():
        copies.start(before, base).wait()
        copies.start(base, out).wait()


def fisher_kernel(tasks, halves, place, *refs):
    del place
    count = tasks * halves
    wides, narrows = refs[:count], refs[count:2 * count]
    weights, outs = refs[2 * count:-2], refs[-2:]
    for kind in range(2):
        top, total = None, None
        for task in range(tasks):
            span = slice(task * halves, (task + 1) * halves)
            left = jnp.concatenate([ref[0, kind] for ref in wides[span]], axis=0)
            right = jnp.concatenate([ref[0, kind] for ref in narrows[span]], axis=0)
            term = tn_dot(left, right)
            scaled = term * weights[task * 2 + kind][...].astype(f32)
            top = scaled if top is None else top + scaled
            total = term if total is None else total + term
        outs[0][kind] = top.astype(bf16)
        outs[1][kind] = total.astype(bf16)


def block_size(width):
    return max(size for size in range(128, 1153, 128) if width % size == 0)


smem = pl.BlockSpec(memory_space=pltpu.SMEM)
anywhere = pl.BlockSpec(memory_space=pl.ANY)
hbm = pl.BlockSpec(memory_space=pltpu.HBM)


def send(block, axis, route):
    return lax.ppermute(block, axis, route)


def walk(spot, count):
    if count % 2:
        return spot
    return jnp.where(spot < count // 2, 2 * spot, 2 * (count - 1 - spot) + 1)


def spot_of(device, count):
    if count % 2:
        return device
    return jnp.where(lax.rem(device, 2) == 0, lax.div(device, 2), count - 1 - lax.div(device, 2))


def block_at(spot, offset, count):
    return walk(lax.rem(spot + offset + 2 * count, count), count)


def ring_routes(axis):
    count = lax.axis_size(axis)
    order = list(range(count)) if count % 2 else list(range(0, count, 2)) + list(range(count - 1, 0, -2))
    ahead = [(order[i], order[(i + 1) % count]) for i in range(count)]
    return count, ahead, [(j, i) for i, j in ahead]


def ring_scatter(own, other, spot, axis):
    count, ahead, back = ring_routes(axis)
    rows = own[0].shape[1] // count
    streams = [(index, kind) for kind in range(own[0].shape[0]) for index in range(2)]

    def part(index, kind, step):
        offset = -1 - step if index == 0 else 1 + step
        start = block_at(spot, offset, count) * rows
        return sum(
            lax.dynamic_slice_in_dim(array[index][kind], start, rows, 0).astype(f32) for array in (own, other)
        )

    moving = {stream: part(*stream, 0).astype(bf16) for stream in streams}
    for step in range(1, count):
        for stream in streams:
            landed = send(moving[stream], axis, back if stream[0] else ahead)
            total = landed.astype(f32) + part(*stream, step)
            moving[stream] = total if step == count - 1 else total.astype(bf16)
    return [jnp.stack([moving[index, kind] for kind in range(own[0].shape[0])]) for index in range(2)]


def ring_gather(own, axis):
    count, ahead, back = ring_routes(axis)
    pieces, offsets = [own], [0]
    down = up = own
    for step in range(1, count // 2 + 1):
        down = send(down, axis, ahead)
        pieces.append(down)
        offsets.append(-step)
        if len(pieces) < count:
            up = send(up, axis, back)
            pieces.append(up)
            offsets.append(step)
    return pieces, offsets


def after(value, done):
    return lax.optimization_barrier((value, done))[0]


def local(entry_states, down_proj, up_proj, label_rows, sampled_labels, eval_states):
    section_count = lax.axis_size("section")
    section = lax.axis_index("section")
    stage, member = section // 2, section % 2
    w_down, w_up = down_proj[0], up_proj[0]
    all_tasks, width, rank = w_down.shape
    tasks = all_tasks // 2
    micro, rows, _ = entry_states.shape
    label_count = label_rows.shape[0]
    halves = 2
    chunks, part = tasks * halves, micro * rows // halves
    spot = spot_of(lax.axis_index("dp"), lax.axis_size("dp"))
    place = jnp.stack([stage, member, section, spot]).astype(jnp.int32)
    sections = range(section_count)
    swap = [(i, i ^ 1) for i in sections]
    upward = [(i, i + 2) for i in sections if i + 2 < section_count]
    downward = [(i, i - 2) for i in sections if i - 2 >= 0]

    away = (1 - member) * tasks
    others = [
        [send(lax.dynamic_index_in_dim(array, away + task, 0, keepdims=False), "section", swap) for array in (w_down, w_up)]
        for task in range(tasks)
    ]

    def weights(turn):
        return (w_down, w_up, *others[turn // halves])

    held = [
        pltpu.VMEM((2, width, rank), bf16),
        pltpu.VMEM((2, width, rank), bf16),
        pltpu.SemaphoreType.DMA((2, 2)),
    ]
    params = pltpu.CompilerParams(vmem_limit_bytes=vmem_bytes)
    state_shape, hidden_shape = (part, width), (2, part, rank)
    wide_shape, narrow_shape = (2, 2, part, width), (2, 2, part, rank)
    state_type = jax.ShapeDtypeStruct(state_shape, bf16)
    square_types = (jax.ShapeDtypeStruct(wide_shape, bf16), jax.ShapeDtypeStruct(narrow_shape, bf16))
    square_scratch = [
        pltpu.VMEM(wide_shape, bf16),
        pltpu.VMEM(narrow_shape, bf16),
        pltpu.SemaphoreType.DMA((2, 2, 2)),
    ]
    layer_flops = 4 * part * width * rank
    weight_bytes = 8 * width * rank

    def stage_call(kernel, turn, name, operands, outputs, scratch, flops, hbm_in=(), hbm_out=(), **more):
        return pl.pallas_call(
            functools.partial(kernel, turn // halves, turn % halves),
            out_shape=outputs,
            in_specs=[smem] + [hbm if index in hbm_in else anywhere for index in range(1, operands + 1)],
            out_specs=tuple(hbm if index in hbm_out else anywhere for index in range(len(outputs))),
            scratch_shapes=scratch + held,
            compiler_params=params,
            cost_estimate=pl.CostEstimate(flops=flops, bytes_accessed=weight_bytes, transcendentals=0),
            name=name,
            **more,
        )

    own_labels = lax.dynamic_slice_in_dim(sampled_labels, member * tasks, tasks, 0)
    label_columns = own_labels.reshape(tasks, halves, part, 1)
    entry = entry_states.reshape(micro * rows, width)
    saved, crossing, returned, picked = {}, {}, {}, {}
    squares = {}
    token = place

    levels, pre = pltpu.VMEM((3,) + state_shape, bf16), pltpu.VMEM(hidden_shape, f32)
    scale_shape = (2, part, 128)
    lanes = 128 * ((part + 127) // 128)
    scales, scale_type = pltpu.VMEM(scale_shape, f32), jax.ShapeDtypeStruct(scale_shape, f32)

    def first_forward(turn):
        nonlocal token
        call = stage_call(
            first_forward_kernel, turn, "first_forward", 5,
            (state_type, state_type, jax.ShapeDtypeStruct(hidden_shape, f32), scale_type),
            [levels, pre, scales, pltpu.SemaphoreType.DMA((4,))],
            2 * layer_flops, hbm_in=(1, 2, 3, 4, 5), hbm_out=(1, 2, 3),
        )
        out, middle, hidden, scale = call(token, entry, *weights(turn))
        saved[turn] = (entry, middle, hidden, scale)
        crossing[turn] = out
        token = after(place, scale)

    def cross(turn):
        nonlocal token
        out = lax.optimization_barrier((crossing[turn], token))[0]
        crossing[turn] = send(out, "section", upward)

    def last_stage(turn):
        nonlocal token
        call = stage_call(
            last_stage_kernel, turn, "last_stage", 7,
            (state_type, jax.ShapeDtypeStruct((8, lanes), f32)) + square_types,
            [
                levels, pltpu.VMEM(label_rows.shape, bf16),
                pltpu.VMEM((part, 1), jnp.int32), pltpu.VMEM((8, lanes), f32),
                pre, scales, levels,
            ] + square_scratch + [pltpu.SemaphoreType.DMA((5,))],
            4 * layer_flops + 4 * part * width * label_count,
            hbm_in=(3, 4, 5, 6, 7), hbm_out=(2, 3),
        )
        grad, picked[turn], *squares[turn] = call(
            token, crossing[turn], label_columns, label_rows, *weights(turn)
        )
        returned[turn] = send(grad, "section", downward)
        token = after(place, picked[turn])

    def first_backward(turn):
        nonlocal token
        call = stage_call(
            first_backward_kernel, turn, "first_backward", 11, square_types,
            [levels, levels, pre, scales] + square_scratch + [pltpu.SemaphoreType.DMA((5,))],
            2 * layer_flops,
            hbm_in=range(2, 12), hbm_out=(0, 1),
            input_output_aliases={6: 0, 7: 1},
        )
        squares[turn] = call(token, returned[turn], *saved[turn], *squares[turn], *weights(turn))
        token = after(place, squares[turn][1])

    block = block_size(width)

    def fisher(away):
        def layer_of(s):
            return 1 - s[1] if away else s[1]

        def own_spec(task):
            return pl.BlockSpec((pl.squeezed, block, rank), lambda i, s: (s[1] * tasks + task, i, 0))

        pairs = [squares[turn] for turn in range(chunks)]
        sum_spec = pl.BlockSpec((2, block, rank), lambda i, s: (0, i, 0))
        other_spec = pl.BlockSpec((block, rank), lambda i, s: (i, 0))
        call = pl.pallas_call(
            functools.partial(fisher_kernel, tasks, halves),
            out_shape=(jax.ShapeDtypeStruct((2, width, rank), bf16),) * 2,
            grid_spec=pltpu.PrefetchScalarGridSpec(
                num_scalar_prefetch=1,
                grid=(width // block,),
                in_specs=[pl.BlockSpec((1, 2, part, block), lambda i, s: (layer_of(s), 0, 0, i))] * chunks
                + [pl.BlockSpec((1, 2, part, rank), lambda i, s: (layer_of(s), 0, 0, 0))] * chunks
                + [other_spec if away else own_spec(task) for task in range(tasks) for _ in range(2)],
                out_specs=(sum_spec,) * 2,
            ),
            compiler_params=params,
            cost_estimate=pl.CostEstimate(
                flops=4 * chunks * part * width * rank,
                bytes_accessed=8 * chunks * part * width,
                transcendentals=0,
            ),
            name="fisher_away" if away else "fisher_own",
        )
        matrices = sum(others, []) if away else [w_down, w_up] * tasks
        return call(token, *[wide for wide, _ in pairs], *[narrow for _, narrow in pairs], *matrices)

    for turn in range(chunks):
        first_forward(turn)
        cross(turn)
    for turn in range(chunks):
        if turn >= 2:
            first_backward(turn - 2)
        last_stage(turn)
    first_backward(chunks - 2)
    values = jnp.stack([picked[turn][0, :part] for turn in range(chunks)]).reshape(tasks, micro, rows)
    values = after(values, token)
    label_logprob = jnp.zeros((micro, rows), f32)
    for index in range(tasks):
        route = [(section_count - 2 + m, m * tasks + index) for m in range(2)]
        landed = send(values[index], "section", route)
        label_logprob = jnp.where(section % tasks == index, landed, label_logprob)
    token = after(token, label_logprob)
    first_backward(chunks - 1)
    away_sums = fisher(True)
    other_sums = lax.optimization_barrier([send(value, "section", swap) for value in away_sums])
    token = after(place, away_sums[0])
    sums = fisher(False)
    shares = ring_scatter(sums, other_sums, spot, "dp")
    numerator, denominator = shares
    merged_part = (numerator / (denominator + merge_eps)).astype(bf16)
    pieces, offsets = ring_gather(merged_part, "dp")
    fisher_log = jnp.log(denominator + merge_eps)

    current, result = eval_states, eval_states
    for step in range(section_count):
        result = pl.pallas_call(
            functools.partial(eval_kernel, step, offsets),
            out_shape=jax.ShapeDtypeStruct(eval_states.shape, bf16),
            in_specs=[smem] + [anywhere] * (2 + len(pieces)),
            out_specs=anywhere,
            scratch_shapes=[
                pltpu.VMEM(eval_states.shape, bf16), pltpu.VMEM(eval_states.shape, bf16),
                pltpu.VMEM((2, width, rank), bf16), pltpu.SemaphoreType.DMA((4 + 2 * len(pieces),)),
            ],
            compiler_params=pltpu.CompilerParams(vmem_limit_bytes=vmem_bytes // 4),
            cost_estimate=pl.CostEstimate(
                flops=4 * eval_states.size * rank, bytes_accessed=4 * width * rank, transcendentals=0
            ),
            name="eval_block",
        )(place, current, result, *pieces)
        if step + 1 < section_count:
            current = send(result, "section", [(step, step + 1)])
    return (result[None], label_logprob[None], fisher_log[None])


def solution(mesh):
    placed = (
        P(None, "dp", None),
        P("section", None, None, None),
        P("section", None, None, None),
        P(),
        P(None, None, "dp"),
        P("dp", None),
    )
    return jax.shard_map(
        local,
        mesh=mesh,
        in_specs=placed,
        out_specs=(
            P("section", "dp", None),
            P("section", None, "dp"),
            P("section", None, "dp", None),
        ),
        check_vma=False,
    )
```

```python
import functools

import jax
import jax.numpy as jnp
from jax import lax
from jax.experimental import pallas as pl
from jax.experimental.pallas import tpu as pltpu
from jax.sharding import PartitionSpec as P

norm_eps = 1e-06
merge_eps = 1e-06
soft_cap = 30.0
gelu_coef = 0.7978845608028654
vmem_bytes = 56 * 1024 * 1024
bf16 = jnp.bfloat16
f32 = jnp.float32


def nt_dot(lhs, rhs):
    return lax.dot_general(lhs, rhs, (((1,), (1,)), ((), ())), preferred_element_type=f32)


def nn_dot(lhs, rhs):
    return lax.dot_general(lhs, rhs, (((1,), (0,)), ((), ())), preferred_element_type=f32)


def tn_dot(lhs, rhs):
    return lax.dot_general(lhs, rhs, (((0,), (0,)), ((), ())), preferred_element_type=f32)


def gelu_value(hidden):
    inner = gelu_coef * (hidden + 0.044715 * hidden * hidden * hidden)
    return 0.5 * hidden * (1.0 + jnp.tanh(inner))


def gelu_slope(hidden):
    inner = gelu_coef * (hidden + 0.044715 * hidden * hidden * hidden)
    tanh_value = jnp.tanh(inner)
    return 0.5 * (1.0 + tanh_value) + 0.5 * hidden * (1.0 - tanh_value * tanh_value) * gelu_coef * (
        1.0 + 3.0 * 0.044715 * hidden * hidden
    )


def tiled(width):
    count = max(n for n in (1, 2, 3) if width % (128 * n) == 0)
    size = width // count

    def loop(body, start=None):
        def step(index, carry):
            return body(pl.ds(pl.multiple_of(index * size, 128), size), carry)

        return lax.fori_loop(0, count, step, start)

    return loop


def row_scale(total, width):
    return lax.rsqrt(total / width + norm_eps)


def row_sum(values):
    return jnp.sum(values, axis=-1, keepdims=True)


def square(values):
    wide = values.astype(f32)
    return (wide * wide).astype(bf16)


def zeros(*shape):
    return jnp.zeros(shape, f32)


def label_head(states, labels, label_rows, grads):
    rows, width = states.shape
    loop, words = tiled(width), label_rows.shape[0]

    def score(cols, carry):
        total, logits = carry
        part = states[:, cols]
        wide = part.astype(f32)
        return total + row_sum(wide * wide), logits + nt_dot(part, label_rows[:, cols])

    total, logits = loop(score, (zeros(rows, 1), zeros(rows, words)))
    scale = row_scale(total, width)
    logits = logits * scale
    bent = jnp.tanh(logits / soft_cap)
    capped = soft_cap * bent
    logprob = capped - jnp.log(row_sum(jnp.exp(capped)))
    one_hot = (labels == lax.broadcasted_iota(jnp.int32, logprob.shape, 1)).astype(f32)
    slope = ((jnp.exp(logprob) - one_hot) * (1.0 - bent * bent)).astype(bf16)
    pull = scale * row_sum(slope.astype(f32) * logits) / width

    def finish(cols, carry):
        wide = states[:, cols].astype(f32)
        grads[:, cols] = (scale * nn_dot(slope, label_rows[:, cols]) - scale * (wide * pull)).astype(bf16)
        return carry

    loop(finish, 0)
    return row_sum(logprob * one_hot)


class Copies:
    def __init__(self, sems):
        self.sems, self.used = sems, 0

    def start(self, source, target):
        copy = pltpu.make_async_copy(source, target, self.sems.at[self.used])
        self.used += 1
        copy.start()
        return copy


class StageWeights:
    def __init__(self, member, task, own, other, held, sems):
        self.member, self.task, self.own, self.other = member, task, own, other
        self.held, self.sems = held, sems

    def copy(self, kind, layer):
        return pltpu.make_async_copy(self.other[kind], self.held[kind].at[layer], self.sems.at[kind, layer])

    def start(self, order):
        tasks = self.own[0].shape[0] // 2
        for kind, layer in order:
            @pl.when(self.member == layer)
            def _():
                pltpu.make_async_copy(
                    self.own[kind].at[layer * tasks + self.task], self.held[kind].at[layer], self.sems.at[kind, layer]
                ).start()

            @pl.when(self.member != layer)
            def _():
                self.copy(kind, layer).start()

    def wait(self, kind, layer):
        self.copy(kind, layer).wait()


def forward_loop(levels, hidden, scales, weights, held_down, held_up, done):
    (rows, width), rank = levels.shape[1:], held_down.shape[-1]
    loop = tiled(width)

    @pl.loop(0, 2)
    def _(layer):
        weights.wait(0, layer)

        def down(cols, carry):
            total, pre = carry
            part = levels[layer, :, cols]
            wide = part.astype(f32)
            return total + row_sum(wide * wide), pre + nn_dot(part, held_down[layer, cols])

        total, pre = loop(down, (zeros(rows, 1), zeros(rows, rank)))
        scale = row_scale(total, width)
        pre = pre * scale
        scales[layer] = jnp.broadcast_to(scale, (rows, 128))
        hidden[layer] = pre
        active = gelu_value(pre).astype(bf16)
        weights.wait(1, layer)

        def up(cols, carry):
            update = nt_dot(active, held_up[layer, cols])
            levels[layer + 1, :, cols] = (levels[layer, :, cols].astype(f32) + update).astype(bf16)
            return carry

        loop(up, 0)
        done(layer)


class Squares:
    def __init__(self, wide, narrow, wide_out, narrow_out, sems):
        self.wide, self.narrow = wide, narrow
        self.pairs = ((wide, wide_out), (narrow, narrow_out))
        self.sems = sems

    def copy(self, which, layer, kind):
        source, target = self.pairs[which]
        return pltpu.make_async_copy(
            source.at[layer, kind], target.at[layer, kind], self.sems.at[which, layer, kind]
        )

    def start(self, layer):
        for kind in range(2):
            for which in range(2):
                self.copy(which, layer, kind).start()

    def wait(self):
        for layer in range(2):
            for kind in range(2):
                for which in range(2):
                    self.copy(which, layer, kind).wait()


def backward_step(layer, levels, grads, hidden, scales, weights, held_down, held_up, squares, pass_on):
    (rows, width), rank = levels.shape[1:], held_down.shape[-1]
    loop = tiled(width)
    if weights is not None:
        weights.wait(1, layer)
    scale = scales[layer][:, :1]
    pre = hidden[layer]

    def up(cols, total):
        grad = grads[layer + 1, :, cols]
        total = total + nn_dot(grad, held_up[layer, cols])
        norm = (levels[layer, :, cols].astype(f32) * scale).astype(bf16)
        squares.wide[layer, 0, :, cols] = square(norm)
        squares.wide[layer, 1, :, cols] = square(grad)
        return total

    grad_hidden = (loop(up, zeros(rows, rank)) * gelu_slope(pre)).astype(bf16)
    squares.narrow[layer, 0] = square(grad_hidden)
    squares.narrow[layer, 1] = square(gelu_value(pre).astype(bf16))
    squares.start(layer)
    if not pass_on:
        return
    if weights is not None:
        weights.wait(0, layer)
    pull = scale * row_sum(grad_hidden.astype(f32) * pre) / width

    def finish(cols, carry):
        grad_norm = nt_dot(grad_hidden, held_down[layer, cols])
        wide = levels[layer, :, cols].astype(f32)
        grads[layer, :, cols] = (
            grads[layer + 1, :, cols].astype(f32) + scale * (grad_norm - wide * pull)
        ).astype(bf16)
        return carry

    loop(finish, 0)


def first_forward_kernel(task, start, place, entry, down, up, down_other, up_other, out, middle, hidden, scales_out,
                         levels, pre, scales, sems, held_down, held_up, weight_sems):
    @pl.when(place[0] == 0)
    def _():
        rows = levels.shape[1]
        copies = Copies(sems)
        load = copies.start(entry.at[pl.ds(start, rows)], levels.at[0])
        weights = StageWeights(
            place[1], task, (down, up), (down_other, up_other), (held_down, held_up), weight_sems
        )
        weights.start([(0, 0), (1, 0), (0, 1), (1, 1)])
        load.wait()

        def leave(layer):
            return pltpu.make_async_copy(levels.at[layer + 1], (middle, out)[layer], sems.at[1 + layer])

        def done(layer):
            for fixed in range(2):
                @pl.when(layer == fixed)
                def _():
                    leave(fixed).start()

        forward_loop(levels, pre, scales, weights, held_down, held_up, done)
        last = [
            pltpu.make_async_copy(pre, hidden, sems.at[0]),
            pltpu.make_async_copy(scales, scales_out, sems.at[3]),
        ]
        for copy in last:
            copy.start()
        for copy in [leave(0), leave(1)] + last:
            copy.wait()


def first_backward_kernel(task, start, place, grad, entry, middle, hidden, scales_in, wide_in, narrow_in,
                          down, up, down_other, up_other, wide_out, narrow_out,
                          grads, levels, pre, scales, wide, narrow, square_sems, sems,
                          held_down, held_up, weight_sems):
    del wide_in, narrow_in

    @pl.when(place[0] == 0)
    def _():
        rows = levels.shape[1]
        copies = Copies(sems)
        loads = [
            copies.start(source, target)
            for source, target in (
                (grad, grads.at[2]), (hidden, pre), (scales_in, scales), (middle, levels.at[1]),
                (entry.at[pl.ds(start, rows)], levels.at[0]),
            )
        ]
        weights = StageWeights(
            place[1], task, (down, up), (down_other, up_other), (held_down, held_up), weight_sems
        )
        weights.start([(1, 1), (0, 1), (1, 0)])
        squares = Squares(wide, narrow, wide_out, narrow_out, square_sems)
        for load in loads:
            load.wait()
        for layer in (1, 0):
            backward_step(layer, levels, grads, pre, scales, weights, held_down, held_up, squares, layer == 1)
        squares.wait()


def last_stage_kernel(task, start, place, states, labels, label_rows, down, up, down_other, up_other,
                      grad_out, picked, wide_out, narrow_out,
                      levels, words, marks, chosen, pre, scales, grads, wide, narrow, square_sems, sems,
                      held_down, held_up, weight_sems):
    @pl.when(place[0] == 1)
    def _():
        rows = levels.shape[1]
        copies = Copies(sems)
        loaded = copies.start(states, levels.at[0])
        weights = StageWeights(
            place[1], task, (down, up), (down_other, up_other), (held_down, held_up), weight_sems
        )
        weights.start([(0, 0), (1, 0), (0, 1), (1, 1)])
        later = [copies.start(label_rows, words), copies.start(labels.at[task, pl.ds(start, rows)], marks)]
        loaded.wait()
        forward_loop(levels, pre, scales, weights, held_down, held_up, lambda layer: None)
        for copy in later:
            copy.wait()
        values = label_head(levels.at[2], marks[...], words, grads.at[2])
        lanes = 128 * ((rows + 127) // 128)
        spread = jnp.broadcast_to(values, (rows, 128))
        if lanes > rows:
            spread = jnp.concatenate([spread, zeros(lanes - rows, 128)], axis=0)
        chosen[...] = spread.T[0:8]
        out_copy = copies.start(chosen, picked)
        squares = Squares(wide, narrow, wide_out, narrow_out, square_sems)

        @pl.loop(0, 2)
        def _(index):
            backward_step(1 - index, levels, grads, pre, scales, None, held_down, held_up, squares, True)

        last = copies.start(grads.at[0], grad_out)
        squares.wait()
        out_copy.wait()
        last.wait()


def block_forward(states, w_down, w_up):
    wide = states.astype(f32)
    scale = row_scale(row_sum(wide * wide), states.shape[-1])
    hidden = jnp.einsum("nd,dr->nr", states, w_down, preferred_element_type=f32) * scale
    update = jnp.einsum("nr,dr->nd", gelu_value(hidden).astype(bf16), w_up, preferred_element_type=f32)
    return (wide + update).astype(bf16)


def fisher_kernel(tasks, halves, place, *refs):
    del place
    count = tasks * halves
    wides, narrows = refs[:count], refs[count:2 * count]
    weights, outs = refs[2 * count:-4], refs[-4:]
    for kind in range(2):
        top, total = None, None
        for task in range(tasks):
            span = slice(task * halves, (task + 1) * halves)
            left = jnp.concatenate([ref[0, kind] for ref in wides[span]], axis=0)
            right = jnp.concatenate([ref[0, kind] for ref in narrows[span]], axis=0)
            term = tn_dot(left, right)
            scaled = term * weights[task * 2 + kind][...].astype(f32)
            top = scaled if top is None else top + scaled
            total = term if total is None else total + term
        outs[kind][...] = top.astype(bf16)
        outs[2 + kind][...] = total.astype(bf16)


def block_size(width):
    return max(size for size in range(128, 1153, 128) if width % size == 0)


smem = pl.BlockSpec(memory_space=pltpu.SMEM)
anywhere = pl.BlockSpec(memory_space=pl.ANY)
hbm = pl.BlockSpec(memory_space=pltpu.HBM)


def send(block, axis, route):
    return lax.ppermute(block, axis, route)


def walk(spot, count):
    if count % 2:
        return spot
    return jnp.where(spot < count // 2, 2 * spot, 2 * (count - 1 - spot) + 1)


def spot_of(device, count):
    if count % 2:
        return device
    return jnp.where(lax.rem(device, 2) == 0, lax.div(device, 2), count - 1 - lax.div(device, 2))


def block_at(spot, offset, count):
    return walk(lax.rem(spot + offset + 2 * count, count), count)


def ring_routes(axis):
    count = lax.axis_size(axis)
    order = list(range(count)) if count % 2 else list(range(0, count, 2)) + list(range(count - 1, 0, -2))
    ahead = [(order[i], order[(i + 1) % count]) for i in range(count)]
    return count, ahead, [(j, i) for i, j in ahead]


def ring_scatter(own, other, spot, axis):
    count, ahead, back = ring_routes(axis)
    rows = own[0][0].shape[0] // count
    streams = [(index, kind) for kind in range(2) for index in range(2)]

    def part(index, kind, step):
        offset = -1 - step if index == 0 else 1 + step
        start = block_at(spot, offset, count) * rows
        return sum(
            lax.dynamic_slice_in_dim(array[index][kind], start, rows, 0).astype(f32) for array in (own, other)
        )

    moving = {stream: part(*stream, 0).astype(bf16) for stream in streams}
    for step in range(1, count):
        for stream in streams:
            landed = send(moving[stream], axis, back if stream[0] else ahead)
            total = landed.astype(f32) + part(*stream, step)
            moving[stream] = total if step == count - 1 else total.astype(bf16)
    return [jnp.stack([moving[index, kind] for kind in range(2)]) for index in range(2)]


def ring_gather(own, spot, axis):
    count, ahead, back = ring_routes(axis)
    kinds, rows, rank = own.shape

    def put(whole, piece, offset):
        return lax.dynamic_update_slice(whole, piece, (0, block_at(spot, offset, count) * rows, 0))

    whole = put(jnp.zeros((kinds, count * rows, rank), own.dtype), own, 0)
    down = up = own
    placed = 1
    for step in range(1, count // 2 + 1):
        down = send(down, axis, ahead)
        whole = put(whole, down, -step)
        placed += 1
        if placed < count:
            up = send(up, axis, back)
            whole = put(whole, up, step)
            placed += 1
    return whole


def after(value, done):
    return lax.optimization_barrier((value, done))[0]


def local(entry_states, down_proj, up_proj, label_rows, sampled_labels, eval_states):
    section_count = lax.axis_size("section")
    section = lax.axis_index("section")
    stage, member = section // 2, section % 2
    w_down, w_up = down_proj[0], up_proj[0]
    all_tasks, width, rank = w_down.shape
    tasks = all_tasks // 2
    micro, rows, _ = entry_states.shape
    label_count = label_rows.shape[0]
    total_rows, halves = micro * rows, 2
    chunks = tasks * halves
    small = max(total_rows * 2 // 5 // 16 * 16, 16)
    parts = []
    for task in range(tasks):
        sizes = (small, total_rows - small) if task == 0 else (total_rows - small, small)
        parts += [(0, sizes[0]), (sizes[0], sizes[1])]
    spot = spot_of(lax.axis_index("dp"), lax.axis_size("dp"))
    place = jnp.stack([stage, member, section, spot]).astype(jnp.int32)
    sections = range(section_count)
    swap = [(i, i ^ 1) for i in sections]
    upward = [(i, i + 2) for i in sections if i + 2 < section_count]
    downward = [(i, i - 2) for i in sections if i - 2 >= 0]

    away = (1 - member) * tasks
    others = [
        [send(lax.dynamic_index_in_dim(array, away + task, 0, keepdims=False), "section", swap) for array in (w_down, w_up)]
        for task in range(tasks)
    ]

    def weights(turn):
        return (w_down, w_up, *others[turn // halves])

    held = [
        pltpu.VMEM((2, width, rank), bf16),
        pltpu.VMEM((2, width, rank), bf16),
        pltpu.SemaphoreType.DMA((2, 2)),
    ]
    params = pltpu.CompilerParams(vmem_limit_bytes=vmem_bytes)

    class Chunk:
        def __init__(self, turn):
            self.start, part = parts[turn]
            self.part, self.lanes = part, 128 * ((part + 127) // 128)
            state, hidden, scale = (part, width), (2, part, rank), (2, part, 128)
            wide, narrow = (2, 2, part, width), (2, 2, part, rank)
            self.state, self.wide, self.narrow = (jax.ShapeDtypeStruct(shape, bf16) for shape in (state, wide, narrow))
            self.hidden, self.scale = (jax.ShapeDtypeStruct(shape, f32) for shape in (hidden, scale))
            self.levels = pltpu.VMEM((3,) + state, bf16)
            self.pre, self.scales = pltpu.VMEM(hidden, f32), pltpu.VMEM(scale, f32)
            self.squares = (self.wide, self.narrow)
            self.square_scratch = [
                pltpu.VMEM(wide, bf16), pltpu.VMEM(narrow, bf16), pltpu.SemaphoreType.DMA((2, 2, 2))
            ]
            self.flops = 4 * part * width * rank

    weight_bytes = 8 * width * rank

    def stage_call(kernel, turn, name, operands, outputs, scratch, flops, hbm_in=(), hbm_out=(), **more):
        return pl.pallas_call(
            functools.partial(kernel, turn // halves, parts[turn][0]),
            out_shape=outputs,
            in_specs=[smem] + [hbm if index in hbm_in else anywhere for index in range(1, operands + 1)],
            out_specs=tuple(hbm if index in hbm_out else anywhere for index in range(len(outputs))),
            scratch_shapes=scratch + held,
            compiler_params=params,
            cost_estimate=pl.CostEstimate(flops=flops, bytes_accessed=weight_bytes, transcendentals=0),
            name=name,
            **more,
        )

    own_labels = lax.dynamic_slice_in_dim(sampled_labels, member * tasks, tasks, 0)
    label_columns = own_labels.reshape(tasks, total_rows, 1)
    entry = entry_states.reshape(total_rows, width)
    saved, crossing, returned, picked = {}, {}, {}, {}
    squares = {}
    token = place

    def first_forward(turn):
        nonlocal token
        chunk = Chunk(turn)
        call = stage_call(
            first_forward_kernel, turn, "first_forward", 5,
            (chunk.state, chunk.state, chunk.hidden, chunk.scale),
            [chunk.levels, chunk.pre, chunk.scales, pltpu.SemaphoreType.DMA((4,))],
            2 * chunk.flops, hbm_in=(1, 2, 3, 4, 5), hbm_out=(1, 2, 3),
        )
        out, middle, hidden, scale = call(token, entry, *weights(turn))
        saved[turn] = (entry, middle, hidden, scale)
        crossing[turn] = out
        token = after(place, scale)

    def cross(turn):
        nonlocal token
        out = lax.optimization_barrier((crossing[turn], token))[0]
        crossing[turn] = send(out, "section", upward)

    def last_stage(turn):
        nonlocal token
        chunk = Chunk(turn)
        call = stage_call(
            last_stage_kernel, turn, "last_stage", 7,
            (chunk.state, jax.ShapeDtypeStruct((8, chunk.lanes), f32)) + chunk.squares,
            [
                chunk.levels, pltpu.VMEM(label_rows.shape, bf16),
                pltpu.VMEM((chunk.part, 1), jnp.int32), pltpu.VMEM((8, chunk.lanes), f32),
                chunk.pre, chunk.scales, chunk.levels,
            ] + chunk.square_scratch + [pltpu.SemaphoreType.DMA((5,))],
            4 * chunk.flops + 4 * chunk.part * width * label_count,
            hbm_in=(3, 4, 5, 6, 7), hbm_out=(2, 3),
        )
        grad, picked[turn], *squares[turn] = call(
            token, crossing[turn], label_columns, label_rows, *weights(turn)
        )
        returned[turn] = send(grad, "section", downward)
        token = after(place, picked[turn])

    def first_backward(turn):
        nonlocal token
        chunk = Chunk(turn)
        call = stage_call(
            first_backward_kernel, turn, "first_backward", 11, chunk.squares,
            [chunk.levels, chunk.levels, chunk.pre, chunk.scales] + chunk.square_scratch + [pltpu.SemaphoreType.DMA((5,))],
            2 * chunk.flops,
            hbm_in=range(2, 12), hbm_out=(0, 1),
            input_output_aliases={6: 0, 7: 1},
        )
        squares[turn] = call(token, returned[turn], *saved[turn], *squares[turn], *weights(turn))
        token = after(place, squares[turn][1])

    block = block_size(width)

    def fisher(away):
        def layer_of(s):
            return 1 - s[1] if away else s[1]

        def own_spec(task):
            return pl.BlockSpec((pl.squeezed, block, rank), lambda i, s: (s[1] * tasks + task, i, 0))

        pairs = [squares[turn] for turn in range(chunks)]
        other_spec = pl.BlockSpec((block, rank), lambda i, s: (i, 0))
        call = pl.pallas_call(
            functools.partial(fisher_kernel, tasks, halves),
            out_shape=(jax.ShapeDtypeStruct((width, rank), bf16),) * 4,
            grid_spec=pltpu.PrefetchScalarGridSpec(
                num_scalar_prefetch=1,
                grid=(width // block,),
                in_specs=[pl.BlockSpec((1, 2, part, block), lambda i, s: (layer_of(s), 0, 0, i)) for _, part in parts]
                + [pl.BlockSpec((1, 2, part, rank), lambda i, s: (layer_of(s), 0, 0, 0)) for _, part in parts]
                + [other_spec if away else own_spec(task) for task in range(tasks) for _ in range(2)],
                out_specs=(other_spec,) * 4,
            ),
            compiler_params=params,
            cost_estimate=pl.CostEstimate(
                flops=4 * tasks * total_rows * width * rank,
                bytes_accessed=8 * tasks * total_rows * width,
                transcendentals=0,
            ),
            name="fisher_away" if away else "fisher_own",
        )
        matrices = sum(others, []) if away else [w_down, w_up] * tasks
        made = call(token, *[wide for wide, _ in pairs], *[narrow for _, narrow in pairs], *matrices)
        return [made[:2], made[2:]]

    for turn in range(chunks):
        if turn == 2:
            token = after(token, crossing[0])
        first_forward(turn)
        if turn == 0:
            token = after(token, others)
        cross(turn)
    for turn in range(chunks):
        if turn >= 2:
            first_backward(turn - 2)
        last_stage(turn)
    first_backward(chunks - 2)
    values = jnp.concatenate([picked[turn][0, :parts[turn][1]] for turn in range(chunks)]).reshape(tasks, micro, rows)
    values = after(values, token)
    label_logprob = jnp.zeros((micro, rows), f32)
    for index in range(tasks):
        route = [(section_count - 2 + m, m * tasks + index) for m in range(2)]
        landed = send(values[index], "section", route)
        label_logprob = jnp.where(section % tasks == index, landed, label_logprob)
    token = after(token, label_logprob)
    first_backward(chunks - 1)
    away_sums = fisher(True)
    other_sums = lax.optimization_barrier([[send(value, "section", swap) for value in pair] for pair in away_sums])
    token = after(place, away_sums[0][0])
    sums = fisher(False)
    shares = ring_scatter(sums, other_sums, spot, "dp")
    numerator, denominator = shares
    merged_part = (numerator / (denominator + merge_eps)).astype(bf16)
    merged = ring_gather(merged_part, spot, "dp")
    fisher_log = jnp.log(denominator + merge_eps)

    current, result = eval_states, eval_states
    for step in range(section_count):
        output = block_forward(current, merged[0], merged[1])
        result = jnp.where(section == step, output, result)
        if step + 1 < section_count:
            current = send(output, "section", [(step, step + 1)])
    return (result[None], label_logprob[None], fisher_log[None])


def solution(mesh):
    placed = (
        P(None, "dp", None),
        P("section", None, None, None),
        P("section", None, None, None),
        P(),
        P(None, None, "dp"),
        P("dp", None),
    )
    return jax.shard_map(
        local,
        mesh=mesh,
        in_specs=placed,
        out_specs=(
            P("section", "dp", None),
            P("section", None, "dp"),
            P("section", None, "dp", None),
        ),
        check_vma=False,
    )
```

```python
import functools

import jax
import jax.numpy as jnp
from jax import lax
from jax.experimental import pallas as pl
from jax.experimental.pallas import tpu as pltpu
from jax.sharding import PartitionSpec as P

norm_eps = 1e-06
merge_eps = 1e-06
soft_cap = 30.0
gelu_coef = 0.7978845608028654
vmem_bytes = 56 * 1024 * 1024
bf16 = jnp.bfloat16
f32 = jnp.float32


def nt_dot(lhs, rhs):
    return lax.dot_general(lhs, rhs, (((1,), (1,)), ((), ())), preferred_element_type=f32)


def nn_dot(lhs, rhs):
    return lax.dot_general(lhs, rhs, (((1,), (0,)), ((), ())), preferred_element_type=f32)


def tn_dot(lhs, rhs):
    return lax.dot_general(lhs, rhs, (((0,), (0,)), ((), ())), preferred_element_type=f32)


def gelu_value(hidden):
    inner = gelu_coef * (hidden + 0.044715 * hidden * hidden * hidden)
    return 0.5 * hidden * (1.0 + jnp.tanh(inner))


def gelu_slope(hidden):
    inner = gelu_coef * (hidden + 0.044715 * hidden * hidden * hidden)
    tanh_value = jnp.tanh(inner)
    return 0.5 * (1.0 + tanh_value) + 0.5 * hidden * (1.0 - tanh_value * tanh_value) * gelu_coef * (
        1.0 + 3.0 * 0.044715 * hidden * hidden
    )


def tiled(width):
    count = max(n for n in (1, 2, 3) if width % (128 * n) == 0)
    size = width // count

    def loop(body, start=None):
        def step(index, carry):
            return body(pl.ds(pl.multiple_of(index * size, 128), size), carry)

        return lax.fori_loop(0, count, step, start)

    return loop


def row_scale(total, width):
    return lax.rsqrt(total / width + norm_eps)


def row_sum(values):
    return jnp.sum(values, axis=-1, keepdims=True)


def square(values):
    wide = values.astype(f32)
    return (wide * wide).astype(bf16)


def zeros(*shape):
    return jnp.zeros(shape, f32)


def label_head(states, labels, label_rows, grads):
    rows, width = states.shape
    loop, words = tiled(width), label_rows.shape[0]

    def score(cols, carry):
        total, logits = carry
        part = states[:, cols]
        wide = part.astype(f32)
        return total + row_sum(wide * wide), logits + nt_dot(part, label_rows[:, cols])

    total, logits = loop(score, (zeros(rows, 1), zeros(rows, words)))
    scale = row_scale(total, width)
    logits = logits * scale
    bent = jnp.tanh(logits / soft_cap)
    capped = soft_cap * bent
    logprob = capped - jnp.log(row_sum(jnp.exp(capped)))
    one_hot = (labels == lax.broadcasted_iota(jnp.int32, logprob.shape, 1)).astype(f32)
    slope = ((jnp.exp(logprob) - one_hot) * (1.0 - bent * bent)).astype(bf16)
    pull = scale * row_sum(slope.astype(f32) * logits) / width

    def finish(cols, carry):
        wide = states[:, cols].astype(f32)
        grads[:, cols] = (scale * nn_dot(slope, label_rows[:, cols]) - scale * (wide * pull)).astype(bf16)
        return carry

    loop(finish, 0)
    return row_sum(logprob * one_hot)


class Copies:
    def __init__(self, sems):
        self.sems, self.used = sems, 0

    def start(self, source, target):
        copy = pltpu.make_async_copy(source, target, self.sems.at[self.used])
        self.used += 1
        copy.start()
        return copy


class StageWeights:
    def __init__(self, member, task, own, other, held, sems):
        self.member, self.task, self.own, self.other = member, task, own, other
        self.held, self.sems = held, sems

    def copy(self, kind, layer):
        return pltpu.make_async_copy(self.other[kind], self.held[kind].at[layer], self.sems.at[kind, layer])

    def start(self, order):
        tasks = self.own[0].shape[0] // 2
        for kind, layer in order:
            @pl.when(self.member == layer)
            def _():
                pltpu.make_async_copy(
                    self.own[kind].at[layer * tasks + self.task], self.held[kind].at[layer], self.sems.at[kind, layer]
                ).start()

            @pl.when(self.member != layer)
            def _():
                self.copy(kind, layer).start()

    def wait(self, kind, layer):
        self.copy(kind, layer).wait()


def forward_loop(levels, hidden, scales, weights, held_down, held_up, done):
    (rows, width), rank = levels.shape[1:], held_down.shape[-1]
    loop = tiled(width)

    @pl.loop(0, 2)
    def _(layer):
        weights.wait(0, layer)

        def down(cols, carry):
            total, pre = carry
            part = levels[layer, :, cols]
            wide = part.astype(f32)
            return total + row_sum(wide * wide), pre + nn_dot(part, held_down[layer, cols])

        total, pre = loop(down, (zeros(rows, 1), zeros(rows, rank)))
        scale = row_scale(total, width)
        pre = pre * scale
        scales[layer] = jnp.broadcast_to(scale, (rows, 128))
        hidden[layer] = pre
        active = gelu_value(pre).astype(bf16)
        weights.wait(1, layer)

        def up(cols, carry):
            update = nt_dot(active, held_up[layer, cols])
            levels[layer + 1, :, cols] = (levels[layer, :, cols].astype(f32) + update).astype(bf16)
            return carry

        loop(up, 0)
        done(layer)


class Squares:
    def __init__(self, wide, narrow, wide_out, narrow_out, sems):
        self.wide, self.narrow = wide, narrow
        self.pairs = ((wide, wide_out), (narrow, narrow_out))
        self.sems = sems

    def copy(self, which, layer, kind):
        source, target = self.pairs[which]
        return pltpu.make_async_copy(
            source.at[layer, kind], target.at[layer, kind], self.sems.at[which, layer, kind]
        )

    def start(self, layer):
        for kind in range(2):
            for which in range(2):
                self.copy(which, layer, kind).start()

    def wait(self):
        for layer in range(2):
            for kind in range(2):
                for which in range(2):
                    self.copy(which, layer, kind).wait()


def backward_step(layer, levels, grads, hidden, scales, weights, held_down, held_up, squares, pass_on):
    (rows, width), rank = levels.shape[1:], held_down.shape[-1]
    loop = tiled(width)
    if weights is not None:
        weights.wait(1, layer)
    scale = scales[layer][:, :1]
    pre = hidden[layer]

    def up(cols, total):
        grad = grads[layer + 1, :, cols]
        total = total + nn_dot(grad, held_up[layer, cols])
        norm = (levels[layer, :, cols].astype(f32) * scale).astype(bf16)
        squares.wide[layer, 0, :, cols] = square(norm)
        squares.wide[layer, 1, :, cols] = square(grad)
        return total

    grad_hidden = (loop(up, zeros(rows, rank)) * gelu_slope(pre)).astype(bf16)
    squares.narrow[layer, 0] = square(grad_hidden)
    squares.narrow[layer, 1] = square(gelu_value(pre).astype(bf16))
    squares.start(layer)
    if not pass_on:
        return
    if weights is not None:
        weights.wait(0, layer)
    pull = scale * row_sum(grad_hidden.astype(f32) * pre) / width

    def finish(cols, carry):
        grad_norm = nt_dot(grad_hidden, held_down[layer, cols])
        wide = levels[layer, :, cols].astype(f32)
        grads[layer, :, cols] = (
            grads[layer + 1, :, cols].astype(f32) + scale * (grad_norm - wide * pull)
        ).astype(bf16)
        return carry

    loop(finish, 0)


def first_forward_kernel(task, start, place, entry, down, up, down_other, up_other, out, middle, hidden, scales_out,
                         levels, pre, scales, sems, held_down, held_up, weight_sems):
    @pl.when(place[0] == 0)
    def _():
        rows = levels.shape[1]
        copies = Copies(sems)
        load = copies.start(entry.at[pl.ds(start, rows)], levels.at[0])
        weights = StageWeights(
            place[1], task, (down, up), (down_other, up_other), (held_down, held_up), weight_sems
        )
        weights.start([(0, 0), (1, 0), (0, 1), (1, 1)])
        load.wait()

        def leave(layer):
            return pltpu.make_async_copy(levels.at[layer + 1], (middle, out)[layer], sems.at[1 + layer])

        def done(layer):
            for fixed in range(2):
                @pl.when(layer == fixed)
                def _():
                    leave(fixed).start()

        forward_loop(levels, pre, scales, weights, held_down, held_up, done)
        last = [
            pltpu.make_async_copy(pre, hidden, sems.at[0]),
            pltpu.make_async_copy(scales, scales_out, sems.at[3]),
        ]
        for copy in last:
            copy.start()
        for copy in [leave(0), leave(1)] + last:
            copy.wait()


def first_backward_kernel(task, start, place, grad, entry, middle, hidden, scales_in, wide_in, narrow_in,
                          down, up, down_other, up_other, wide_out, narrow_out,
                          grads, levels, pre, scales, wide, narrow, square_sems, sems,
                          held_down, held_up, weight_sems):
    del wide_in, narrow_in

    @pl.when(place[0] == 0)
    def _():
        rows = levels.shape[1]
        copies = Copies(sems)
        loads = [
            copies.start(source, target)
            for source, target in (
                (grad, grads.at[2]), (hidden, pre), (scales_in, scales), (middle, levels.at[1]),
                (entry.at[pl.ds(start, rows)], levels.at[0]),
            )
        ]
        weights = StageWeights(
            place[1], task, (down, up), (down_other, up_other), (held_down, held_up), weight_sems
        )
        weights.start([(1, 1), (0, 1), (1, 0)])
        squares = Squares(wide, narrow, wide_out, narrow_out, square_sems)
        for load in loads:
            load.wait()
        for layer in (1, 0):
            backward_step(layer, levels, grads, pre, scales, weights, held_down, held_up, squares, layer == 1)
        squares.wait()


def last_stage_kernel(task, start, place, states, labels, label_rows, down, up, down_other, up_other,
                      grad_out, picked, wide_out, narrow_out,
                      levels, words, marks, chosen, pre, scales, grads, wide, narrow, square_sems, sems,
                      held_down, held_up, weight_sems):
    @pl.when(place[0] == 1)
    def _():
        rows = levels.shape[1]
        copies = Copies(sems)
        loaded = copies.start(states, levels.at[0])
        weights = StageWeights(
            place[1], task, (down, up), (down_other, up_other), (held_down, held_up), weight_sems
        )
        weights.start([(0, 0), (1, 0), (0, 1), (1, 1)])
        later = [copies.start(label_rows, words), copies.start(labels.at[task, pl.ds(start, rows)], marks)]
        loaded.wait()
        forward_loop(levels, pre, scales, weights, held_down, held_up, lambda layer: None)
        for copy in later:
            copy.wait()
        values = label_head(levels.at[2], marks[...], words, grads.at[2])
        lanes = 128 * ((rows + 127) // 128)
        spread = jnp.broadcast_to(values, (rows, 128))
        if lanes > rows:
            spread = jnp.concatenate([spread, zeros(lanes - rows, 128)], axis=0)
        chosen[...] = spread.T[0:8]
        out_copy = copies.start(chosen, picked)
        squares = Squares(wide, narrow, wide_out, narrow_out, square_sems)

        @pl.loop(0, 2)
        def _(index):
            backward_step(1 - index, levels, grads, pre, scales, None, held_down, held_up, squares, True)

        last = copies.start(grads.at[0], grad_out)
        squares.wait()
        out_copy.wait()
        last.wait()


def block_forward(states, w_down, w_up):
    wide = states.astype(f32)
    scale = row_scale(row_sum(wide * wide), states.shape[-1])
    hidden = jnp.einsum("nd,dr->nr", states, w_down, preferred_element_type=f32) * scale
    update = jnp.einsum("nr,dr->nd", gelu_value(hidden).astype(bf16), w_up, preferred_element_type=f32)
    return (wide + update).astype(bf16)


def fisher_kernel(tasks, halves, place, *refs):
    del place
    count = tasks * halves
    wides, narrows = refs[:count], refs[count:2 * count]
    weights, outs = refs[2 * count:-4], refs[-4:]
    for kind in range(2):
        top, total = None, None
        for task in range(tasks):
            span = slice(task * halves, (task + 1) * halves)
            left = jnp.concatenate([ref[0, kind] for ref in wides[span]], axis=0)
            right = jnp.concatenate([ref[0, kind] for ref in narrows[span]], axis=0)
            term = tn_dot(left, right)
            scaled = term * weights[task * 2 + kind][...].astype(f32)
            top = scaled if top is None else top + scaled
            total = term if total is None else total + term
        outs[kind][...] = top.astype(bf16)
        outs[2 + kind][...] = total.astype(bf16)


def block_size(width):
    return max(size for size in range(128, 1153, 128) if width % size == 0)


smem = pl.BlockSpec(memory_space=pltpu.SMEM)
anywhere = pl.BlockSpec(memory_space=pl.ANY)
hbm = pl.BlockSpec(memory_space=pltpu.HBM)


def send(block, axis, route):
    return lax.ppermute(block, axis, route)


def walk(spot, count):
    if count % 2:
        return spot
    return jnp.where(spot < count // 2, 2 * spot, 2 * (count - 1 - spot) + 1)


def spot_of(device, count):
    if count % 2:
        return device
    return jnp.where(lax.rem(device, 2) == 0, lax.div(device, 2), count - 1 - lax.div(device, 2))


def block_at(spot, offset, count):
    return walk(lax.rem(spot + offset + 2 * count, count), count)


def ring_routes(axis):
    count = lax.axis_size(axis)
    order = list(range(count)) if count % 2 else list(range(0, count, 2)) + list(range(count - 1, 0, -2))
    ahead = [(order[i], order[(i + 1) % count]) for i in range(count)]
    return count, ahead, [(j, i) for i, j in ahead]


def ring_scatter(own, other, spot, axis):
    count, ahead, back = ring_routes(axis)
    rows = own[0][0].shape[0] // count
    streams = [(index, kind) for kind in range(2) for index in range(2)]

    def part(index, kind, step):
        offset = -1 - step if index == 0 else 1 + step
        start = block_at(spot, offset, count) * rows
        return sum(
            lax.dynamic_slice_in_dim(array[index][kind], start, rows, 0).astype(f32) for array in (own, other)
        )

    moving = {stream: part(*stream, 0).astype(bf16) for stream in streams}
    for step in range(1, count):
        for stream in streams:
            landed = send(moving[stream], axis, back if stream[0] else ahead)
            total = landed.astype(f32) + part(*stream, step)
            moving[stream] = total if step == count - 1 else total.astype(bf16)
    return [jnp.stack([moving[index, kind] for kind in range(2)]) for index in range(2)]


def ring_gather(own, spot, axis):
    count, *routes = ring_routes(axis)
    rows, rank = own[0].shape

    def put(whole, piece, offset):
        return lax.dynamic_update_slice(whole, piece, (block_at(spot, offset, count) * rows, 0))

    whole = [put(jnp.zeros((count * rows, rank), piece.dtype), piece, 0) for piece in own]
    moving = {(way, kind): piece for kind, piece in enumerate(own) for way in range(2)}
    for step in range(1, count // 2 + 1):
        for way, kind in moving:
            if 2 * step == count and way != kind % 2:
                continue
            moving[way, kind] = send(moving[way, kind], axis, routes[way])
            whole[kind] = put(whole[kind], moving[way, kind], step if way else -step)
    return whole


def after(value, done):
    return lax.optimization_barrier((value, done))[0]


def local(entry_states, down_proj, up_proj, label_rows, sampled_labels, eval_states):
    section_count = lax.axis_size("section")
    section = lax.axis_index("section")
    stage, member = section // 2, section % 2
    w_down, w_up = down_proj[0], up_proj[0]
    all_tasks, width, rank = w_down.shape
    tasks = all_tasks // 2
    micro, rows, _ = entry_states.shape
    label_count = label_rows.shape[0]
    total_rows, halves = micro * rows, 2
    chunks = tasks * halves
    parts = [(half * (total_rows // halves), total_rows // halves) for _ in range(tasks) for half in range(halves)]
    spot = spot_of(lax.axis_index("dp"), lax.axis_size("dp"))
    place = jnp.stack([stage, member, section, spot]).astype(jnp.int32)
    sections = range(section_count)
    swap = [(i, i ^ 1) for i in sections]
    upward = [(i, i + 2) for i in sections if i + 2 < section_count]
    downward = [(i, i - 2) for i in sections if i - 2 >= 0]

    away = (1 - member) * tasks
    others = [
        [send(lax.dynamic_index_in_dim(array, away + task, 0, keepdims=False), "section", swap) for array in (w_down, w_up)]
        for task in range(tasks)
    ]

    def weights(turn):
        return (w_down, w_up, *others[turn // halves])

    held = [
        pltpu.VMEM((2, width, rank), bf16),
        pltpu.VMEM((2, width, rank), bf16),
        pltpu.SemaphoreType.DMA((2, 2)),
    ]
    params = pltpu.CompilerParams(vmem_limit_bytes=vmem_bytes)

    class Chunk:
        def __init__(self, turn):
            self.start, part = parts[turn]
            self.part, self.lanes = part, 128 * ((part + 127) // 128)
            state, hidden, scale = (part, width), (2, part, rank), (2, part, 128)
            wide, narrow = (2, 2, part, width), (2, 2, part, rank)
            self.state, self.wide, self.narrow = (jax.ShapeDtypeStruct(shape, bf16) for shape in (state, wide, narrow))
            self.hidden, self.scale = (jax.ShapeDtypeStruct(shape, f32) for shape in (hidden, scale))
            self.levels = pltpu.VMEM((3,) + state, bf16)
            self.pre, self.scales = pltpu.VMEM(hidden, f32), pltpu.VMEM(scale, f32)
            self.squares = (self.wide, self.narrow)
            self.square_scratch = [
                pltpu.VMEM(wide, bf16), pltpu.VMEM(narrow, bf16), pltpu.SemaphoreType.DMA((2, 2, 2))
            ]
            self.flops = 4 * part * width * rank

    weight_bytes = 8 * width * rank

    def stage_call(kernel, turn, name, operands, outputs, scratch, flops, hbm_in=(), hbm_out=(), **more):
        return pl.pallas_call(
            functools.partial(kernel, turn // halves, parts[turn][0]),
            out_shape=outputs,
            in_specs=[smem] + [hbm if index in hbm_in else anywhere for index in range(1, operands + 1)],
            out_specs=tuple(hbm if index in hbm_out else anywhere for index in range(len(outputs))),
            scratch_shapes=scratch + held,
            compiler_params=params,
            cost_estimate=pl.CostEstimate(flops=flops, bytes_accessed=weight_bytes, transcendentals=0),
            name=name,
            **more,
        )

    own_labels = lax.dynamic_slice_in_dim(sampled_labels, member * tasks, tasks, 0)
    label_columns = own_labels.reshape(tasks, total_rows, 1)
    entry = entry_states.reshape(total_rows, width)
    saved, crossing, returned, picked = {}, {}, {}, {}
    squares = {}
    token = place

    def first_forward(turn):
        nonlocal token
        chunk = Chunk(turn)
        call = stage_call(
            first_forward_kernel, turn, "first_forward", 5,
            (chunk.state, chunk.state, chunk.hidden, chunk.scale),
            [chunk.levels, chunk.pre, chunk.scales, pltpu.SemaphoreType.DMA((4,))],
            2 * chunk.flops, hbm_in=(1, 2, 3, 4, 5), hbm_out=(1, 2, 3),
        )
        out, middle, hidden, scale = call(token, entry, *weights(turn))
        saved[turn] = (entry, middle, hidden, scale)
        crossing[turn] = out
        token = after(place, scale)

    def cross(turn):
        nonlocal token
        out = lax.optimization_barrier((crossing[turn], token))[0]
        crossing[turn] = send(out, "section", upward)

    def last_stage(turn):
        nonlocal token
        chunk = Chunk(turn)
        call = stage_call(
            last_stage_kernel, turn, "last_stage", 7,
            (chunk.state, jax.ShapeDtypeStruct((8, chunk.lanes), f32)) + chunk.squares,
            [
                chunk.levels, pltpu.VMEM(label_rows.shape, bf16),
                pltpu.VMEM((chunk.part, 1), jnp.int32), pltpu.VMEM((8, chunk.lanes), f32),
                chunk.pre, chunk.scales, chunk.levels,
            ] + chunk.square_scratch + [pltpu.SemaphoreType.DMA((5,))],
            4 * chunk.flops + 4 * chunk.part * width * label_count,
            hbm_in=(3, 4, 5, 6, 7), hbm_out=(2, 3),
        )
        grad, picked[turn], *squares[turn] = call(
            token, crossing[turn], label_columns, label_rows, *weights(turn)
        )
        returned[turn] = send(grad, "section", downward)
        token = after(place, picked[turn])

    def first_backward(turn):
        nonlocal token
        chunk = Chunk(turn)
        call = stage_call(
            first_backward_kernel, turn, "first_backward", 11, chunk.squares,
            [chunk.levels, chunk.levels, chunk.pre, chunk.scales] + chunk.square_scratch + [pltpu.SemaphoreType.DMA((5,))],
            2 * chunk.flops,
            hbm_in=range(2, 12), hbm_out=(0, 1),
            input_output_aliases={6: 0, 7: 1},
        )
        squares[turn] = call(token, returned[turn], *saved[turn], *squares[turn], *weights(turn))
        token = after(place, squares[turn][1])

    block = block_size(width)

    def fisher(away):
        def layer_of(s):
            return 1 - s[1] if away else s[1]

        def own_spec(task):
            return pl.BlockSpec((pl.squeezed, block, rank), lambda i, s: (s[1] * tasks + task, i, 0))

        pairs = [squares[turn] for turn in range(chunks)]
        other_spec = pl.BlockSpec((block, rank), lambda i, s: (i, 0))
        call = pl.pallas_call(
            functools.partial(fisher_kernel, tasks, halves),
            out_shape=(jax.ShapeDtypeStruct((width, rank), bf16),) * 4,
            grid_spec=pltpu.PrefetchScalarGridSpec(
                num_scalar_prefetch=1,
                grid=(width // block,),
                in_specs=[pl.BlockSpec((1, 2, part, block), lambda i, s: (layer_of(s), 0, 0, i)) for _, part in parts]
                + [pl.BlockSpec((1, 2, part, rank), lambda i, s: (layer_of(s), 0, 0, 0)) for _, part in parts]
                + [other_spec if away else own_spec(task) for task in range(tasks) for _ in range(2)],
                out_specs=(other_spec,) * 4,
            ),
            compiler_params=params,
            cost_estimate=pl.CostEstimate(
                flops=4 * tasks * total_rows * width * rank,
                bytes_accessed=8 * tasks * total_rows * width,
                transcendentals=0,
            ),
            name="fisher_away" if away else "fisher_own",
        )
        matrices = sum(others, []) if away else [w_down, w_up] * tasks
        made = call(token, *[wide for wide, _ in pairs], *[narrow for _, narrow in pairs], *matrices)
        return [made[:2], made[2:]]

    for turn in range(chunks):
        first_forward(turn)
        if turn == 0:
            token = after(token, others)
        cross(turn)
    for turn in range(chunks):
        if turn >= 2:
            first_backward(turn - 2)
        last_stage(turn)
    first_backward(chunks - 2)
    values = jnp.concatenate([picked[turn][0, :parts[turn][1]] for turn in range(chunks)]).reshape(tasks, micro, rows)
    values = after(values, token)
    label_logprob = jnp.zeros((micro, rows), f32)
    for index in range(tasks):
        route = [(section_count - 2 + m, m * tasks + index) for m in range(2)]
        landed = send(values[index], "section", route)
        label_logprob = jnp.where(section % tasks == index, landed, label_logprob)
    token = after(token, label_logprob)
    first_backward(chunks - 1)
    away_sums = fisher(True)
    other_sums = lax.optimization_barrier([[send(value, "section", swap) for value in pair] for pair in away_sums])
    token = after(place, away_sums[0][0])
    sums = fisher(False)
    shares = ring_scatter(sums, other_sums, spot, "dp")
    numerator, denominator = shares
    merged_part = (numerator / (denominator + merge_eps)).astype(bf16)
    merged = ring_gather([merged_part[0], merged_part[1]], spot, "dp")
    fisher_log = jnp.log(denominator + merge_eps)

    current, result = eval_states, eval_states
    for step in range(section_count):
        output = block_forward(current, merged[0], merged[1])
        result = jnp.where(section == step, output, result)
        if step + 1 < section_count:
            current = send(output, "section", [(step, step + 1)])
    return (result[None], label_logprob[None], fisher_log[None])


def solution(mesh):
    placed = (
        P(None, "dp", None),
        P("section", None, None, None),
        P("section", None, None, None),
        P(),
        P(None, None, "dp"),
        P("dp", None),
    )
    return jax.shard_map(
        local,
        mesh=mesh,
        in_specs=placed,
        out_specs=(
            P("section", "dp", None),
            P("section", None, "dp"),
            P("section", None, "dp", None),
        ),
        check_vma=False,
    )
```
